32 devices in a mesh: lat: 2 (over core), lon: 16 (over z, y, x).
Axes of the slice: x: 2, y: 2, z: 4, core: 2. Of those that a mesh axis runs over, the one named last changes fastest.
Arguments:
- fields: bfloat16 [2, 8, 640, 384], P(None, 'lat', None, 'lon'), may hold values from -6 to 6
- kernel: bfloat16 [5, 8, 3, 3, 64, 64], P(None, 'lat'), may hold values from -0.25 to 0.25
- band_low: int32 [5, 8], replicated, may hold values from -2 to 0
- block_shift: int32 [8, 3], replicated, may hold values from -3 to 3
- mix_weight: bfloat16 [5, 640, 640], P(None, 'lon'), may hold values from -0.109375 to 0.109375
Outputs:
- mixed: bfloat16 [2, 8, 384, 640], P(None, 'lat', 'lon')
The draws below stay inside these ranges and needn't reach their ends.
All inputs are finite; a program needn't handle non-finite values.
Results may differ from the reference program's by a relative error of at most 0.005.
Values may be sent and summed in bfloat16 or wider, within the bound.
No kernel may reach another device: no remote copies, remote signals or barrier semaphores. Data moves between devices by JAX's collectives and lax.ppermute only.
A program may use at most 128 MiB of HBM per device.

```python
import jax
import jax.numpy as jnp
from jax import lax

C = 640
K = 5
BL = 64
TAPS = 3
J = 3
E = 2
NLAT = 8
NLON = 384
NB = 6


def set_ends(values, own_key, smallest, high):
    longest = values.shape.index(max(values.shape))
    spots = []
    for shift in (0, 1):
        where = [jax.random.randint(jax.random.fold_in(own_key, axis), (), 0, length) for axis, length in enumerate(values.shape)]
        where[longest] = (where[longest] + shift) % values.shape[longest]
        spots.append(tuple(where))
    return values.at[spots[0]].set(smallest).at[spots[1]].set(high)


def block_levels(stream_key, shape, shards, low, largest):
    gain = 1.0
    for axis_at, blocks in shards:
        draws = jax.random.uniform(jax.random.fold_in(jax.random.fold_in(stream_key, 6), axis_at), (blocks,), jnp.float32, low / len(shards), largest / len(shards))
        gain = gain * jnp.repeat(jnp.exp(draws), shape[axis_at] // blocks).reshape((-1,) + (1,) * (len(shape) - 1 - axis_at))
    return gain


def normal_values(own_key, extent, spread, limit, cuts=(), held_as=jnp.bfloat16):
    values = jax.random.normal(own_key, extent, jnp.float32) * spread
    if len(cuts) > 0:
        values = block_levels(own_key, extent, cuts, -0.22, 0.18) * values
    return jnp.clip(values, min=-limit, max=limit).astype(held_as)


def setup_inputs(seed: int = 0) -> dict:
    key_list = jax.random.split(jax.random.key(seed), 6)
    return {
        "fields": normal_values(key_list[0], (E, NLAT, C, NLON), 1.0, 6.0, ((1, 2), (3, 16))),
        "kernel": normal_values(key_list[1], (K, NLAT, TAPS, J, BL, BL), (TAPS * J * BL) ** -0.5, 0.25, ((1, 2),)),
        "band_low": set_ends(jax.random.randint(key_list[2], (K, NLAT), -2, 1), jax.random.fold_in(key_list[2], 1), -2, 0).astype(jnp.int32),
        "block_shift": set_ends(jax.random.randint(key_list[3], (NLAT, J), -3, 4), jax.random.fold_in(key_list[3], 1), -3, 3).astype(jnp.int32),
        "mix_weight": normal_values(key_list[4], (K, C, C), (K * C) ** -0.5, 0.109375, ((1, 16),)),
    }


def reference(fields, kernel, band_low, block_shift, mix_weight):
    blocks = fields.reshape(E, NLAT, C, NB, BL)
    lane_ids = jnp.arange(NB, dtype=jnp.int32)
    tap_ids = jnp.arange(TAPS, dtype=jnp.int32)
    weight_mix = mix_weight.astype(jnp.float32)

    def one_row(out_row):
        total = jnp.zeros((K, E, C, NB, BL), jnp.float32)
        for delta in range(-2, 3):
            source = out_row + delta
            valid = (source >= 0) & (source < NLAT)
            row_id = jnp.clip(source, 0, NLAT - 1).astype(jnp.int32)
            source_row = lax.dynamic_index_in_dim(blocks, row_id, 1, keepdims=False)
            shifts = lax.dynamic_index_in_dim(block_shift, row_id, 0, keepdims=False)
            index = (lane_ids[None, :] + shifts[:, None]) % NB
            picked = jnp.take(source_row, index, axis=2)
            kernel_row = lax.dynamic_index_in_dim(kernel, row_id, 1, keepdims=False)
            lows = lax.dynamic_index_in_dim(band_low, row_id, 1, keepdims=False)
            target = row_id + lows[:, None] + tap_ids[None, :]
            select = ((target == out_row) & valid).astype(jnp.float32)
            effective = jnp.einsum('kt,ktjpq->kjpq', select, kernel_row.astype(jnp.float32))
            total = total + jnp.einsum('ecjbp,kjpq->kecbq', picked.astype(jnp.float32), effective)
        conv = total.astype(jnp.bfloat16).reshape(K, E, C, NLON)
        summed = jnp.einsum('kecn,kcd->end', conv.astype(jnp.float32), weight_mix)
        return jax.nn.gelu(summed, approximate=False).astype(jnp.bfloat16)

    result = lax.map(one_row, jnp.arange(NLAT, dtype=jnp.int32))
    return jnp.transpose(result, (1, 0, 2, 3))
```

```python
import functools
import math

import jax
import jax.numpy as jnp
from jax import lax
from jax.experimental import pallas as pl
from jax.experimental.pallas import tpu as pltpu
from jax.sharding import Mesh
from jax.sharding import PartitionSpec as P

HALO = 2
VMEM = pltpu.VMEM
LIMIT = 48 * 1024 * 1024


def pack_kernel(groups, owners, x_ref, out_ref):
    members, rows, cells, channels = x_ref.shape
    width = channels // (groups * owners)
    for e in range(members):
        for q in range(groups):
            parts = [
                x_ref[e, i, :, (p * groups + q) * width : (p * groups + q + 1) * width]
                for i in range(rows)
                for p in range(owners)
            ]
            block = jnp.concatenate(parts, axis=-1)
            for p in range(owners):
                out_ref[e, p, q] = block


def pack(x, groups, owners):
    members, rows, cells, channels = x.shape
    return pl.pallas_call(
        functools.partial(pack_kernel, groups, owners),
        out_shape=jax.ShapeDtypeStruct((members, owners, groups, cells, rows * channels // groups), x.dtype),
        in_specs=[pl.BlockSpec(memory_space=VMEM)],
        out_specs=pl.BlockSpec(memory_space=VMEM),
        compiler_params=pltpu.CompilerParams(vmem_limit_bytes=LIMIT),
        name="pack",
    )(x)


def conv_mix_kernel(bases, taps, slots, halo, sub, low_ref, shift_ref, place_ref, fields_ref, *refs):
    late = fields_ref.shape[1]
    weight_refs = refs[:late]
    mix_ref = refs[late]
    outs = refs[late + 1 : -2]
    field_rows, total = refs[-2:]
    owners, _, span, _ = fields_ref.shape
    channels = mix_ref.shape[1]
    rows = weight_refs[0].shape[0]
    block = weight_refs[0].shape[2]
    nblocks = owners * span // block
    member, owner = place_ref[0], place_ref[1]

    total[...] = jnp.zeros_like(total)
    for s in range(late):
        lat = lax.rem(member + s, late)
        for r in range(rows):
            for p in range(owners):
                field_rows[r, p * span : (p + 1) * span] = fields_ref[
                    p, lat, :, r * channels : (r + 1) * channels
                ]
        for r in range(rows):
            row = lat * rows + r
            for piece in range(span // sub):
                cell = owner * span + piece * sub
                b = lax.div(cell, block)
                q = pl.multiple_of(lax.rem(cell, block), sub)
                chosen = []
                for j in range(slots):
                    source = lax.rem(b + shift_ref[row, j] + nblocks, nblocks)
                    chosen.append(field_rows[r, pl.ds(pl.multiple_of(source * block, block), block)])
                picked = jnp.concatenate(chosen, axis=0)
                lhs = weight_refs[s][r, :, pl.ds(q, sub), :].reshape(bases * taps * sub, slots * block)
                product = jnp.dot(lhs, picked, preferred_element_type=jnp.float32)
                for k in range(bases):
                    first = row + low_ref[k, row] + HALO
                    for t in range(taps):
                        at = (k * taps + t) * sub
                        total[k, first + t, piece * sub : (piece + 1) * sub] += product[at : at + sub]
    main = outs[0]
    _, groups, _, cells, _ = main.shape
    for o in range(-halo, late * rows + halo):
        mixed = sum(
            jnp.dot(total[k, o + HALO].astype(jnp.bfloat16), mix_ref[k], preferred_element_type=jnp.float32)
            for k in range(bases)
        )
        for q in range(groups):
            value = mixed[q * cells : (q + 1) * cells].astype(jnp.bfloat16)
            if 0 <= o < late * rows:
                main[o // rows, q, o % rows] = value
            else:
                outs[1][o + halo if o < 0 else o + halo - late * rows, q] = value


def conv_mix(low, shift, place, fields, weights, mix, halo, groups, block):
    bases, all_rows = low.shape
    slots = shift.shape[1]
    owners, late, span, _ = fields.shape
    rows = all_rows // late
    channels, width = mix.shape[1:]
    taps = weights[0].shape[1] // bases
    sub = math.gcd(span, block)
    shapes = [jax.ShapeDtypeStruct((late, groups, rows, span // groups, width), jnp.bfloat16)]
    if halo:
        shapes.append(jax.ShapeDtypeStruct((2 * halo, groups, span // groups, width), jnp.bfloat16))
    smem = pl.BlockSpec(memory_space=pltpu.SMEM)
    vmem = pl.BlockSpec(memory_space=VMEM)
    return pl.pallas_call(
        functools.partial(conv_mix_kernel, bases, taps, slots, halo, sub),
        out_shape=shapes,
        in_specs=[smem] * 3 + [vmem] * (2 + late),
        out_specs=[vmem] * len(shapes),
        scratch_shapes=[
            VMEM((rows, owners * span, channels), jnp.bfloat16),
            VMEM((bases, all_rows + 2 * HALO, span, channels), jnp.float32),
        ],
        compiler_params=pltpu.CompilerParams(vmem_limit_bytes=LIMIT),
        name="conv_mix",
    )(low, shift, place, fields, *weights, mix)


def per_device(sizes, fields, kernel, band_low, block_shift, mix_weight):
    halves, late, owners, groups = sizes
    members, rows, channels, cells = fields.shape
    bases, _, taps, slots, block, _ = kernel.shape
    all_rows = late * rows
    halo = HALO if halves > 1 else 0

    packed = pack(fields.transpose(0, 1, 3, 2), groups, owners)
    packed = packed.reshape((late * owners * groups,) + packed.shape[3:])
    spread = lax.all_to_all(packed, ("late", "lonp", "lonq"), split_axis=0, concat_axis=0, tiled=True)
    spread = spread.reshape(late, owners, groups * cells, -1).transpose(1, 0, 2, 3)

    own = kernel.transpose(1, 0, 2, 5, 3, 4).reshape(rows, bases * taps, block, slots * block)
    weights = [own]
    for s in range(1, late):
        route = [((i + s) % late, i) for i in range(late)]
        weights.append(lax.ppermute(own, "late", route))
    mix = lax.all_gather(mix_weight, "lonp", axis=1, tiled=True)

    start = lax.axis_index("lath") * all_rows
    low = lax.dynamic_slice_in_dim(band_low, start, all_rows, 1)
    shift = lax.dynamic_slice_in_dim(block_shift, start, all_rows, 0)
    place = jnp.stack([lax.axis_index("late"), lax.axis_index("lonp")]).astype(jnp.int32)
    partial, *beyond = conv_mix(low, shift, place, spread, weights, mix, halo, groups, block)
    if halo:
        beyond = beyond[0]
        below = lax.ppermute(beyond[halo:], "lath", [(i, i + 1) for i in range(halves - 1)])
        above = lax.ppermute(beyond[:halo], "lath", [(i + 1, i) for i in range(halves - 1)])
        body = partial.transpose(0, 2, 1, 3, 4).reshape((all_rows,) + beyond.shape[1:])
        body = body.astype(jnp.float32)
        body = body.at[:halo].add(below.astype(jnp.float32)).at[-halo:].add(above.astype(jnp.float32))
        body = body.astype(jnp.bfloat16).reshape((late, rows) + beyond.shape[1:])
        partial = body.transpose(0, 2, 1, 3, 4)
    partial = partial.reshape(late * groups, rows * cells, -1)
    parts = lax.all_to_all(partial, ("late", "lonq"), split_axis=0, concat_axis=0, tiled=True)
    parts = parts.reshape(members, groups, rows, cells, -1)
    summed = jnp.sum(parts.astype(jnp.float32), axis=1)
    return jax.nn.gelu(summed, approximate=False).astype(jnp.bfloat16)


def solution(mesh):
    lat, lon = mesh.shape["lat"], mesh.shape["lon"]
    groups = max(g for g in range(1, lon + 1) if lon % g == 0 and g * g <= lon)

    def whole(fields, kernel, band_low, block_shift, mix_weight):
        late = fields.shape[0]
        sizes = (lat // late, late, lon // groups, groups)
        split = Mesh(mesh.devices.reshape(sizes), ("lath", "late", "lonp", "lonq"))
        rows, cells = ("lath", "late"), ("lonp", "lonq")
        return jax.shard_map(
            functools.partial(per_device, sizes),
            mesh=split,
            in_specs=(
                P(None, rows, None, cells),
                P(None, rows, None, None, None, None),
                P(),
                P(),
                P(None, cells, None),
            ),
            out_specs=P(None, rows, cells, None),
            check_vma=False,
        )(fields, kernel, band_low, block_shift, mix_weight)

    return whole
```

```python
import functools
import math

import jax
import jax.numpy as jnp
from jax import lax
from jax.experimental import pallas as pl
from jax.experimental.pallas import tpu as pltpu
from jax.sharding import Mesh
from jax.sharding import PartitionSpec as P

HALO = 2
LANES = 128
VMEM = pltpu.VMEM
LIMIT = 48 * 1024 * 1024
SMEM_SPEC = pl.BlockSpec(memory_space=pltpu.SMEM)
VMEM_SPEC = pl.BlockSpec(memory_space=VMEM)


def partner(index, distance, size):
    if size & (size - 1) == 0:
        return index ^ distance
    return (distance - index) % size


def partner_in_kernel(index, distance, size):
    if size & (size - 1) == 0:
        return lax.bitwise_xor(index, distance)
    return lax.rem(distance - index + size, size)


def trade(x, axis, distance, size):
    return lax.ppermute(x, axis, [(i, partner(i, distance, size)) for i in range(size)])


def pack_kernel(groups, owners, x_ref, out_ref):
    members, rows, cells, channels = x_ref.shape
    width = channels // (groups * owners)
    for e in range(members):
        for q in range(groups):
            parts = [
                x_ref[e, i, :, (p * groups + q) * width : (p * groups + q + 1) * width]
                for i in range(rows)
                for p in range(owners)
            ]
            out_ref[e, q] = jnp.concatenate(parts, axis=-1)


def pack(x, groups, owners):
    members, rows, cells, channels = x.shape
    return pl.pallas_call(
        functools.partial(pack_kernel, groups, owners),
        out_shape=jax.ShapeDtypeStruct((members, groups, cells, rows * channels // groups), x.dtype),
        in_specs=[VMEM_SPEC],
        out_specs=VMEM_SPEC,
        compiler_params=pltpu.CompilerParams(vmem_limit_bytes=LIMIT),
        name="pack",
    )(x)


def added(refs, *at):
    value = refs[0][at]
    for ref in refs[1:]:
        value = value + ref[at]
    return value


def conv_mix_kernel(geometry, counts, low_ref, shift_ref, place_ref, *refs):
    bases, taps, slots, halo, sub, groups = geometry
    refs = list(refs)
    field_slots = [[refs.pop(0) for _ in range(n)] for n in counts[0]]
    weight_refs = [refs.pop(0) for _ in range(counts[1])]
    mix_slots = [[refs.pop(0) for _ in range(n)] for n in counts[2]]
    field_rows, total, mix_all, mixed = refs[-4:]
    outs = refs[:-4]
    late, span, _ = field_slots[0][0].shape
    owners = len(field_slots)
    depth, width = mix_slots[0][0].shape[1:]
    channels = owners * depth
    padded = total.shape[-1]
    rows, _, block, _ = weight_refs[0].shape
    nblocks = owners * span // block
    cells = span // groups
    member, owner, group = place_ref[0], place_ref[1], place_ref[2]

    total[...] = jnp.zeros_like(total)
    field_rows[...] = jnp.zeros_like(field_rows)
    for s in range(late):
        lat = partner_in_kernel(member, s, late)
        for d, slot in enumerate(field_slots):
            base = pl.multiple_of(partner_in_kernel(owner, d, owners) * span, sub)
            value = added(slot, lat)
            for r in range(rows):
                field_rows[r, pl.ds(base, span), :channels] = value[:, r * channels : (r + 1) * channels]

        def one_row(r, carry):
            row = lat * rows + r
            for piece in range(span // sub):
                cell = owner * span + piece * sub
                b = lax.div(cell, block)
                q = pl.multiple_of(lax.rem(cell, block), sub)
                chosen = []
                for j in range(slots):
                    source = lax.rem(b + shift_ref[row, j] + nblocks, nblocks)
                    chosen.append(field_rows[r, pl.ds(pl.multiple_of(source * block, block), block)])
                picked = jnp.concatenate(chosen, axis=0)
                lhs = weight_refs[s][r, :, pl.ds(q, sub), :].reshape(bases * taps * sub, slots * block)
                product = jnp.dot(lhs, picked, preferred_element_type=jnp.float32)
                for k in range(bases):
                    first = row + low_ref[k, row] + HALO
                    for t in range(taps):
                        at = (k * taps + t) * sub
                        total[k, first + t, piece * sub : (piece + 1) * sub] += product[at : at + sub]
            return carry

        lax.fori_loop(0, rows, one_row, 0)

    for d, slot in enumerate(mix_slots):
        for k in range(bases):
            mix_all[place_ref[3 + d], k] = added(slot, k)
    fill = jnp.zeros((padded - channels, width), jnp.bfloat16)
    matrix = jnp.concatenate(
        [x for k in range(bases) for x in [mix_all[p, k] for p in range(owners)] + [fill]], axis=0
    )

    def one_out(first, count):
        at = pl.ds(first + HALO, count)
        lhs = [total[k, at].astype(jnp.bfloat16).reshape(count * span, padded) for k in range(bases)]
        product = jnp.dot(jnp.concatenate(lhs, axis=-1), matrix, preferred_element_type=jnp.float32)
        return product.reshape(count, span, width)

    for lat in range(late):
        mixed[lat * rows : (lat + 1) * rows] = one_out(lat * rows, rows)
    for dl in range(late):
        lat = partner_in_kernel(member, dl, late)
        for dq in range(groups):
            start = pl.multiple_of(partner_in_kernel(group, dq, groups) * cells, 8 if cells % 8 == 0 else cells)
            for r in range(rows):
                outs[dl * groups + dq][r] = mixed[lat * rows + r, pl.ds(start, cells)].astype(jnp.bfloat16)
    if halo:
        for side, first in enumerate((-halo, late * rows)):
            outs[-1][side] = one_out(first, halo).astype(jnp.bfloat16)


def conv_mix(low, shift, place, fields, weights, mix, halo, groups, block):
    bases, all_rows = low.shape
    slots = shift.shape[1]
    late, span, _ = fields[0][0].shape
    owners = len(fields)
    rows = all_rows // late
    depth, width = mix[0][0].shape[1:]
    padded = -(-owners * depth // LANES) * LANES
    taps = weights[0].shape[1] // bases
    sub = math.gcd(span, block)
    shapes = [jax.ShapeDtypeStruct((rows, span // groups, width), jnp.bfloat16)] * (late * groups)
    if halo:
        shapes.append(jax.ShapeDtypeStruct((2, halo, span, width), jnp.bfloat16))
    operands = [x for slot in fields for x in slot] + weights + [x for slot in mix for x in slot]
    counts = ([len(s) for s in fields], len(weights), [len(s) for s in mix])
    return pl.pallas_call(
        functools.partial(conv_mix_kernel, (bases, taps, slots, halo, sub, groups), counts),
        out_shape=shapes,
        in_specs=[SMEM_SPEC] * 3 + [VMEM_SPEC] * len(operands),
        out_specs=[VMEM_SPEC] * len(shapes),
        scratch_shapes=[
            VMEM((rows, owners * span, padded), jnp.bfloat16),
            VMEM((bases, all_rows + 2 * HALO, span, padded), jnp.float32),
            VMEM((owners, bases, depth, width), jnp.bfloat16),
            VMEM((all_rows, span, width), jnp.float32),
        ],
        compiler_params=pltpu.CompilerParams(vmem_limit_bytes=LIMIT),
        name="conv_mix",
    )(low, shift, place, *operands)


def finish_kernel(groups, place_ref, *refs):
    out_ref = refs[-1]
    late = out_ref.shape[0]
    for dl in range(late):
        total = refs[dl * groups][...].astype(jnp.float32)
        for dq in range(1, groups):
            total += refs[dl * groups + dq][...].astype(jnp.float32)
        value = total * (1.0 + lax.erf(total * (0.5**0.5))) * 0.5
        out_ref[partner_in_kernel(place_ref[0], dl, late)] = value.astype(jnp.bfloat16)


def finish(place, parts, groups):
    return pl.pallas_call(
        functools.partial(finish_kernel, groups),
        out_shape=jax.ShapeDtypeStruct((len(parts) // groups,) + parts[0].shape, jnp.bfloat16),
        in_specs=[SMEM_SPEC] + [VMEM_SPEC] * len(parts),
        out_specs=VMEM_SPEC,
        compiler_params=pltpu.CompilerParams(vmem_limit_bytes=LIMIT),
        name="finish",
    )(place, *parts)


def gather_fields(x, owners):
    if owners == 4:
        two = lax.ppermute(x, "lonp", [(0, 2), (2, 0), (1, 3), (3, 1)])
        one = lax.ppermute(x, "lonp", [(0, 1), (1, 0), (2, 3), (3, 2)])
        middle = lax.ppermute(x, "lonp", [(1, 2), (2, 1)])
        passed = lax.ppermute(two, "lonp", [(1, 0), (2, 3)])
        return [[x], [one], [two], [middle, passed]]
    return [[x]] + [[trade(x, "lonp", d, owners)] for d in range(1, owners)]


def gather_mix(x, late, owners):
    core, own = lax.axis_index("late"), lax.axis_index("lonp")
    if owners == 4 and late == 2:
        def both(pairs_first, pairs_second):
            return [(a, b) for a, b in pairs_first] + [(4 + a, 4 + b) for a, b in pairs_second]

        near, far = [(0, 1), (1, 0), (2, 3), (3, 2)], [(0, 2), (2, 0), (1, 3), (3, 1)]
        fetched = lax.ppermute(x, ("late", "lonp"), both(near, far))
        other = trade(fetched, "late", 1, late)
        source = jnp.where(core == 0, x, fetched)
        third = lax.ppermute(source, ("late", "lonp"), both([(1, 2), (2, 1)], [(1, 0), (2, 3)]))
        copied = lax.ppermute(third, ("late", "lonp"), [(1, 5), (2, 6), (4, 0), (7, 3)])
        return [[x], [fetched], [other], [third, copied]], [own, own ^ (1 + core), own ^ (2 - core), own ^ 3]
    slots = [[x]] + [[trade(x, "lonp", d, owners)] for d in range(1, owners)]
    return slots, [partner(own, d, owners) for d in range(owners)]


def per_device(sizes, fields, kernel, band_low, block_shift, mix_weight):
    halves, late, owners, groups = sizes
    members, rows, channels, cells = fields.shape
    bases, _, taps, slots, block, _ = kernel.shape
    all_rows = late * rows
    halo = HALO if halves > 1 else 0

    mix, origins = gather_mix(mix_weight, late, owners)
    packed = pack(fields.transpose(0, 1, 3, 2), groups, owners)
    packed = packed.reshape((late * groups,) + packed.shape[2:])
    spread = lax.all_to_all(packed, ("late", "lonq"), split_axis=0, concat_axis=0, tiled=True)
    gathered = gather_fields(spread.reshape(late, groups * cells, -1), owners)

    own = kernel.transpose(1, 0, 2, 5, 3, 4).reshape(rows, bases * taps, block, slots * block)
    weights = [own] + [trade(own, "late", s, late) for s in range(1, late)]

    start = lax.axis_index("lath") * all_rows
    low = lax.dynamic_slice_in_dim(band_low, start, all_rows, 1)
    shift = lax.dynamic_slice_in_dim(block_shift, start, all_rows, 0)
    place = [lax.axis_index("late"), lax.axis_index("lonp"), lax.axis_index("lonq")] + origins
    place = jnp.stack(place).astype(jnp.int32)
    partial = conv_mix(low, shift, place, gathered, weights, mix, halo, groups, block)
    if halo:
        *partial, beyond = partial
        below = lax.ppermute(beyond[1], "lath", [(i, i + 1) for i in range(halves - 1)])
        above = lax.ppermute(beyond[0], "lath", [(i + 1, i) for i in range(halves - 1)])
        filler = jnp.zeros((all_rows - 2 * halo,) + below.shape[1:], below.dtype)
        extra = jnp.concatenate([below, filler, above], axis=0).reshape(late, rows, groups, cells, -1)
        for dl in range(late):
            lat = partner(lax.axis_index("late"), dl, late)
            for dq in range(groups):
                group = partner(lax.axis_index("lonq"), dq, groups)
                partial[dl * groups + dq] += extra[lat, :, group]
    parts = [
        lax.ppermute(
            partial[dl * groups + dq],
            ("late", "lonq"),
            [
                (l * groups + q, partner(l, dl, late) * groups + partner(q, dq, groups))
                for l in range(late)
                for q in range(groups)
            ],
        )
        if dl or dq
        else partial[0]
        for dl in range(late)
        for dq in range(groups)
    ]
    return finish(place, parts, groups)


def solution(mesh):
    lat, lon = mesh.shape["lat"], mesh.shape["lon"]
    groups = max(g for g in range(1, lon + 1) if lon % g == 0 and g * g <= lon)

    def whole(fields, kernel, band_low, block_shift, mix_weight):
        late = fields.shape[0]
        sizes = (lat // late, late, lon // groups, groups)
        split = Mesh(mesh.devices.reshape(sizes), ("lath", "late", "lonp", "lonq"))
        rows, cells = ("lath", "late"), ("lonp", "lonq")
        return jax.shard_map(
            functools.partial(per_device, sizes),
            mesh=split,
            in_specs=(
                P(None, rows, None, cells),
                P(None, rows, None, None, None, None),
                P(),
                P(),
                P(None, cells, None),
            ),
            out_specs=P(None, rows, cells, None),
            check_vma=False,
        )(fields, kernel, band_low, block_shift, mix_weight)

    return whole
```

```python
import functools
import math

import jax
import jax.numpy as jnp
from jax import lax
from jax.experimental import pallas as pl
from jax.experimental.pallas import tpu as pltpu
from jax.sharding import Mesh
from jax.sharding import PartitionSpec as P

HALO = 2
LANES = 128
VMEM = pltpu.VMEM
LIMIT = 24 * 1024 * 1024
SMEM_SPEC = pl.BlockSpec(memory_space=pltpu.SMEM)
VMEM_SPEC = pl.BlockSpec(memory_space=VMEM)


def partner(index, distance, size):
    if size & (size - 1) == 0:
        return index ^ distance
    return (distance - index) % size


def partner_in_kernel(index, distance, size):
    if size & (size - 1) == 0:
        return lax.bitwise_xor(index, distance)
    return lax.rem(distance - index + size, size)


def trade(x, axis, distance, size):
    return lax.ppermute(x, axis, [(i, partner(i, distance, size)) for i in range(size)])


def pack_kernel(groups, owners, x_ref, out_ref):
    members, rows, cells, channels = x_ref.shape
    width = channels // (groups * owners)
    for e in range(members):
        for q in range(groups):
            parts = [
                x_ref[e, i, :, (p * groups + q) * width : (p * groups + q + 1) * width]
                for i in range(rows)
                for p in range(owners)
            ]
            out_ref[e, q] = jnp.concatenate(parts, axis=-1)


def pack(x, groups, owners):
    members, rows, cells, channels = x.shape
    return pl.pallas_call(
        functools.partial(pack_kernel, groups, owners),
        out_shape=jax.ShapeDtypeStruct((members, groups, cells, rows * channels // groups), x.dtype),
        in_specs=[VMEM_SPEC],
        out_specs=VMEM_SPEC,
        compiler_params=pltpu.CompilerParams(vmem_limit_bytes=LIMIT),
        name="pack",
    )(x)


def added(refs, *at):
    value = refs[0][at]
    for ref in refs[1:]:
        value = value + ref[at]
    return value


def conv_mix_kernel(geometry, counts, low_ref, shift_ref, place_ref, *refs):
    bases, taps, slots, halo, sub, groups = geometry
    refs = list(refs)
    field_slots = [[refs.pop(0) for _ in range(n)] for n in counts[0]]
    weight_refs = [refs.pop(0) for _ in range(counts[1])]
    mix_slots = [[refs.pop(0) for _ in range(n)] for n in counts[2]]
    field_rows, total, mix_all, mixed = refs[-4:]
    outs = refs[:-4]
    late, span, _ = field_slots[0][0].shape
    owners = len(field_slots)
    depth, width = mix_slots[0][0].shape[1:]
    channels = owners * depth
    padded = total.shape[-1]
    rows, _, block, _ = weight_refs[0].shape
    nblocks = owners * span // block
    cells = span // groups
    member, owner, group = place_ref[0], place_ref[1], place_ref[2]

    total[...] = jnp.zeros_like(total)
    field_rows[...] = jnp.zeros_like(field_rows)
    for s in range(late):
        lat = partner_in_kernel(member, s, late)
        for d, slot in enumerate(field_slots):
            base = pl.multiple_of(partner_in_kernel(owner, d, owners) * span, sub)
            value = added(slot, lat)
            for r in range(rows):
                field_rows[r, pl.ds(base, span), :channels] = value[:, r * channels : (r + 1) * channels]

        def one_row(r, carry):
            row = lat * rows + r
            for piece in range(span // sub):
                cell = owner * span + piece * sub
                b = lax.div(cell, block)
                q = pl.multiple_of(lax.rem(cell, block), sub)
                chosen = []
                for j in range(slots):
                    source = lax.rem(b + shift_ref[row, j] + nblocks, nblocks)
                    chosen.append(field_rows[r, pl.ds(pl.multiple_of(source * block, block), block)])
                picked = jnp.concatenate(chosen, axis=0)
                lhs = weight_refs[s][r, :, pl.ds(q, sub), :].reshape(bases * taps * sub, slots * block)
                product = jnp.dot(lhs, picked, preferred_element_type=jnp.float32)
                for k in range(bases):
                    first = row + low_ref[k, row] + HALO
                    for t in range(taps):
                        at = (k * taps + t) * sub
                        total[k, first + t, piece * sub : (piece + 1) * sub] += product[at : at + sub]
            return carry

        lax.fori_loop(0, rows, one_row, 0)

    for d, slot in enumerate(mix_slots):
        for k in range(bases):
            mix_all[place_ref[3 + d], k] = added(slot, k)
    fill = jnp.zeros((padded - channels, width), jnp.bfloat16)
    matrix = jnp.concatenate(
        [x for k in range(bases) for x in [mix_all[p, k] for p in range(owners)] + [fill]], axis=0
    )

    def one_out(first, count):
        at = pl.ds(first + HALO, count)
        lhs = [total[k, at].astype(jnp.bfloat16).reshape(count * span, padded) for k in range(bases)]
        product = jnp.dot(jnp.concatenate(lhs, axis=-1), matrix, preferred_element_type=jnp.float32)
        return product.reshape(count, span, width)

    for lat in range(late):
        mixed[lat * rows : (lat + 1) * rows] = one_out(lat * rows, rows)
    for dl in range(late):
        lat = partner_in_kernel(member, dl, late)
        for dq in range(groups):
            start = pl.multiple_of(partner_in_kernel(group, dq, groups) * cells, 8 if cells % 8 == 0 else cells)
            for r in range(rows):
                outs[dl * groups + dq][r] = mixed[lat * rows + r, pl.ds(start, cells)].astype(jnp.bfloat16)
    if halo:
        for side, first in enumerate((-halo, late * rows)):
            outs[-1][side] = one_out(first, halo).astype(jnp.bfloat16)


def conv_mix(low, shift, place, fields, weights, mix, halo, groups, block):
    bases, all_rows = low.shape
    slots = shift.shape[1]
    late, span, _ = fields[0][0].shape
    owners = len(fields)
    rows = all_rows // late
    depth, width = mix[0][0].shape[1:]
    padded = -(-owners * depth // LANES) * LANES
    taps = weights[0].shape[1] // bases
    sub = math.gcd(span, block)
    shapes = [jax.ShapeDtypeStruct((rows, span // groups, width), jnp.bfloat16)] * (late * groups)
    if halo:
        shapes.append(jax.ShapeDtypeStruct((2, halo, span, width), jnp.bfloat16))
    operands = [x for slot in fields for x in slot] + weights + [x for slot in mix for x in slot]
    counts = ([len(s) for s in fields], len(weights), [len(s) for s in mix])
    return pl.pallas_call(
        functools.partial(conv_mix_kernel, (bases, taps, slots, halo, sub, groups), counts),
        out_shape=shapes,
        in_specs=[SMEM_SPEC] * 3 + [VMEM_SPEC] * len(operands),
        out_specs=[VMEM_SPEC] * len(shapes),
        scratch_shapes=[
            VMEM((rows, owners * span, padded), jnp.bfloat16),
            VMEM((bases, all_rows + 2 * HALO, span, padded), jnp.float32),
            VMEM((owners, bases, depth, width), jnp.bfloat16),
            VMEM((all_rows, span, width), jnp.float32),
        ],
        compiler_params=pltpu.CompilerParams(vmem_limit_bytes=LIMIT),
        name="conv_mix",
    )(low, shift, place, *operands)


def finish_kernel(groups, place_ref, *refs):
    out_ref = refs[-1]
    late = out_ref.shape[0]
    for dl in range(late):
        total = refs[dl * groups][...].astype(jnp.float32)
        for dq in range(1, groups):
            total += refs[dl * groups + dq][...].astype(jnp.float32)
        value = total * (1.0 + lax.erf(total * (0.5**0.5))) * 0.5
        out_ref[partner_in_kernel(place_ref[0], dl, late)] = value.astype(jnp.bfloat16)


def finish(place, parts, groups):
    return pl.pallas_call(
        functools.partial(finish_kernel, groups),
        out_shape=jax.ShapeDtypeStruct((len(parts) // groups,) + parts[0].shape, jnp.bfloat16),
        in_specs=[SMEM_SPEC] + [VMEM_SPEC] * len(parts),
        out_specs=VMEM_SPEC,
        compiler_params=pltpu.CompilerParams(vmem_limit_bytes=LIMIT),
        name="finish",
    )(place, *parts)


def chain(*cores):
    return [(4 * c + a, 4 * c + b) for c, pairs in enumerate(cores) for a, b in pairs]


NEAR = [(0, 1), (1, 0), (2, 3), (3, 2)]
FAR = [(0, 2), (2, 0), (1, 3), (3, 1)]
MIDDLE = [(1, 2), (2, 1)]
ENDS = [(1, 0), (2, 3)]


def both_kernels(kernel, late):
    bases, rows, taps, slots, block, _ = kernel.shape
    own = kernel.transpose(1, 0, 2, 5, 3, 4).reshape(rows, bases * taps, block, slots * block)
    return [own] + [trade(own, "late", s, late) for s in range(1, late)]


def gather(packed, kernel, mix, late, groups, owners):
    core, own = lax.axis_index("late"), lax.axis_index("lonp")
    chained = owners == 4 and late == 2
    if chained:
        mix, packed = lax.optimization_barrier((mix, packed))
        fetched = lax.ppermute(mix, ("late", "lonp"), chain(NEAR, FAR))
    cells = packed.shape[1]
    x = lax.all_to_all(packed, ("late", "lonq"), split_axis=0, concat_axis=0, tiled=True)
    x = x.reshape(late, groups * cells, -1)
    if not chained:
        weights = both_kernels(kernel, late)
        fields = [[x]] + [[trade(x, "lonp", d, owners)] for d in range(1, owners)]
        mixes = [[mix]] + [[trade(mix, "lonp", d, owners)] for d in range(1, owners)]
        return fields, weights, mixes, [partner(own, d, owners) for d in range(owners)]
    two = lax.ppermute(x, "lonp", FAR)
    one = lax.ppermute(x, "lonp", NEAR)
    other = trade(fetched, "late", 1, late)
    source = jnp.where(core == 0, mix, fetched)
    third = lax.ppermute(source, ("late", "lonp"), chain(MIDDLE, ENDS))
    copied = lax.ppermute(third, ("late", "lonp"), [(1, 5), (2, 6), (4, 0), (7, 3)])
    kernel, third = lax.optimization_barrier((kernel, third))
    weights = both_kernels(kernel, late)
    late_x, two, other, third = lax.optimization_barrier((x, two, other, third))
    middle = lax.ppermute(late_x, "lonp", MIDDLE)
    passed = lax.ppermute(two, "lonp", ENDS)
    origins = [own, own ^ (1 + core), own ^ (2 - core), own ^ 3]
    return [[x], [one], [two], [middle, passed]], weights, [[mix], [fetched], [other], [third, copied]], origins


def per_device(sizes, fields, kernel, band_low, block_shift, mix_weight):
    halves, late, owners, groups = sizes
    members, rows, channels, cells = fields.shape
    bases, _, taps, slots, block, _ = kernel.shape
    all_rows = late * rows
    halo = HALO if halves > 1 else 0

    packed = pack(fields.transpose(0, 1, 3, 2), groups, owners)
    packed = packed.reshape((late * groups,) + packed.shape[2:])
    gathered, weights, mix, origins = gather(packed, kernel, mix_weight, late, groups, owners)

    start = lax.axis_index("lath") * all_rows
    low = lax.dynamic_slice_in_dim(band_low, start, all_rows, 1)
    shift = lax.dynamic_slice_in_dim(block_shift, start, all_rows, 0)
    place = [lax.axis_index("late"), lax.axis_index("lonp"), lax.axis_index("lonq")] + origins
    place = jnp.stack(place).astype(jnp.int32)
    partial = conv_mix(low, shift, place, gathered, weights, mix, halo, groups, block)
    if halo:
        *partial, beyond = partial
        below = lax.ppermute(beyond[1], "lath", [(i, i + 1) for i in range(halves - 1)])
        above = lax.ppermute(beyond[0], "lath", [(i + 1, i) for i in range(halves - 1)])
        filler = jnp.zeros((all_rows - 2 * halo,) + below.shape[1:], below.dtype)
        extra = jnp.concatenate([below, filler, above], axis=0).reshape(late, rows, groups, cells, -1)
        for dl in range(late):
            lat = partner(lax.axis_index("late"), dl, late)
            for dq in range(groups):
                group = partner(lax.axis_index("lonq"), dq, groups)
                partial[dl * groups + dq] += extra[lat, :, group]
    parts = [
        lax.ppermute(
            partial[dl * groups + dq],
            ("late", "lonq"),
            [
                (l * groups + q, partner(l, dl, late) * groups + partner(q, dq, groups))
                for l in range(late)
                for q in range(groups)
            ],
        )
        if dl or dq
        else partial[0]
        for dl in range(late)
        for dq in range(groups)
    ]
    return finish(place, parts, groups)


def solution(mesh):
    lat, lon = mesh.shape["lat"], mesh.shape["lon"]
    groups = max(g for g in range(1, lon + 1) if lon % g == 0 and g * g <= lon)

    def whole(fields, kernel, band_low, block_shift, mix_weight):
        late = fields.shape[0]
        sizes = (lat // late, late, lon // groups, groups)
        split = Mesh(mesh.devices.reshape(sizes), ("lath", "late", "lonp", "lonq"))
        rows, cells = ("lath", "late"), ("lonp", "lonq")
        return jax.shard_map(
            functools.partial(per_device, sizes),
            mesh=split,
            in_specs=(
                P(None, rows, None, cells),
                P(None, rows, None, None, None, None),
                P(),
                P(),
                P(None, cells, None),
            ),
            out_specs=P(None, rows, cells, None),
            check_vma=False,
        )(fields, kernel, band_low, block_shift, mix_weight)

    return whole
```

```python
import functools
import math

import jax
import jax.numpy as jnp
from jax import lax
from jax.experimental import pallas as pl
from jax.experimental.pallas import tpu as pltpu
from jax.sharding import Mesh
from jax.sharding import PartitionSpec as P

HALO = 2
LANES = 128
VMEM = pltpu.VMEM
LIMIT = 24 * 1024 * 1024
SMEM_SPEC = pl.BlockSpec(memory_space=pltpu.SMEM)
VMEM_SPEC = pl.BlockSpec(memory_space=VMEM)


def partner(index, distance, size):
    if size & (size - 1) == 0:
        return index ^ distance
    return (distance - index) % size


def partner_in_kernel(index, distance, size):
    if size & (size - 1) == 0:
        return lax.bitwise_xor(index, distance)
    return lax.rem(distance - index + size, size)


def trade(x, axis, distance, size):
    return lax.ppermute(x, axis, [(i, partner(i, distance, size)) for i in range(size)])


def pack_kernel(groups, owners, x_ref, out_ref):
    members, rows, cells, channels = x_ref.shape
    width = channels // (groups * owners)
    for e in range(members):
        for q in range(groups):
            parts = [
                x_ref[e, i, :, (p * groups + q) * width : (p * groups + q + 1) * width]
                for i in range(rows)
                for p in range(owners)
            ]
            block = jnp.concatenate(parts, axis=-1)
            for p in range(owners):
                out_ref[e, p, q] = block


def pack(x, groups, owners):
    members, rows, cells, channels = x.shape
    return pl.pallas_call(
        functools.partial(pack_kernel, groups, owners),
        out_shape=jax.ShapeDtypeStruct((members, owners, groups, cells, rows * channels // groups), x.dtype),
        in_specs=[VMEM_SPEC],
        out_specs=VMEM_SPEC,
        compiler_params=pltpu.CompilerParams(vmem_limit_bytes=LIMIT),
        name="pack",
    )(x)


def added(refs, *at):
    value = refs[0][at]
    for ref in refs[1:]:
        value = value + ref[at]
    return value


def conv_mix_kernel(geometry, counts, low_ref, shift_ref, place_ref, *refs):
    bases, taps, slots, halo, sub, groups = geometry
    refs = list(refs)
    fields_ref = refs.pop(0)
    weight_refs = [refs.pop(0) for _ in range(counts[0])]
    mix_slots = [[refs.pop(0) for _ in range(n)] for n in counts[1]]
    field_rows, total, mix_all, mixed = refs[-4:]
    outs = refs[:-4]
    late, owners, span, _ = fields_ref.shape
    depth, width = mix_slots[0][0].shape[1:]
    channels = owners * depth
    padded = total.shape[-1]
    rows, _, block, _ = weight_refs[0].shape
    nblocks = owners * span // block
    cells = span // groups
    member, owner, group = place_ref[0], place_ref[1], place_ref[2]

    total[...] = jnp.zeros_like(total)
    field_rows[...] = jnp.zeros_like(field_rows)
    for s in range(late):
        lat = partner_in_kernel(member, s, late)
        for p in range(owners):
            value = fields_ref[lat, p]
            for r in range(rows):
                field_rows[r, p * span : (p + 1) * span, :channels] = value[:, r * channels : (r + 1) * channels]

        def one_row(r, carry):
            row = lat * rows + r
            for piece in range(span // sub):
                cell = owner * span + piece * sub
                b = lax.div(cell, block)
                q = pl.multiple_of(lax.rem(cell, block), sub)
                chosen = []
                for j in range(slots):
                    source = lax.rem(b + shift_ref[row, j] + nblocks, nblocks)
                    chosen.append(field_rows[r, pl.ds(pl.multiple_of(source * block, block), block)])
                picked = jnp.concatenate(chosen, axis=0)
                lhs = weight_refs[s][r, :, pl.ds(q, sub), :].reshape(bases * taps * sub, slots * block)
                product = jnp.dot(lhs, picked, preferred_element_type=jnp.float32)
                for k in range(bases):
                    at = pl.ds(row + low_ref[k, row] + HALO, taps)
                    slab = product[k * taps * sub : (k + 1) * taps * sub].reshape(taps, sub, padded)
                    total[k, at, piece * sub : (piece + 1) * sub] += slab
            return carry

        lax.fori_loop(0, rows, one_row, 0)

    for d, slot in enumerate(mix_slots):
        for k in range(bases):
            mix_all[place_ref[3 + d], k] = added(slot, k)
    fill = jnp.zeros((padded - channels, width), jnp.bfloat16)
    matrix = jnp.concatenate(
        [x for k in range(bases) for x in [mix_all[p, k] for p in range(owners)] + [fill]], axis=0
    )

    def one_out(first, count):
        at = pl.ds(first + HALO, count)
        lhs = [total[k, at].astype(jnp.bfloat16).reshape(count * span, padded) for k in range(bases)]
        product = jnp.dot(jnp.concatenate(lhs, axis=-1), matrix, preferred_element_type=jnp.float32)
        return product.reshape(count, span, width)

    for lat in range(late):
        mixed[lat * rows : (lat + 1) * rows] = one_out(lat * rows, rows)
    for dl in range(late):
        lat = partner_in_kernel(member, dl, late)
        for dq in range(groups):
            start = pl.multiple_of(partner_in_kernel(group, dq, groups) * cells, 8 if cells % 8 == 0 else cells)
            for r in range(rows):
                outs[dl * groups + dq][r] = mixed[lat * rows + r, pl.ds(start, cells)].astype(jnp.bfloat16)
    if halo:
        for side, first in enumerate((-halo, late * rows)):
            outs[-1][side] = one_out(first, halo).astype(jnp.bfloat16)


def conv_mix(low, shift, place, fields, weights, mix, halo, groups, block):
    bases, all_rows = low.shape
    slots = shift.shape[1]
    late, owners, span, _ = fields.shape
    rows = all_rows // late
    depth, width = mix[0][0].shape[1:]
    padded = -(-owners * depth // LANES) * LANES
    taps = weights[0].shape[1] // bases
    sub = math.gcd(span, block)
    shapes = [jax.ShapeDtypeStruct((rows, span // groups, width), jnp.bfloat16)] * (late * groups)
    if halo:
        shapes.append(jax.ShapeDtypeStruct((2, halo, span, width), jnp.bfloat16))
    operands = [fields] + weights + [x for slot in mix for x in slot]
    counts = (len(weights), [len(s) for s in mix])
    return pl.pallas_call(
        functools.partial(conv_mix_kernel, (bases, taps, slots, halo, sub, groups), counts),
        out_shape=shapes,
        in_specs=[SMEM_SPEC] * 3 + [VMEM_SPEC] * len(operands),
        out_specs=[VMEM_SPEC] * len(shapes),
        scratch_shapes=[
            VMEM((rows, owners * span, padded), jnp.bfloat16),
            VMEM((bases, all_rows + 2 * HALO, span, padded), jnp.float32),
            VMEM((owners, bases, depth, width), jnp.bfloat16),
            VMEM((all_rows, span, width), jnp.float32),
        ],
        compiler_params=pltpu.CompilerParams(vmem_limit_bytes=LIMIT),
        name="conv_mix",
    )(low, shift, place, *operands)


def finish_kernel(groups, place_ref, *refs):
    out_ref = refs[-1]
    late = out_ref.shape[0]
    for dl in range(late):
        total = refs[dl * groups][...].astype(jnp.float32)
        for dq in range(1, groups):
            total += refs[dl * groups + dq][...].astype(jnp.float32)
        value = total * (1.0 + lax.erf(total * (0.5**0.5))) * 0.5
        out_ref[partner_in_kernel(place_ref[0], dl, late)] = value.astype(jnp.bfloat16)


def finish(place, parts, groups):
    return pl.pallas_call(
        functools.partial(finish_kernel, groups),
        out_shape=jax.ShapeDtypeStruct((len(parts) // groups,) + parts[0].shape, jnp.bfloat16),
        in_specs=[SMEM_SPEC] + [VMEM_SPEC] * len(parts),
        out_specs=VMEM_SPEC,
        compiler_params=pltpu.CompilerParams(vmem_limit_bytes=LIMIT),
        name="finish",
    )(place, *parts)


def both_kernels(kernel, late):
    bases, rows, taps, slots, block, _ = kernel.shape
    own = kernel.transpose(1, 0, 2, 5, 3, 4).reshape(rows, bases * taps, block, slots * block)
    return [own] + [trade(own, "late", s, late) for s in range(1, late)]


def gather_mix(mix, late, owners):
    core, own = lax.axis_index("late"), lax.axis_index("lonp")
    if owners == 4 and late == 2:
        def fetch(distances):
            route = [
                (c * owners + p, c * owners + (p ^ d)) for p in range(owners) for c, d in enumerate(distances(p)) if d
            ]
            return lax.ppermute(mix, ("late", "lonp"), route)

        first = fetch(lambda p: (1, 2))
        third = fetch(lambda p: (3, 0) if p in (0, 3) else (0, 3))
        other = trade(first, "late", 1, late)
        copied = trade(third, "late", 1, late)
        return [[mix], [first], [other], [third, copied]], [own, own ^ (1 + core), own ^ (2 - core), own ^ 3]
    slots = [[mix]] + [[trade(mix, "lonp", d, owners)] for d in range(1, owners)]
    return slots, [partner(own, d, owners) for d in range(owners)]


def per_device(sizes, fields, kernel, band_low, block_shift, mix_weight):
    halves, late, owners, groups = sizes
    members, rows, channels, cells = fields.shape
    bases, _, taps, slots, block, _ = kernel.shape
    all_rows = late * rows
    halo = HALO if halves > 1 else 0

    packed = pack(fields.transpose(0, 1, 3, 2), groups, owners)
    packed = packed.reshape((-1,) + packed.shape[3:])
    spread = lax.all_to_all(packed, ("late", "lonp", "lonq"), split_axis=0, concat_axis=0, tiled=True)
    spread = spread.reshape(late, owners, groups * cells, -1)
    weights = both_kernels(kernel, late)
    mix, origins = gather_mix(mix_weight, late, owners)

    start = lax.axis_index("lath") * all_rows
    low = lax.dynamic_slice_in_dim(band_low, start, all_rows, 1)
    shift = lax.dynamic_slice_in_dim(block_shift, start, all_rows, 0)
    place = [lax.axis_index("late"), lax.axis_index("lonp"), lax.axis_index("lonq")] + origins
    place = jnp.stack(place).astype(jnp.int32)
    partial = conv_mix(low, shift, place, spread, weights, mix, halo, groups, block)
    if halo:
        *partial, beyond = partial
        below = lax.ppermute(beyond[1], "lath", [(i, i + 1) for i in range(halves - 1)])
        above = lax.ppermute(beyond[0], "lath", [(i + 1, i) for i in range(halves - 1)])
        filler = jnp.zeros((all_rows - 2 * halo,) + below.shape[1:], below.dtype)
        extra = jnp.concatenate([below, filler, above], axis=0).reshape(late, rows, groups, cells, -1)
        for dl in range(late):
            lat = partner(lax.axis_index("late"), dl, late)
            for dq in range(groups):
                group = partner(lax.axis_index("lonq"), dq, groups)
                partial[dl * groups + dq] += extra[lat, :, group]
    parts = [
        lax.ppermute(
            partial[dl * groups + dq],
            ("late", "lonq"),
            [
                (l * groups + q, partner(l, dl, late) * groups + partner(q, dq, groups))
                for l in range(late)
                for q in range(groups)
            ],
        )
        if dl or dq
        else partial[0]
        for dl in range(late)
        for dq in range(groups)
    ]
    return finish(place, parts, groups)


def solution(mesh):
    lat, lon = mesh.shape["lat"], mesh.shape["lon"]
    groups = max(g for g in range(1, lon + 1) if lon % g == 0 and g * g <= lon)

    def whole(fields, kernel, band_low, block_shift, mix_weight):
        late = fields.shape[0]
        sizes = (lat // late, late, lon // groups, groups)
        split = Mesh(mesh.devices.reshape(sizes), ("lath", "late", "lonp", "lonq"))
        rows, cells = ("lath", "late"), ("lonp", "lonq")
        return jax.shard_map(
            functools.partial(per_device, sizes),
            mesh=split,
            in_specs=(
                P(None, rows, None, cells),
                P(None, rows, None, None, None, None),
                P(),
                P(),
                P(None, cells, None),
            ),
            out_specs=P(None, rows, cells, None),
            check_vma=False,
        )(fields, kernel, band_low, block_shift, mix_weight)

    return whole
```

```python
import functools
import math

import jax
import jax.numpy as jnp
from jax import lax
from jax.experimental import pallas as pl
from jax.experimental.pallas import tpu as pltpu
from jax.sharding import Mesh
from jax.sharding import PartitionSpec as P

HALO = 2
LANES = 128
VMEM = pltpu.VMEM
LIMIT = 24 * 1024 * 1024
SMEM_SPEC = pl.BlockSpec(memory_space=pltpu.SMEM)
VMEM_SPEC = pl.BlockSpec(memory_space=VMEM)


def partner(index, distance, size):
    if size & (size - 1) == 0:
        return index ^ distance
    return (distance - index) % size


def partner_in_kernel(index, distance, size):
    if size & (size - 1) == 0:
        return lax.bitwise_xor(index, distance)
    return lax.rem(distance - index + size, size)


def trade(x, axis, distance, size):
    return lax.ppermute(x, axis, [(i, partner(i, distance, size)) for i in range(size)])


def pack_kernel(parts, x_ref, out_ref):
    members, rows, cells, channels = x_ref.shape
    na, nb, nc, nd = parts
    width = channels // (na * nb * nc * nd)
    for e in range(members):
        for b in range(nb):
            for d in range(nd):
                firsts = [(((a * nb + b) * nc + c) * nd + d) * width for a in range(na) for c in range(nc)]
                taken = [x_ref[e, i, :, at : at + width] for i in range(rows) for at in firsts]
                block = jnp.concatenate(taken, axis=-1)
                for a in range(na):
                    out_ref[e, a, b, d] = block


def pack(x, parts):
    members, rows, cells, channels = x.shape
    na, nb, _, nd = parts
    return pl.pallas_call(
        functools.partial(pack_kernel, parts),
        out_shape=jax.ShapeDtypeStruct((members, na, nb, nd, cells, rows * channels // (nb * nd)), x.dtype),
        in_specs=[VMEM_SPEC],
        out_specs=VMEM_SPEC,
        compiler_params=pltpu.CompilerParams(vmem_limit_bytes=LIMIT),
        name="pack",
    )(x)


def added(refs, *at):
    value = refs[0][at]
    for ref in refs[1:]:
        value = value + ref[at]
    return value


def conv_mix_kernel(geometry, counts, low_ref, shift_ref, place_ref, *refs):
    bases, taps, slots, halo, sub, groups = geometry
    refs = list(refs)
    field_refs = [refs.pop(0) for _ in range(counts[0])]
    weight_refs = [refs.pop(0) for _ in range(counts[1])]
    mix_slots = [[refs.pop(0) for _ in range(n)] for n in counts[2]]
    field_rows, total, mix_all, mixed = refs[-4:]
    outs = refs[:-4]
    late, na, nb, stripe, _ = field_refs[0].shape
    nc = len(field_refs)
    span = nb * stripe
    owners = len(mix_slots)
    depth, width = mix_slots[0][0].shape[1:]
    channels = owners * depth
    padded = total.shape[-1]
    rows, _, block, _ = weight_refs[0].shape
    nblocks = field_rows.shape[1] // block
    cells = span // groups
    member, place_a, place_c, group = [place_ref[i] for i in range(4)]

    total[...] = jnp.zeros_like(total)
    field_rows[...] = jnp.zeros_like(field_rows)
    for s in range(late):
        lat = partner_in_kernel(member, s, late)
        for a in range(na):
            for b in range(nb):
                for dc, ref in enumerate(field_refs):
                    stripe_at = (a * nb + b) * nc + partner_in_kernel(place_c, dc, nc)
                    at = pl.ds(pl.multiple_of(stripe_at * stripe, sub), stripe)
                    value = ref[lat, a, b]
                    for r in range(rows):
                        field_rows[r, at, :channels] = value[:, r * channels : (r + 1) * channels]

        def one_row(r, carry):
            row = lat * rows + r
            for piece in range(span // sub):
                b_at, in_stripe = divmod(piece * sub, stripe)
                cell = ((place_a * nb + b_at) * nc + place_c) * stripe + in_stripe
                b = lax.div(cell, block)
                q = pl.multiple_of(lax.rem(cell, block), sub)
                chosen = []
                for j in range(slots):
                    source = lax.rem(b + shift_ref[row, j] + nblocks, nblocks)
                    chosen.append(field_rows[r, pl.ds(pl.multiple_of(source * block, block), block)])
                picked = jnp.concatenate(chosen, axis=0)
                lhs = weight_refs[s][r, :, pl.ds(q, sub), :].reshape(bases * taps * sub, slots * block)
                product = jnp.dot(lhs, picked, preferred_element_type=jnp.float32)
                for k in range(bases):
                    at = pl.ds(row + low_ref[k, row] + HALO, taps)
                    slab = product[k * taps * sub : (k + 1) * taps * sub].reshape(taps, sub, padded)
                    total[k, at, piece * sub : (piece + 1) * sub] += slab
            return carry

        lax.fori_loop(0, rows, one_row, 0)

    for d, slot in enumerate(mix_slots):
        for k in range(bases):
            mix_all[place_ref[4 + d], k] = added(slot, k)
    fill = jnp.zeros((padded - channels, width), jnp.bfloat16)
    matrix = jnp.concatenate(
        [x for k in range(bases) for x in [mix_all[p, k] for p in range(owners)] + [fill]], axis=0
    )

    def one_out(first, count):
        at = pl.ds(first + HALO, count)
        lhs = [total[k, at].astype(jnp.bfloat16).reshape(count * span, padded) for k in range(bases)]
        product = jnp.dot(jnp.concatenate(lhs, axis=-1), matrix, preferred_element_type=jnp.float32)
        return product.reshape(count, span, width)

    for lat in range(late):
        mixed[lat * rows : (lat + 1) * rows] = one_out(lat * rows, rows)
    for dl in range(late):
        lat = partner_in_kernel(member, dl, late)
        for dq in range(groups):
            start = pl.multiple_of(partner_in_kernel(group, dq, groups) * cells, 8 if cells % 8 == 0 else cells)
            for r in range(rows):
                outs[dl * groups + dq][r] = mixed[lat * rows + r, pl.ds(start, cells)].astype(jnp.bfloat16)
    if halo:
        for side, first in enumerate((-halo, late * rows)):
            outs[-1][side] = one_out(first, halo).astype(jnp.bfloat16)


def conv_mix(low, shift, place, fields, weights, mix, halo, groups, block):
    bases, all_rows = low.shape
    slots = shift.shape[1]
    late, na, nb, stripe, _ = fields[0].shape
    span = nb * stripe
    longitudes = na * len(fields) * span
    owners = len(mix)
    rows = all_rows // late
    depth, width = mix[0][0].shape[1:]
    padded = -(-owners * depth // LANES) * LANES
    taps = weights[0].shape[1] // bases
    sub = math.gcd(stripe, block)
    shapes = [jax.ShapeDtypeStruct((rows, span // groups, width), jnp.bfloat16)] * (late * groups)
    if halo:
        shapes.append(jax.ShapeDtypeStruct((2, halo, span, width), jnp.bfloat16))
    operands = fields + weights + [x for slot in mix for x in slot]
    counts = (len(fields), len(weights), [len(s) for s in mix])
    return pl.pallas_call(
        functools.partial(conv_mix_kernel, (bases, taps, slots, halo, sub, groups), counts),
        out_shape=shapes,
        in_specs=[SMEM_SPEC] * 3 + [VMEM_SPEC] * len(operands),
        out_specs=[VMEM_SPEC] * len(shapes),
        scratch_shapes=[
            VMEM((rows, longitudes, padded), jnp.bfloat16),
            VMEM((bases, all_rows + 2 * HALO, span, padded), jnp.float32),
            VMEM((owners, bases, depth, width), jnp.bfloat16),
            VMEM((all_rows, span, width), jnp.float32),
        ],
        compiler_params=pltpu.CompilerParams(vmem_limit_bytes=LIMIT),
        name="conv_mix",
    )(low, shift, place, *operands)


def finish_kernel(groups, place_ref, *refs):
    out_ref = refs[-1]
    late = out_ref.shape[0]
    for dl in range(late):
        total = refs[dl * groups][...].astype(jnp.float32)
        for dq in range(1, groups):
            total += refs[dl * groups + dq][...].astype(jnp.float32)
        value = total * (1.0 + lax.erf(total * (0.5**0.5))) * 0.5
        out_ref[partner_in_kernel(place_ref[0], dl, late)] = value.astype(jnp.bfloat16)


def finish(place, parts, groups):
    return pl.pallas_call(
        functools.partial(finish_kernel, groups),
        out_shape=jax.ShapeDtypeStruct((len(parts) // groups,) + parts[0].shape, jnp.bfloat16),
        in_specs=[SMEM_SPEC] + [VMEM_SPEC] * len(parts),
        out_specs=VMEM_SPEC,
        compiler_params=pltpu.CompilerParams(vmem_limit_bytes=LIMIT),
        name="finish",
    )(place, *parts)


def both_kernels(kernel, late):
    bases, rows, taps, slots, block, _ = kernel.shape
    own = kernel.transpose(1, 0, 2, 5, 3, 4).reshape(rows, bases * taps, block, slots * block)
    return [own] + [trade(own, "late", s, late) for s in range(1, late)]


def gather_mix(mix, late, na, nc):
    core, own = lax.axis_index("late"), lax.axis_index("a") * nc + lax.axis_index("c")
    owners = na * nc
    if na == nc == late == 2:
        route = [(p, p ^ 2) for p in range(4)] + [(4 + p, 4 + (p ^ 1)) for p in range(4)]
        first = lax.ppermute(mix, ("late", "a", "c"), route)
        third = lax.ppermute(mix, ("late", "a", "c"), [(4 + p, 4 + (p ^ 3)) for p in range(4)])
        other = trade(first, "late", 1, late)
        copied = lax.ppermute(third, "late", [(1, 0)])
        return [[mix], [first], [other], [third, copied]], [own, own ^ (2 - core), own ^ (1 + core), own ^ 3]
    slots = [[mix]] + [[trade(mix, ("a", "c"), d, owners)] for d in range(1, owners)]
    return slots, [partner(own, d, owners) for d in range(owners)]


def per_device(sizes, fields, kernel, band_low, block_shift, mix_weight):
    halves, late, na, nb, nc, nd = sizes
    groups = nb * nd
    members, rows, channels, cells = fields.shape
    block = kernel.shape[-1]
    all_rows = late * rows
    halo = HALO if halves > 1 else 0

    packed = pack(fields.transpose(0, 1, 3, 2), sizes[2:])
    packed = packed.reshape((-1,) + packed.shape[4:])
    spread = lax.all_to_all(packed, ("late", "a", "b", "d"), split_axis=0, concat_axis=0, tiled=True)
    weights = both_kernels(kernel, late)
    mix_weight, spread = lax.optimization_barrier((mix_weight, spread))
    spread = spread.reshape(late, na, nb, nd * cells, -1)
    spread = [spread] + [trade(spread, "c", s, nc) for s in range(1, nc)]
    mix, origins = gather_mix(mix_weight, late, na, nc)

    start = lax.axis_index("lath") * all_rows
    low = lax.dynamic_slice_in_dim(band_low, start, all_rows, 1)
    shift = lax.dynamic_slice_in_dim(block_shift, start, all_rows, 0)
    group = lax.axis_index("b") * nd + lax.axis_index("d")
    place = [lax.axis_index("late"), lax.axis_index("a"), lax.axis_index("c"), group] + origins
    place = jnp.stack(place).astype(jnp.int32)
    partial = conv_mix(low, shift, place, spread, weights, mix, halo, groups, block)
    if halo:
        *partial, beyond = partial
        below = lax.ppermute(beyond[1], "lath", [(i, i + 1) for i in range(halves - 1)])
        above = lax.ppermute(beyond[0], "lath", [(i + 1, i) for i in range(halves - 1)])
        filler = jnp.zeros((all_rows - 2 * halo,) + below.shape[1:], below.dtype)
        extra = jnp.concatenate([below, filler, above], axis=0).reshape(late, rows, groups, cells, -1)
        for dl in range(late):
            lat = partner(lax.axis_index("late"), dl, late)
            for dq in range(groups):
                partial[dl * groups + dq] += extra[lat, :, partner(group, dq, groups)]
    parts = [
        lax.ppermute(
            partial[dl * groups + dq],
            ("late", "b", "d"),
            [
                (l * groups + q, partner(l, dl, late) * groups + partner(q, dq, groups))
                for l in range(late)
                for q in range(groups)
            ],
        )
        if dl or dq
        else partial[0]
        for dl in range(late)
        for dq in range(groups)
    ]
    return finish(place, parts, groups)


def solution(mesh):
    lat, lon = mesh.shape["lat"], mesh.shape["lon"]
    halves = [2 if lon % 8 == 0 else 1] * 3

    def whole(fields, kernel, band_low, block_shift, mix_weight):
        late = fields.shape[0]
        sizes = (lat // late, late, lon // math.prod(halves), *halves)
        split = Mesh(mesh.devices.reshape(sizes), ("lath", "late", "a", "b", "c", "d"))
        rows, cells = ("lath", "late"), ("a", "b", "c", "d")
        return jax.shard_map(
            functools.partial(per_device, sizes),
            mesh=split,
            in_specs=(
                P(None, rows, None, cells),
                P(None, rows, None, None, None, None),
                P(),
                P(),
                P(None, cells, None),
            ),
            out_specs=P(None, rows, cells, None),
            check_vma=False,
        )(fields, kernel, band_low, block_shift, mix_weight)

    return whole
```

```python
import functools
import math

import jax
import jax.numpy as jnp
from jax import lax
from jax.experimental import pallas as pl
from jax.experimental.pallas import tpu as pltpu
from jax.sharding import Mesh
from jax.sharding import PartitionSpec as P

HALO = 2
LANES = 128
VMEM = pltpu.VMEM
LIMIT = 24 * 1024 * 1024
SMEM_SPEC = pl.BlockSpec(memory_space=pltpu.SMEM)
VMEM_SPEC = pl.BlockSpec(memory_space=VMEM)


def partner(index, distance, size):
    if size & (size - 1) == 0:
        return index ^ distance
    return (distance - index) % size


def partner_in_kernel(index, distance, size):
    if size & (size - 1) == 0:
        return lax.bitwise_xor(index, distance)
    return lax.rem(distance - index + size, size)


def trade(x, axis, distance, size):
    return lax.ppermute(x, axis, [(i, partner(i, distance, size)) for i in range(size)])


def pack_kernel(groups, owners, x_ref, out_ref):
    members, rows, cells, channels = x_ref.shape
    width = channels // (groups * owners)
    for e in range(members):
        for q in range(groups):
            parts = [
                x_ref[e, i, :, (p * groups + q) * width : (p * groups + q + 1) * width]
                for i in range(rows)
                for p in range(owners)
            ]
            block = jnp.concatenate(parts, axis=-1)
            for p in range(owners):
                out_ref[e, p, q] = block


def pack(x, groups, owners):
    members, rows, cells, channels = x.shape
    return pl.pallas_call(
        functools.partial(pack_kernel, groups, owners),
        out_shape=jax.ShapeDtypeStruct((members, owners, groups, cells, rows * channels // groups), x.dtype),
        in_specs=[VMEM_SPEC],
        out_specs=VMEM_SPEC,
        compiler_params=pltpu.CompilerParams(vmem_limit_bytes=LIMIT),
        name="pack",
    )(x)


def added(refs, *at):
    value = refs[0][at]
    for ref in refs[1:]:
        value = value + ref[at]
    return value


def conv_mix_kernel(geometry, counts, low_ref, shift_ref, place_ref, *refs):
    bases, taps, slots, halo, sub, groups = geometry
    refs = list(refs)
    fields_ref = refs.pop(0)
    weight_refs = [refs.pop(0) for _ in range(counts[0])]
    mix_slots = [[refs.pop(0) for _ in range(n)] for n in counts[1]]
    field_rows, total, mix_all, mixed = refs[-4:]
    outs = refs[:-4]
    late, owners, span, _ = fields_ref.shape
    depth, width = mix_slots[0][0].shape[1:]
    channels = owners * depth
    padded = total.shape[-1]
    rows, _, block, _ = weight_refs[0].shape
    nblocks = owners * span // block
    cells = span // groups
    member, owner, group = place_ref[0], place_ref[1], place_ref[2]

    total[...] = jnp.zeros_like(total)
    field_rows[...] = jnp.zeros_like(field_rows)
    for s in range(late):
        lat = partner_in_kernel(member, s, late)
        for p in range(owners):
            value = fields_ref[lat, p]
            for r in range(rows):
                field_rows[r, p * span : (p + 1) * span, :channels] = value[:, r * channels : (r + 1) * channels]

        def one_row(r, carry):
            row = lat * rows + r
            for piece in range(span // sub):
                cell = owner * span + piece * sub
                b = lax.div(cell, block)
                q = pl.multiple_of(lax.rem(cell, block), sub)
                chosen = []
                for j in range(slots):
                    source = lax.rem(b + shift_ref[row, j] + nblocks, nblocks)
                    chosen.append(field_rows[r, pl.ds(pl.multiple_of(source * block, block), block)])
                picked = jnp.concatenate(chosen, axis=0)
                lhs = weight_refs[s][r, :, pl.ds(q, sub), :].reshape(bases * taps * sub, slots * block)
                product = jnp.dot(lhs, picked, preferred_element_type=jnp.float32)
                for k in range(bases):
                    at = pl.ds(row + low_ref[k, row] + HALO, taps)
                    slab = product[k * taps * sub : (k + 1) * taps * sub].reshape(taps, sub, padded)
                    total[k, at, piece * sub : (piece + 1) * sub] += slab
            return carry

        lax.fori_loop(0, rows, one_row, 0, unroll=True)

    for d, slot in enumerate(mix_slots):
        for k in range(bases):
            mix_all[place_ref[3 + d], k] = added(slot, k)
    fill = jnp.zeros((padded - channels, width), jnp.bfloat16)
    matrix = jnp.concatenate(
        [x for k in range(bases) for x in [mix_all[p, k] for p in range(owners)] + [fill]], axis=0
    )

    def one_out(first, count):
        at = pl.ds(first + HALO, count)
        lhs = [total[k, at].astype(jnp.bfloat16).reshape(count * span, padded) for k in range(bases)]
        product = jnp.dot(jnp.concatenate(lhs, axis=-1), matrix, preferred_element_type=jnp.float32)
        return product.reshape(count, span, width)

    for lat in range(late):
        mixed[lat * rows : (lat + 1) * rows] = one_out(lat * rows, rows)
    for dl in range(late):
        lat = partner_in_kernel(member, dl, late)
        for dq in range(groups):
            start = pl.multiple_of(partner_in_kernel(group, dq, groups) * cells, 8 if cells % 8 == 0 else cells)
            for r in range(rows):
                outs[dl * groups + dq][r] = mixed[lat * rows + r, pl.ds(start, cells)].astype(jnp.bfloat16)
    if halo:
        for side, first in enumerate((-halo, late * rows)):
            outs[-1][side] = one_out(first, halo).astype(jnp.bfloat16)


def conv_mix(low, shift, place, fields, weights, mix, halo, groups, block):
    bases, all_rows = low.shape
    slots = shift.shape[1]
    late, owners, span, _ = fields.shape
    rows = all_rows // late
    depth, width = mix[0][0].shape[1:]
    padded = -(-owners * depth // LANES) * LANES
    taps = weights[0].shape[1] // bases
    sub = math.gcd(span, block)
    shapes = [jax.ShapeDtypeStruct((rows, span // groups, width), jnp.bfloat16)] * (late * groups)
    if halo:
        shapes.append(jax.ShapeDtypeStruct((2, halo, span, width), jnp.bfloat16))
    operands = [fields] + weights + [x for slot in mix for x in slot]
    counts = (len(weights), [len(s) for s in mix])
    return pl.pallas_call(
        functools.partial(conv_mix_kernel, (bases, taps, slots, halo, sub, groups), counts),
        out_shape=shapes,
        in_specs=[SMEM_SPEC] * 3 + [VMEM_SPEC] * len(operands),
        out_specs=[VMEM_SPEC] * len(shapes),
        scratch_shapes=[
            VMEM((rows, owners * span, padded), jnp.bfloat16),
            VMEM((bases, all_rows + 2 * HALO, span, padded), jnp.float32),
            VMEM((owners, bases, depth, width), jnp.bfloat16),
            VMEM((all_rows, span, width), jnp.float32),
        ],
        compiler_params=pltpu.CompilerParams(vmem_limit_bytes=LIMIT),
        name="conv_mix",
    )(low, shift, place, *operands)


def finish_kernel(groups, place_ref, *refs):
    out_ref = refs[-1]
    late = out_ref.shape[0]
    for dl in range(late):
        total = refs[dl * groups][...].astype(jnp.float32)
        for dq in range(1, groups):
            total += refs[dl * groups + dq][...].astype(jnp.float32)
        value = total * (1.0 + lax.erf(total * (0.5**0.5))) * 0.5
        out_ref[partner_in_kernel(place_ref[0], dl, late)] = value.astype(jnp.bfloat16)


def finish(place, parts, groups):
    return pl.pallas_call(
        functools.partial(finish_kernel, groups),
        out_shape=jax.ShapeDtypeStruct((len(parts) // groups,) + parts[0].shape, jnp.bfloat16),
        in_specs=[SMEM_SPEC] + [VMEM_SPEC] * len(parts),
        out_specs=VMEM_SPEC,
        compiler_params=pltpu.CompilerParams(vmem_limit_bytes=LIMIT),
        name="finish",
    )(place, *parts)


def both_kernels(kernel, late):
    bases, rows, taps, slots, block, _ = kernel.shape
    own = kernel.transpose(1, 0, 2, 5, 3, 4).reshape(rows, bases * taps, block, slots * block)
    return [own] + [trade(own, "late", s, late) for s in range(1, late)]


def gather_mix(mix, kernel, late, owners):
    core, own = lax.axis_index("late"), lax.axis_index("lonp")
    if owners == 4 and late == 2:
        def fetch(distances):
            route = [
                (c * owners + p, c * owners + (p ^ d)) for p in range(owners) for c, d in enumerate(distances(p)) if d
            ]
            return lax.ppermute(mix, ("late", "lonp"), route)

        first = fetch(lambda p: (1, 2))
        third = fetch(lambda p: (3, 0) if p in (0, 3) else (0, 3))
        kernel, first, third = lax.optimization_barrier((kernel, first, third))
        other = trade(first, "late", 1, late)
        copied = trade(third, "late", 1, late)
        return [[mix], [first], [other], [third, copied]], [own, own ^ (1 + core), own ^ (2 - core), own ^ 3], kernel
    slots = [[mix]] + [[trade(mix, "lonp", d, owners)] for d in range(1, owners)]
    return slots, [partner(own, d, owners) for d in range(owners)], kernel


def per_device(sizes, fields, kernel, band_low, block_shift, mix_weight):
    halves, late, owners, groups = sizes
    members, rows, channels, cells = fields.shape
    bases, _, taps, slots, block, _ = kernel.shape
    all_rows = late * rows
    halo = HALO if halves > 1 else 0

    packed = pack(fields.transpose(0, 1, 3, 2), groups, owners)
    packed = packed.reshape((-1,) + packed.shape[3:])
    spread = lax.all_to_all(packed, ("late", "lonp", "lonq"), split_axis=0, concat_axis=0, tiled=True)
    spread = spread.reshape(late, owners, groups * cells, -1)
    mix, origins, kernel = gather_mix(mix_weight, kernel, late, owners)
    weights = both_kernels(kernel, late)

    start = lax.axis_index("lath") * all_rows
    low = lax.dynamic_slice_in_dim(band_low, start, all_rows, 1)
    shift = lax.dynamic_slice_in_dim(block_shift, start, all_rows, 0)
    place = [lax.axis_index("late"), lax.axis_index("lonp"), lax.axis_index("lonq")] + origins
    place = jnp.stack(place).astype(jnp.int32)
    partial = conv_mix(low, shift, place, spread, weights, mix, halo, groups, block)
    if halo:
        *partial, beyond = partial
        below = lax.ppermute(beyond[1], "lath", [(i, i + 1) for i in range(halves - 1)])
        above = lax.ppermute(beyond[0], "lath", [(i + 1, i) for i in range(halves - 1)])
        filler = jnp.zeros((all_rows - 2 * halo,) + below.shape[1:], below.dtype)
        extra = jnp.concatenate([below, filler, above], axis=0).reshape(late, rows, groups, cells, -1)
        for dl in range(late):
            lat = partner(lax.axis_index("late"), dl, late)
            for dq in range(groups):
                group = partner(lax.axis_index("lonq"), dq, groups)
                partial[dl * groups + dq] += extra[lat, :, group]
    parts = [
        lax.ppermute(
            partial[dl * groups + dq],
            ("late", "lonq"),
            [
                (l * groups + q, partner(l, dl, late) * groups + partner(q, dq, groups))
                for l in range(late)
                for q in range(groups)
            ],
        )
        if dl or dq
        else partial[0]
        for dl in range(late)
        for dq in range(groups)
    ]
    return finish(place, parts, groups)


def solution(mesh):
    lat, lon = mesh.shape["lat"], mesh.shape["lon"]
    groups = max(g for g in range(1, lon + 1) if lon % g == 0 and g * g <= lon)

    def whole(fields, kernel, band_low, block_shift, mix_weight):
        late = fields.shape[0]
        sizes = (lat // late, late, lon // groups, groups)
        split = Mesh(mesh.devices.reshape(sizes), ("lath", "late", "lonp", "lonq"))
        rows, cells = ("lath", "late"), ("lonp", "lonq")
        return jax.shard_map(
            functools.partial(per_device, sizes),
            mesh=split,
            in_specs=(
                P(None, rows, None, cells),
                P(None, rows, None, None, None, None),
                P(),
                P(),
                P(None, cells, None),
            ),
            out_specs=P(None, rows, cells, None),
            check_vma=False,
        )(fields, kernel, band_low, block_shift, mix_weight)

    return whole
```

```python
import functools
import math

import jax
import jax.numpy as jnp
from jax import lax
from jax.experimental import pallas as pl
from jax.experimental.pallas import tpu as pltpu
from jax.sharding import Mesh
from jax.sharding import PartitionSpec as P

HALO = 2
LANES = 128
VMEM = pltpu.VMEM
LIMIT = 24 * 1024 * 1024
SMEM_SPEC = pl.BlockSpec(memory_space=pltpu.SMEM)
VMEM_SPEC = pl.BlockSpec(memory_space=VMEM)


def partner(index, distance, size):
    if size & (size - 1) == 0:
        return index ^ distance
    return (distance - index) % size


def partner_in_kernel(index, distance, size):
    if size & (size - 1) == 0:
        return lax.bitwise_xor(index, distance)
    return lax.rem(distance - index + size, size)


def trade(x, axis, distance, size):
    return lax.ppermute(x, axis, [(i, partner(i, distance, size)) for i in range(size)])


def pack_kernel(parts, x_ref, out_ref):
    members, rows, cells, channels = x_ref.shape
    na, nb, nc, nd = parts
    width = channels // (na * nb * nc * nd)
    for e in range(members):
        for b in range(nb):
            for d in range(nd):
                firsts = [(((a * nb + b) * nc + c) * nd + d) * width for a in range(na) for c in range(nc)]
                taken = [x_ref[e, i, :, at : at + width] for i in range(rows) for at in firsts]
                block = jnp.concatenate(taken, axis=-1)
                for a in range(na):
                    out_ref[e, a, b, d] = block


def pack(x, parts):
    members, rows, cells, channels = x.shape
    na, nb, _, nd = parts
    return pl.pallas_call(
        functools.partial(pack_kernel, parts),
        out_shape=jax.ShapeDtypeStruct((members, na, nb, nd, cells, rows * channels // (nb * nd)), x.dtype),
        in_specs=[VMEM_SPEC],
        out_specs=VMEM_SPEC,
        compiler_params=pltpu.CompilerParams(vmem_limit_bytes=LIMIT),
        name="pack",
    )(x)


def added(refs, *at):
    value = refs[0][at]
    for ref in refs[1:]:
        value = value + ref[at]
    return value


def conv_mix_kernel(geometry, counts, low_ref, shift_ref, place_ref, *refs):
    bases, taps, slots, halo, sub, groups = geometry
    refs = list(refs)
    field_refs = [refs.pop(0) for _ in range(counts[0])]
    weight_refs = [refs.pop(0) for _ in range(counts[1])]
    mix_slots = [[refs.pop(0) for _ in range(n)] for n in counts[2]]
    field_rows, total, mix_all, mixed = refs[-4:]
    outs = refs[:-4]
    late, na, nb, stripe, _ = field_refs[0].shape
    nc = len(field_refs)
    span = nb * stripe
    owners = len(mix_slots)
    depth, width = mix_slots[0][0].shape[1:]
    channels = owners * depth
    padded = total.shape[-1]
    rows, _, block, _ = weight_refs[0].shape
    nblocks = field_rows.shape[1] // block
    cells = span // groups
    member, place_a, place_c, group = [place_ref[i] for i in range(4)]

    total[...] = jnp.zeros_like(total)
    field_rows[...] = jnp.zeros_like(field_rows)
    for s in range(late):
        lat = partner_in_kernel(member, s, late)
        for a in range(na):
            for b in range(nb):
                for dc, ref in enumerate(field_refs):
                    stripe_at = (a * nb + b) * nc + partner_in_kernel(place_c, dc, nc)
                    at = pl.ds(pl.multiple_of(stripe_at * stripe, sub), stripe)
                    value = ref[lat, a, b]
                    for r in range(rows):
                        field_rows[r, at, :channels] = value[:, r * channels : (r + 1) * channels]

        def one_row(r, carry):
            row = lat * rows + r
            for piece in range(span // sub):
                b_at, in_stripe = divmod(piece * sub, stripe)
                cell = ((place_a * nb + b_at) * nc + place_c) * stripe + in_stripe
                b = lax.div(cell, block)
                q = pl.multiple_of(lax.rem(cell, block), sub)
                chosen = []
                for j in range(slots):
                    source = lax.rem(b + shift_ref[row, j] + nblocks, nblocks)
                    chosen.append(field_rows[r, pl.ds(pl.multiple_of(source * block, block), block)])
                picked = jnp.concatenate(chosen, axis=0)
                lhs = weight_refs[s][r, :, pl.ds(q, sub), :].reshape(bases * taps * sub, slots * block)
                product = jnp.dot(lhs, picked, preferred_element_type=jnp.float32)
                for k in range(bases):
                    at = pl.ds(row + low_ref[k, row] + HALO, taps)
                    slab = product[k * taps * sub : (k + 1) * taps * sub].reshape(taps, sub, padded)
                    total[k, at, piece * sub : (piece + 1) * sub] += slab
            return carry

        lax.fori_loop(0, rows, one_row, 0, unroll=2)

    for d, slot in enumerate(mix_slots):
        for k in range(bases):
            mix_all[place_ref[4 + d], k] = added(slot, k)
    fill = jnp.zeros((padded - channels, width), jnp.bfloat16)
    matrix = jnp.concatenate(
        [x for k in range(bases) for x in [mix_all[p, k] for p in range(owners)] + [fill]], axis=0
    )

    def one_out(first, count):
        at = pl.ds(first + HALO, count)
        lhs = [total[k, at].astype(jnp.bfloat16).reshape(count * span, padded) for k in range(bases)]
        product = jnp.dot(jnp.concatenate(lhs, axis=-1), matrix, preferred_element_type=jnp.float32)
        return product.reshape(count, span, width)

    for lat in range(late):
        mixed[lat * rows : (lat + 1) * rows] = one_out(lat * rows, rows)
    for dl in range(late):
        lat = partner_in_kernel(member, dl, late)
        for dq in range(groups):
            start = pl.multiple_of(partner_in_kernel(group, dq, groups) * cells, 8 if cells % 8 == 0 else cells)
            for r in range(rows):
                outs[dl * groups + dq][r] = mixed[lat * rows + r, pl.ds(start, cells)].astype(jnp.bfloat16)
    if halo:
        for side, first in enumerate((-halo, late * rows)):
            outs[-1][side] = one_out(first, halo).astype(jnp.bfloat16)


def conv_mix(low, shift, place, fields, weights, mix, halo, groups, block):
    bases, all_rows = low.shape
    slots = shift.shape[1]
    late, na, nb, stripe, _ = fields[0].shape
    span = nb * stripe
    longitudes = na * len(fields) * span
    owners = len(mix)
    rows = all_rows // late
    depth, width = mix[0][0].shape[1:]
    padded = -(-owners * depth // LANES) * LANES
    taps = weights[0].shape[1] // bases
    sub = math.gcd(stripe, block)
    shapes = [jax.ShapeDtypeStruct((rows, span // groups, width), jnp.bfloat16)] * (late * groups)
    if halo:
        shapes.append(jax.ShapeDtypeStruct((2, halo, span, width), jnp.bfloat16))
    operands = fields + weights + [x for slot in mix for x in slot]
    counts = (len(fields), len(weights), [len(s) for s in mix])
    return pl.pallas_call(
        functools.partial(conv_mix_kernel, (bases, taps, slots, halo, sub, groups), counts),
        out_shape=shapes,
        in_specs=[SMEM_SPEC] * 3 + [VMEM_SPEC] * len(operands),
        out_specs=[VMEM_SPEC] * len(shapes),
        scratch_shapes=[
            VMEM((rows, longitudes, padded), jnp.bfloat16),
            VMEM((bases, all_rows + 2 * HALO, span, padded), jnp.float32),
            VMEM((owners, bases, depth, width), jnp.bfloat16),
            VMEM((all_rows, span, width), jnp.float32),
        ],
        compiler_params=pltpu.CompilerParams(vmem_limit_bytes=LIMIT),
        name="conv_mix",
    )(low, shift, place, *operands)


def finish_kernel(groups, place_ref, *refs):
    out_ref = refs[-1]
    late = out_ref.shape[0]
    for dl in range(late):
        total = refs[dl * groups][...].astype(jnp.float32)
        for dq in range(1, groups):
            total += refs[dl * groups + dq][...].astype(jnp.float32)
        value = total * (1.0 + lax.erf(total * (0.5**0.5))) * 0.5
        out_ref[partner_in_kernel(place_ref[0], dl, late)] = value.astype(jnp.bfloat16)


def finish(place, parts, groups):
    return pl.pallas_call(
        functools.partial(finish_kernel, groups),
        out_shape=jax.ShapeDtypeStruct((len(parts) // groups,) + parts[0].shape, jnp.bfloat16),
        in_specs=[SMEM_SPEC] + [VMEM_SPEC] * len(parts),
        out_specs=VMEM_SPEC,
        compiler_params=pltpu.CompilerParams(vmem_limit_bytes=LIMIT),
        name="finish",
    )(place, *parts)


def both_kernels(kernel, late):
    bases, rows, taps, slots, block, _ = kernel.shape
    own = kernel.transpose(1, 0, 2, 5, 3, 4).reshape(rows, bases * taps, block, slots * block)
    return [own] + [trade(own, "late", s, late) for s in range(1, late)]


def gather_mix(mix, spread, late, na, nc):
    core, own = lax.axis_index("late"), lax.axis_index("a") * nc + lax.axis_index("c")
    owners = na * nc
    if na == nc == late == 2:
        route = [(p, p ^ 2) for p in range(4)] + [(4 + p, 4 + (p ^ 1)) for p in range(4)]
        first = lax.ppermute(mix, ("late", "a", "c"), route)
        third = lax.ppermute(mix, ("late", "a", "c"), [(4 + p, 4 + (p ^ 3)) for p in range(4)])
        first_late, third_late, _ = lax.optimization_barrier((first, third, spread))
        other = trade(first_late, "late", 1, late)
        copied = lax.ppermute(third_late, "late", [(1, 0)])
        return [[mix], [first], [other], [third, copied]], [own, own ^ (2 - core), own ^ (1 + core), own ^ 3]
    slots = [[mix]] + [[trade(mix, ("a", "c"), d, owners)] for d in range(1, owners)]
    return slots, [partner(own, d, owners) for d in range(owners)]


def per_device(sizes, fields, kernel, band_low, block_shift, mix_weight):
    halves, late, na, nb, nc, nd = sizes
    groups = nb * nd
    members, rows, channels, cells = fields.shape
    block = kernel.shape[-1]
    all_rows = late * rows
    halo = HALO if halves > 1 else 0

    packed = pack(fields.transpose(0, 1, 3, 2), sizes[2:])
    packed = packed.reshape((-1,) + packed.shape[4:])
    spread = lax.all_to_all(packed, ("late", "a", "b", "d"), split_axis=0, concat_axis=0, tiled=True)
    weights = both_kernels(kernel, late)
    arrived = spread
    spread = spread.reshape(late, na, nb, nd * cells, -1)
    spread = [spread] + [trade(spread, "c", s, nc) for s in range(1, nc)]
    mix, origins = gather_mix(mix_weight, arrived, late, na, nc)

    start = lax.axis_index("lath") * all_rows
    low = lax.dynamic_slice_in_dim(band_low, start, all_rows, 1)
    shift = lax.dynamic_slice_in_dim(block_shift, start, all_rows, 0)
    group = lax.axis_index("b") * nd + lax.axis_index("d")
    place = [lax.axis_index("late"), lax.axis_index("a"), lax.axis_index("c"), group] + origins
    place = jnp.stack(place).astype(jnp.int32)
    partial = conv_mix(low, shift, place, spread, weights, mix, halo, groups, block)
    if halo:
        *partial, beyond = partial
        below = lax.ppermute(beyond[1], "lath", [(i, i + 1) for i in range(halves - 1)])
        above = lax.ppermute(beyond[0], "lath", [(i + 1, i) for i in range(halves - 1)])
        filler = jnp.zeros((all_rows - 2 * halo,) + below.shape[1:], below.dtype)
        extra = jnp.concatenate([below, filler, above], axis=0).reshape(late, rows, groups, cells, -1)
        for dl in range(late):
            lat = partner(lax.axis_index("late"), dl, late)
            for dq in range(groups):
                partial[dl * groups + dq] += extra[lat, :, partner(group, dq, groups)]
    parts = [
        lax.ppermute(
            partial[dl * groups + dq],
            ("late", "b", "d"),
            [
                (l * groups + q, partner(l, dl, late) * groups + partner(q, dq, groups))
                for l in range(late)
                for q in range(groups)
            ],
        )
        if dl or dq
        else partial[0]
        for dl in range(late)
        for dq in range(groups)
    ]
    return finish(place, parts, groups)


def solution(mesh):
    lat, lon = mesh.shape["lat"], mesh.shape["lon"]
    halves = [2 if lon % 8 == 0 else 1] * 3

    def whole(fields, kernel, band_low, block_shift, mix_weight):
        late = fields.shape[0]
        sizes = (lat // late, late, lon // math.prod(halves), *halves)
        split = Mesh(mesh.devices.reshape(sizes), ("lath", "late", "a", "b", "c", "d"))
        rows, cells = ("lath", "late"), ("a", "b", "c", "d")
        return jax.shard_map(
            functools.partial(per_device, sizes),
            mesh=split,
            in_specs=(
                P(None, rows, None, cells),
                P(None, rows, None, None, None, None),
                P(),
                P(),
                P(None, cells, None),
            ),
            out_specs=P(None, rows, cells, None),
            check_vma=False,
        )(fields, kernel, band_low, block_shift, mix_weight)

    return whole
```

```python
import functools
import math

import jax
import jax.numpy as jnp
from jax import lax
from jax.experimental import pallas as pl
from jax.experimental.pallas import tpu as pltpu
from jax.sharding import Mesh
from jax.sharding import PartitionSpec as P

HALO = 2
LANES = 128
VMEM = pltpu.VMEM
LIMIT = 24 * 1024 * 1024
SMEM_SPEC = pl.BlockSpec(memory_space=pltpu.SMEM)
VMEM_SPEC = pl.BlockSpec(memory_space=VMEM)


def partner(index, distance, size):
    if size & (size - 1) == 0:
        return index ^ distance
    return (distance - index) % size


def partner_in_kernel(index, distance, size):
    if size & (size - 1) == 0:
        return lax.bitwise_xor(index, distance)
    return lax.rem(distance - index + size, size)


def trade(x, axis, distance, size):
    return lax.ppermute(x, axis, [(i, partner(i, distance, size)) for i in range(size)])


def pack_kernel(groups, owners, x_ref, out_ref):
    members, rows, cells, channels = x_ref.shape
    width = channels // (groups * owners)
    for e in range(members):
        for q in range(groups):
            parts = [
                x_ref[e, i, :, (p * groups + q) * width : (p * groups + q + 1) * width]
                for i in range(rows)
                for p in range(owners)
            ]
            block = jnp.concatenate(parts, axis=-1)
            for p in range(owners):
                out_ref[e, p, q] = block


def pack(x, groups, owners):
    members, rows, cells, channels = x.shape
    return pl.pallas_call(
        functools.partial(pack_kernel, groups, owners),
        out_shape=jax.ShapeDtypeStruct((members, owners, groups, cells, rows * channels // groups), x.dtype),
        in_specs=[VMEM_SPEC],
        out_specs=VMEM_SPEC,
        compiler_params=pltpu.CompilerParams(vmem_limit_bytes=LIMIT),
        name="pack",
    )(x)


def added(refs, *at):
    value = refs[0][at]
    for ref in refs[1:]:
        value = value + ref[at]
    return value


def conv_mix_kernel(geometry, counts, low_ref, shift_ref, place_ref, *refs):
    bases, taps, slots, halo, sub, groups = geometry
    refs = list(refs)
    fields_ref = refs.pop(0)
    weight_refs = [refs.pop(0) for _ in range(counts[0])]
    mix_slots = [[refs.pop(0) for _ in range(n)] for n in counts[1]]
    field_rows, total, mix_all, mixed = refs[-4:]
    outs = refs[:-4]
    late, owners, span, _ = fields_ref.shape
    depth, width = mix_slots[0][0].shape[1:]
    channels = owners * depth
    padded = total.shape[-1]
    rows, _, block, _ = weight_refs[0].shape
    nblocks = owners * span // block
    cells = span // groups
    member, owner, group = place_ref[0], place_ref[1], place_ref[2]

    total[...] = jnp.zeros_like(total)
    field_rows[...] = jnp.zeros_like(field_rows)
    for s in range(late):
        lat = partner_in_kernel(member, s, late)
        for p in range(owners):
            value = fields_ref[lat, p]
            for r in range(rows):
                field_rows[r, p * span : (p + 1) * span, :channels] = value[:, r * channels : (r + 1) * channels]

        def one_row(r, carry):
            row = lat * rows + r
            for piece in range(span // sub):
                cell = owner * span + piece * sub
                b = lax.div(cell, block)
                q = pl.multiple_of(lax.rem(cell, block), sub)
                chosen = []
                for j in range(slots):
                    source = lax.rem(b + shift_ref[row, j] + nblocks, nblocks)
                    chosen.append(field_rows[r, pl.ds(pl.multiple_of(source * block, block), block)])
                picked = jnp.concatenate(chosen, axis=0)
                lhs = weight_refs[s][r, :, pl.ds(q, sub), :].reshape(bases * taps * sub, slots * block)
                product = jnp.dot(lhs, picked, preferred_element_type=jnp.float32)
                for k in range(bases):
                    at = pl.ds(row + low_ref[k, row] + HALO, taps)
                    slab = product[k * taps * sub : (k + 1) * taps * sub].reshape(taps, sub, padded)
                    total[k, at, piece * sub : (piece + 1) * sub] += slab
            return carry

        lax.fori_loop(0, rows, one_row, 0, unroll=2)

    for d, slot in enumerate(mix_slots):
        for k in range(bases):
            mix_all[place_ref[3 + d], k] = added(slot, k)
    fill = jnp.zeros((padded - channels, width), jnp.bfloat16)
    matrix = jnp.concatenate(
        [x for k in range(bases) for x in [mix_all[p, k] for p in range(owners)] + [fill]], axis=0
    )

    def one_out(first, count):
        at = pl.ds(first + HALO, count)
        lhs = [total[k, at].astype(jnp.bfloat16).reshape(count * span, padded) for k in range(bases)]
        product = jnp.dot(jnp.concatenate(lhs, axis=-1), matrix, preferred_element_type=jnp.float32)
        return product.reshape(count, span, width)

    for lat in range(late):
        mixed[lat * rows : (lat + 1) * rows] = one_out(lat * rows, rows)
    for dl in range(late):
        lat = partner_in_kernel(member, dl, late)
        for dq in range(groups):
            start = pl.multiple_of(partner_in_kernel(group, dq, groups) * cells, 8 if cells % 8 == 0 else cells)
            for r in range(rows):
                outs[dl * groups + dq][r] = mixed[lat * rows + r, pl.ds(start, cells)].astype(jnp.bfloat16)
    if halo:
        for side, first in enumerate((-halo, late * rows)):
            outs[-1][side] = one_out(first, halo).astype(jnp.bfloat16)


def conv_mix(low, shift, place, fields, weights, mix, halo, groups, block):
    bases, all_rows = low.shape
    slots = shift.shape[1]
    late, owners, span, _ = fields.shape
    rows = all_rows // late
    depth, width = mix[0][0].shape[1:]
    padded = -(-owners * depth // LANES) * LANES
    taps = weights[0].shape[1] // bases
    sub = math.gcd(span, block)
    shapes = [jax.ShapeDtypeStruct((rows, span // groups, width), jnp.bfloat16)] * (late * groups)
    if halo:
        shapes.append(jax.ShapeDtypeStruct((2, halo, span, width), jnp.bfloat16))
    operands = [fields] + weights + [x for slot in mix for x in slot]
    counts = (len(weights), [len(s) for s in mix])
    return pl.pallas_call(
        functools.partial(conv_mix_kernel, (bases, taps, slots, halo, sub, groups), counts),
        out_shape=shapes,
        in_specs=[SMEM_SPEC] * 3 + [VMEM_SPEC] * len(operands),
        out_specs=[VMEM_SPEC] * len(shapes),
        scratch_shapes=[
            VMEM((rows, owners * span, padded), jnp.bfloat16),
            VMEM((bases, all_rows + 2 * HALO, span, padded), jnp.float32),
            VMEM((owners, bases, depth, width), jnp.bfloat16),
            VMEM((all_rows, span, width), jnp.float32),
        ],
        compiler_params=pltpu.CompilerParams(vmem_limit_bytes=LIMIT),
        name="conv_mix",
    )(low, shift, place, *operands)


def finish_kernel(groups, place_ref, *refs):
    out_ref = refs[-1]
    late = out_ref.shape[0]
    for dl in range(late):
        total = refs[dl * groups][...].astype(jnp.float32)
        for dq in range(1, groups):
            total += refs[dl * groups + dq][...].astype(jnp.float32)
        value = total * (1.0 + lax.erf(total * (0.5**0.5))) * 0.5
        out_ref[partner_in_kernel(place_ref[0], dl, late)] = value.astype(jnp.bfloat16)


def finish(place, parts, groups):
    return pl.pallas_call(
        functools.partial(finish_kernel, groups),
        out_shape=jax.ShapeDtypeStruct((len(parts) // groups,) + parts[0].shape, jnp.bfloat16),
        in_specs=[SMEM_SPEC] + [VMEM_SPEC] * len(parts),
        out_specs=VMEM_SPEC,
        compiler_params=pltpu.CompilerParams(vmem_limit_bytes=LIMIT),
        name="finish",
    )(place, *parts)


def both_kernels(kernel, late):
    bases, rows, taps, slots, block, _ = kernel.shape
    own = kernel.transpose(1, 0, 2, 5, 3, 4).reshape(rows, bases * taps, block, slots * block)
    return [own] + [trade(own, "late", s, late) for s in range(1, late)]


def gather_mix(mix, packed, late, owners):
    core, own = lax.axis_index("late"), lax.axis_index("lonp")
    if owners == 4 and late == 2:
        route = [(p, p ^ 1) for p in range(4)] + [(4 + p, 4 + (p ^ 2)) for p in range(4)]
        first = lax.ppermute(mix, ("late", "lonp"), route)
        packed, first = lax.optimization_barrier((packed, first))
        third = lax.ppermute(first, ("late", "lonp"), [(4 + p, 4 + (p ^ 1)) for p in range(4)])
        other = trade(first, "late", 1, late)
        copied = lax.ppermute(third, "late", [(1, 0)])
        slots, origins = [[mix], [first], [other], [third, copied]], [own, own ^ (1 + core), own ^ (2 - core), own ^ 3]
        return slots, origins, packed
    slots = [[mix]] + [[trade(mix, "lonp", d, owners)] for d in range(1, owners)]
    return slots, [partner(own, d, owners) for d in range(owners)], packed


def per_device(sizes, fields, kernel, band_low, block_shift, mix_weight):
    halves, late, owners, groups = sizes
    members, rows, channels, cells = fields.shape
    bases, _, taps, slots, block, _ = kernel.shape
    all_rows = late * rows
    halo = HALO if halves > 1 else 0

    packed = pack(fields.transpose(0, 1, 3, 2), groups, owners)
    packed = packed.reshape((-1,) + packed.shape[3:])
    mix, origins, packed = gather_mix(mix_weight, packed, late, owners)
    spread = lax.all_to_all(packed, ("late", "lonp", "lonq"), split_axis=0, concat_axis=0, tiled=True)
    spread = spread.reshape(late, owners, groups * cells, -1)
    weights = both_kernels(kernel, late)

    start = lax.axis_index("lath") * all_rows
    low = lax.dynamic_slice_in_dim(band_low, start, all_rows, 1)
    shift = lax.dynamic_slice_in_dim(block_shift, start, all_rows, 0)
    place = [lax.axis_index("late"), lax.axis_index("lonp"), lax.axis_index("lonq")] + origins
    place = jnp.stack(place).astype(jnp.int32)
    partial = conv_mix(low, shift, place, spread, weights, mix, halo, groups, block)
    if halo:
        *partial, beyond = partial
        below = lax.ppermute(beyond[1], "lath", [(i, i + 1) for i in range(halves - 1)])
        above = lax.ppermute(beyond[0], "lath", [(i + 1, i) for i in range(halves - 1)])
        filler = jnp.zeros((all_rows - 2 * halo,) + below.shape[1:], below.dtype)
        extra = jnp.concatenate([below, filler, above], axis=0).reshape(late, rows, groups, cells, -1)
        for dl in range(late):
            lat = partner(lax.axis_index("late"), dl, late)
            for dq in range(groups):
                group = partner(lax.axis_index("lonq"), dq, groups)
                partial[dl * groups + dq] += extra[lat, :, group]
    parts = [
        lax.ppermute(
            partial[dl * groups + dq],
            ("late", "lonq"),
            [
                (l * groups + q, partner(l, dl, late) * groups + partner(q, dq, groups))
                for l in range(late)
                for q in range(groups)
            ],
        )
        if dl or dq
        else partial[0]
        for dl in range(late)
        for dq in range(groups)
    ]
    return finish(place, parts, groups)


def solution(mesh):
    lat, lon = mesh.shape["lat"], mesh.shape["lon"]
    groups = max(g for g in range(1, lon + 1) if lon % g == 0 and g * g <= lon)

    def whole(fields, kernel, band_low, block_shift, mix_weight):
        late = fields.shape[0]
        sizes = (lat // late, late, lon // groups, groups)
        split = Mesh(mesh.devices.reshape(sizes), ("lath", "late", "lonp", "lonq"))
        rows, cells = ("lath", "late"), ("lonp", "lonq")
        return jax.shard_map(
            functools.partial(per_device, sizes),
            mesh=split,
            in_specs=(
                P(None, rows, None, cells),
                P(None, rows, None, None, None, None),
                P(),
                P(),
                P(None, cells, None),
            ),
            out_specs=P(None, rows, cells, None),
            check_vma=False,
        )(fields, kernel, band_low, block_shift, mix_weight)

    return whole
```

```python
import functools
import math

import jax
import jax.numpy as jnp
from jax import lax
from jax.experimental import pallas as pl
from jax.experimental.pallas import tpu as pltpu
from jax.sharding import Mesh
from jax.sharding import PartitionSpec as P

HALO = 2
LANES = 128
VMEM = pltpu.VMEM
LIMIT = 16 * 1024 * 1024
SMEM_SPEC = pl.BlockSpec(memory_space=pltpu.SMEM)
VMEM_SPEC = pl.BlockSpec(memory_space=VMEM)


def partner(index, distance, size):
    if size & (size - 1) == 0:
        return index ^ distance
    return (distance - index) % size


def partner_in_kernel(index, distance, size):
    if size & (size - 1) == 0:
        return lax.bitwise_xor(index, distance)
    return lax.rem(distance - index + size, size)


def trade(x, axis, distance, size):
    return lax.ppermute(x, axis, [(i, partner(i, distance, size)) for i in range(size)])


def pack_kernel(groups, owners, x_ref, out_ref):
    members, rows, cells, channels = x_ref.shape
    width = channels // (groups * owners)
    for e in range(members):
        for q in range(groups):
            parts = [
                x_ref[e, i, :, (p * groups + q) * width : (p * groups + q + 1) * width]
                for i in range(rows)
                for p in range(owners)
            ]
            out_ref[e, q] = jnp.concatenate(parts, axis=-1)


def pack(x, groups, owners):
    members, rows, cells, channels = x.shape
    return pl.pallas_call(
        functools.partial(pack_kernel, groups, owners),
        out_shape=jax.ShapeDtypeStruct((members, groups, cells, rows * channels // groups), x.dtype),
        in_specs=[VMEM_SPEC],
        out_specs=VMEM_SPEC,
        compiler_params=pltpu.CompilerParams(vmem_limit_bytes=LIMIT),
        name="pack",
    )(x)


def added(refs, *at):
    value = refs[0][at]
    for ref in refs[1:]:
        value = value + ref[at]
    return value


def conv_mix_kernel(geometry, counts, low_ref, shift_ref, place_ref, *refs):
    bases, taps, slots, halo, sub, groups = geometry
    refs = list(refs)
    field_refs = [refs.pop(0) for _ in range(counts[0])]
    weight_refs = [refs.pop(0) for _ in range(counts[1])]
    mix_slots = [[refs.pop(0) for _ in range(n)] for n in counts[2]]
    field_rows, total, mix_all, mixed = refs[-4:]
    outs = refs[:-4]
    late, span, _ = field_refs[0].shape
    owners = len(field_refs)
    depth, width = mix_slots[0][0].shape[1:]
    channels = owners * depth
    padded = total.shape[-1]
    rows, _, block, _ = weight_refs[0].shape
    nblocks = owners * span // block
    cells = span // groups
    member, owner, group = place_ref[0], place_ref[1], place_ref[2]

    total[...] = jnp.zeros_like(total)
    field_rows[...] = jnp.zeros_like(field_rows)
    for s in range(late):
        lat = partner_in_kernel(member, s, late)
        for d, ref in enumerate(field_refs):
            at = pl.ds(pl.multiple_of(partner_in_kernel(owner, d, owners) * span, sub), span)
            value = ref[lat]
            for r in range(rows):
                field_rows[r, at, :channels] = value[:, r * channels : (r + 1) * channels]

        def one_row(r, carry):
            row = lat * rows + r
            for piece in range(span // sub):
                cell = owner * span + piece * sub
                b = lax.div(cell, block)
                q = pl.multiple_of(lax.rem(cell, block), sub)
                chosen = []
                for j in range(slots):
                    source = lax.rem(b + shift_ref[row, j] + nblocks, nblocks)
                    chosen.append(field_rows[r, pl.ds(pl.multiple_of(source * block, block), block)])
                picked = jnp.concatenate(chosen, axis=0)
                lhs = weight_refs[s][r, :, pl.ds(q, sub), :].reshape(bases * taps * sub, slots * block)
                product = jnp.dot(lhs, picked, preferred_element_type=jnp.float32)
                for k in range(bases):
                    at = pl.ds(row + low_ref[k, row] + HALO, taps)
                    slab = product[k * taps * sub : (k + 1) * taps * sub].reshape(taps, sub, padded)
                    total[k, at, piece * sub : (piece + 1) * sub] += slab
            return carry

        lax.fori_loop(0, rows, one_row, 0, unroll=2)

    for d, slot in enumerate(mix_slots):
        for k in range(bases):
            mix_all[place_ref[3 + d], k] = added(slot, k)
    fill = jnp.zeros((padded - channels, width), jnp.bfloat16)
    matrix = jnp.concatenate(
        [x for k in range(bases) for x in [mix_all[p, k] for p in range(owners)] + [fill]], axis=0
    )

    def one_out(first, count):
        at = pl.ds(first + HALO, count)
        lhs = [total[k, at].astype(jnp.bfloat16).reshape(count * span, padded) for k in range(bases)]
        product = jnp.dot(jnp.concatenate(lhs, axis=-1), matrix, preferred_element_type=jnp.float32)
        return product.reshape(count, span, width)

    for lat in range(late):
        mixed[lat * rows : (lat + 1) * rows] = one_out(lat * rows, rows)
    for dl in range(late):
        lat = partner_in_kernel(member, dl, late)
        for dq in range(groups):
            start = pl.multiple_of(partner_in_kernel(group, dq, groups) * cells, 8 if cells % 8 == 0 else cells)
            for r in range(rows):
                outs[dl * groups + dq][r] = mixed[lat * rows + r, pl.ds(start, cells)].astype(jnp.bfloat16)
    if halo:
        for side, first in enumerate((-halo, late * rows)):
            outs[-1][side] = one_out(first, halo).astype(jnp.bfloat16)


def conv_mix(low, shift, place, fields, weights, mix, halo, groups, block):
    bases, all_rows = low.shape
    slots = shift.shape[1]
    late, span, _ = fields[0].shape
    owners = len(fields)
    rows = all_rows // late
    depth, width = mix[0][0].shape[1:]
    padded = -(-owners * depth // LANES) * LANES
    taps = weights[0].shape[1] // bases
    sub = math.gcd(span, block)
    shapes = [jax.ShapeDtypeStruct((rows, span // groups, width), jnp.bfloat16)] * (late * groups)
    if halo:
        shapes.append(jax.ShapeDtypeStruct((2, halo, span, width), jnp.bfloat16))
    operands = fields + weights + [x for slot in mix for x in slot]
    counts = (len(fields), len(weights), [len(s) for s in mix])
    return pl.pallas_call(
        functools.partial(conv_mix_kernel, (bases, taps, slots, halo, sub, groups), counts),
        out_shape=shapes,
        in_specs=[SMEM_SPEC] * 3 + [VMEM_SPEC] * len(operands),
        out_specs=[VMEM_SPEC] * len(shapes),
        scratch_shapes=[
            VMEM((rows, owners * span, padded), jnp.bfloat16),
            VMEM((bases, all_rows + 2 * HALO, span, padded), jnp.float32),
            VMEM((owners, bases, depth, width), jnp.bfloat16),
            VMEM((all_rows, span, width), jnp.float32),
        ],
        compiler_params=pltpu.CompilerParams(vmem_limit_bytes=LIMIT),
        name="conv_mix",
    )(low, shift, place, *operands)


def finish_kernel(groups, place_ref, *refs):
    out_ref = refs[-1]
    late = out_ref.shape[0]
    for dl in range(late):
        total = refs[dl * groups][...].astype(jnp.float32)
        for dq in range(1, groups):
            total += refs[dl * groups + dq][...].astype(jnp.float32)
        value = total * (1.0 + lax.erf(total * (0.5**0.5))) * 0.5
        out_ref[partner_in_kernel(place_ref[0], dl, late)] = value.astype(jnp.bfloat16)


def finish(place, parts, groups):
    return pl.pallas_call(
        functools.partial(finish_kernel, groups),
        out_shape=jax.ShapeDtypeStruct((len(parts) // groups,) + parts[0].shape, jnp.bfloat16),
        in_specs=[SMEM_SPEC] + [VMEM_SPEC] * len(parts),
        out_specs=VMEM_SPEC,
        compiler_params=pltpu.CompilerParams(vmem_limit_bytes=LIMIT),
        name="finish",
    )(place, *parts)


def turn_kernel(x_ref, out_ref):
    bases, rows, taps, slots, block, _ = x_ref.shape
    unit = (lax.broadcasted_iota(jnp.int32, (block, block), 0) == lax.broadcasted_iota(jnp.int32, (block, block), 1))
    unit = unit.astype(jnp.float32).astype(x_ref.dtype)

    def one_row(r, carry):
        for k in range(bases):
            for t in range(taps):
                cells = x_ref[k, r, t].reshape(slots * block, block)
                turned = lax.dot_general(unit, cells, (((1,), (1,)), ((), ())), preferred_element_type=jnp.float32)
                out_ref[r, k * taps + t] = turned.astype(out_ref.dtype)
        return carry

    lax.fori_loop(0, rows, one_row, 0)


def turn(x):
    bases, rows, taps, slots, block, _ = x.shape
    return pl.pallas_call(
        turn_kernel,
        out_shape=jax.ShapeDtypeStruct((rows, bases * taps, block, slots * block), x.dtype),
        in_specs=[VMEM_SPEC],
        out_specs=VMEM_SPEC,
        compiler_params=pltpu.CompilerParams(vmem_limit_bytes=LIMIT),
        name="turn",
    )(x)


def gather_mix(mix, spread, late, owners):
    core, own = lax.axis_index("late"), lax.axis_index("lonp")
    if owners == 4 and late == 2:
        route = [(p, p ^ 1) for p in range(4)] + [(4 + p, 4 + (p ^ 2)) for p in range(4)]
        first = lax.ppermute(mix, ("late", "lonp"), route)
        spread, first = lax.optimization_barrier((spread, first))
        third = lax.ppermute(first, ("late", "lonp"), [(4 + p, 4 + (p ^ 1)) for p in range(4)])
        other = trade(first, "late", 1, late)
        copied = lax.ppermute(third, "late", [(1, 0)])
        slots, origins = [[mix], [first], [other], [third, copied]], [own, own ^ (1 + core), own ^ (2 - core), own ^ 3]
        return slots, origins, spread
    slots = [[mix]] + [[trade(mix, "lonp", d, owners)] for d in range(1, owners)]
    return slots, [partner(own, d, owners) for d in range(owners)], spread


def per_device(sizes, fields, kernel, band_low, block_shift, mix_weight):
    halves, late, owners, groups = sizes
    members, rows, channels, cells = fields.shape
    block = kernel.shape[-1]
    all_rows = late * rows
    halo = HALO if halves > 1 else 0

    kernels = [kernel] + [trade(kernel, "late", s, late) for s in range(1, late)]
    packed = pack(fields.transpose(0, 1, 3, 2), groups, owners)
    packed = packed.reshape((late * groups,) + packed.shape[2:])
    spread = lax.all_to_all(packed, ("late", "lonq"), split_axis=0, concat_axis=0, tiled=True)
    mix, origins, spread = gather_mix(mix_weight, spread, late, owners)
    *kernels, spread = lax.optimization_barrier((*kernels, spread))
    weights = [turn(x) for x in kernels]
    spread = spread.reshape(late, groups * cells, -1)
    spread = [spread] + [trade(spread, "lonp", d, owners) for d in range(1, owners)]

    start = lax.axis_index("lath") * all_rows
    low = lax.dynamic_slice_in_dim(band_low, start, all_rows, 1)
    shift = lax.dynamic_slice_in_dim(block_shift, start, all_rows, 0)
    place = [lax.axis_index("late"), lax.axis_index("lonp"), lax.axis_index("lonq")] + origins
    place = jnp.stack(place).astype(jnp.int32)
    partial = conv_mix(low, shift, place, spread, weights, mix, halo, groups, block)
    if halo:
        *partial, beyond = partial
        below = lax.ppermute(beyond[1], "lath", [(i, i + 1) for i in range(halves - 1)])
        above = lax.ppermute(beyond[0], "lath", [(i + 1, i) for i in range(halves - 1)])
        filler = jnp.zeros((all_rows - 2 * halo,) + below.shape[1:], below.dtype)
        extra = jnp.concatenate([below, filler, above], axis=0).reshape(late, rows, groups, cells, -1)
        for dl in range(late):
            lat = partner(lax.axis_index("late"), dl, late)
            for dq in range(groups):
                group = partner(lax.axis_index("lonq"), dq, groups)
                partial[dl * groups + dq] += extra[lat, :, group]
    parts = [
        lax.ppermute(
            partial[dl * groups + dq],
            ("late", "lonq"),
            [
                (l * groups + q, partner(l, dl, late) * groups + partner(q, dq, groups))
                for l in range(late)
                for q in range(groups)
            ],
        )
        if dl or dq
        else partial[0]
        for dl in range(late)
        for dq in range(groups)
    ]
    return finish(place, parts, groups)


def solution(mesh):
    lat, lon = mesh.shape["lat"], mesh.shape["lon"]
    groups = max(g for g in range(1, lon + 1) if lon % g == 0 and g * g <= lon)

    def whole(fields, kernel, band_low, block_shift, mix_weight):
        late = fields.shape[0]
        sizes = (lat // late, late, lon // groups, groups)
        split = Mesh(mesh.devices.reshape(sizes), ("lath", "late", "lonp", "lonq"))
        rows, cells = ("lath", "late"), ("lonp", "lonq")
        return jax.shard_map(
            functools.partial(per_device, sizes),
            mesh=split,
            in_specs=(
                P(None, rows, None, cells),
                P(None, rows, None, None, None, None),
                P(),
                P(),
                P(None, cells, None),
            ),
            out_specs=P(None, rows, cells, None),
            check_vma=False,
        )(fields, kernel, band_low, block_shift, mix_weight)

    return whole
```

```python
import functools
import math

import jax
import jax.numpy as jnp
from jax import lax
from jax.experimental import pallas as pl
from jax.experimental.pallas import tpu as pltpu
from jax.sharding import Mesh
from jax.sharding import PartitionSpec as P

HALO = 2
LANES = 128
VMEM = pltpu.VMEM
LIMIT = 16 * 1024 * 1024
SMEM_SPEC = pl.BlockSpec(memory_space=pltpu.SMEM)
VMEM_SPEC = pl.BlockSpec(memory_space=VMEM)


def partner(index, distance, size):
    if size & (size - 1) == 0:
        return index ^ distance
    return (distance - index) % size


def partner_in_kernel(index, distance, size):
    if size & (size - 1) == 0:
        return lax.bitwise_xor(index, distance)
    return lax.rem(distance - index + size, size)


def trade(x, axis, distance, size):
    return lax.ppermute(x, axis, [(i, partner(i, distance, size)) for i in range(size)])


def pack_kernel(groups, owners, x_ref, out_ref):
    members, rows, cells, channels = x_ref.shape
    width = channels // (groups * owners)
    for e in range(members):
        for q in range(groups):
            parts = [
                x_ref[e, i, :, (p * groups + q) * width : (p * groups + q + 1) * width]
                for i in range(rows)
                for p in range(owners)
            ]
            out_ref[e, q] = jnp.concatenate(parts, axis=-1)


def pack(x, groups, owners):
    members, rows, cells, channels = x.shape
    return pl.pallas_call(
        functools.partial(pack_kernel, groups, owners),
        out_shape=jax.ShapeDtypeStruct((members, groups, cells, rows * channels // groups), x.dtype),
        in_specs=[VMEM_SPEC],
        out_specs=VMEM_SPEC,
        compiler_params=pltpu.CompilerParams(vmem_limit_bytes=LIMIT),
        name="pack",
    )(x)


def added(refs, *at):
    value = refs[0][at]
    for ref in refs[1:]:
        value = value + ref[at]
    return value


def conv_mix_kernel(geometry, counts, low_ref, shift_ref, place_ref, *refs):
    bases, taps, slots, halo, sub, groups = geometry
    refs = list(refs)
    field_slots = [[refs.pop(0) for _ in range(n)] for n in counts[0]]
    weight_refs = [refs.pop(0) for _ in range(counts[1])]
    mix_slots = [[refs.pop(0) for _ in range(n)] for n in counts[2]]
    field_rows, total, mix_all, mixed = refs[-4:]
    outs = refs[:-4]
    late, span, _ = field_slots[0][0].shape
    owners = len(field_slots)
    depth, width = mix_slots[0][0].shape[1:]
    channels = owners * depth
    padded = total.shape[-1]
    rows, _, block, _ = weight_refs[0].shape
    nblocks = owners * span // block
    cells = span // groups
    member, owner, group = place_ref[0], place_ref[1], place_ref[2]

    total[...] = jnp.zeros_like(total)
    field_rows[...] = jnp.zeros_like(field_rows)
    for s in range(late):
        lat = partner_in_kernel(member, s, late)
        for d, slot in enumerate(field_slots):
            at = pl.ds(pl.multiple_of(partner_in_kernel(owner, d, owners) * span, sub), span)
            value = added(slot, lat)
            for r in range(rows):
                field_rows[r, at, :channels] = value[:, r * channels : (r + 1) * channels]

        def one_row(r, carry):
            row = lat * rows + r
            for piece in range(span // sub):
                cell = owner * span + piece * sub
                b = lax.div(cell, block)
                q = pl.multiple_of(lax.rem(cell, block), sub)
                chosen = []
                for j in range(slots):
                    source = lax.rem(b + shift_ref[row, j] + nblocks, nblocks)
                    chosen.append(field_rows[r, pl.ds(pl.multiple_of(source * block, block), block)])
                picked = jnp.concatenate(chosen, axis=0)
                lhs = weight_refs[s][r, :, pl.ds(q, sub), :].reshape(bases * taps * sub, slots * block)
                product = jnp.dot(lhs, picked, preferred_element_type=jnp.float32)
                for k in range(bases):
                    at = pl.ds(row + low_ref[k, row] + HALO, taps)
                    slab = product[k * taps * sub : (k + 1) * taps * sub].reshape(taps, sub, padded)
                    total[k, at, piece * sub : (piece + 1) * sub] += slab
            return carry

        lax.fori_loop(0, rows, one_row, 0, unroll=2)

    for d, slot in enumerate(mix_slots):
        for k in range(bases):
            mix_all[place_ref[3 + d], k] = added(slot, k)
    fill = jnp.zeros((padded - channels, width), jnp.bfloat16)
    matrix = jnp.concatenate(
        [x for k in range(bases) for x in [mix_all[p, k] for p in range(owners)] + [fill]], axis=0
    )

    def one_out(first, count):
        at = pl.ds(first + HALO, count)
        lhs = [total[k, at].astype(jnp.bfloat16).reshape(count * span, padded) for k in range(bases)]
        product = jnp.dot(jnp.concatenate(lhs, axis=-1), matrix, preferred_element_type=jnp.float32)
        return product.reshape(count, span, width)

    for lat in range(late):
        mixed[lat * rows : (lat + 1) * rows] = one_out(lat * rows, rows)
    for dl in range(late):
        lat = partner_in_kernel(member, dl, late)
        for dq in range(groups):
            start = pl.multiple_of(partner_in_kernel(group, dq, groups) * cells, 8 if cells % 8 == 0 else cells)
            for r in range(rows):
                outs[dl * groups + dq][r] = mixed[lat * rows + r, pl.ds(start, cells)].astype(jnp.bfloat16)
    if halo:
        for side, first in enumerate((-halo, late * rows)):
            outs[-1][side] = one_out(first, halo).astype(jnp.bfloat16)


def conv_mix(low, shift, place, fields, weights, mix, halo, groups, block):
    bases, all_rows = low.shape
    slots = shift.shape[1]
    late, span, _ = fields[0][0].shape
    owners = len(fields)
    rows = all_rows // late
    depth, width = mix[0][0].shape[1:]
    padded = -(-owners * depth // LANES) * LANES
    taps = weights[0].shape[1] // bases
    sub = math.gcd(span, block)
    shapes = [jax.ShapeDtypeStruct((rows, span // groups, width), jnp.bfloat16)] * (late * groups)
    if halo:
        shapes.append(jax.ShapeDtypeStruct((2, halo, span, width), jnp.bfloat16))
    operands = [x for slot in fields for x in slot] + weights + [x for slot in mix for x in slot]
    counts = ([len(s) for s in fields], len(weights), [len(s) for s in mix])
    return pl.pallas_call(
        functools.partial(conv_mix_kernel, (bases, taps, slots, halo, sub, groups), counts),
        out_shape=shapes,
        in_specs=[SMEM_SPEC] * 3 + [VMEM_SPEC] * len(operands),
        out_specs=[VMEM_SPEC] * len(shapes),
        scratch_shapes=[
            VMEM((rows, owners * span, padded), jnp.bfloat16),
            VMEM((bases, all_rows + 2 * HALO, span, padded), jnp.float32),
            VMEM((owners, bases, depth, width), jnp.bfloat16),
            VMEM((all_rows, span, width), jnp.float32),
        ],
        compiler_params=pltpu.CompilerParams(vmem_limit_bytes=LIMIT),
        name="conv_mix",
    )(low, shift, place, *operands)


def finish_kernel(groups, place_ref, *refs):
    out_ref = refs[-1]
    late = out_ref.shape[0]
    for dl in range(late):
        total = refs[dl * groups][...].astype(jnp.float32)
        for dq in range(1, groups):
            total += refs[dl * groups + dq][...].astype(jnp.float32)
        value = total * (1.0 + lax.erf(total * (0.5**0.5))) * 0.5
        out_ref[partner_in_kernel(place_ref[0], dl, late)] = value.astype(jnp.bfloat16)


def finish(place, parts, groups):
    return pl.pallas_call(
        functools.partial(finish_kernel, groups),
        out_shape=jax.ShapeDtypeStruct((len(parts) // groups,) + parts[0].shape, jnp.bfloat16),
        in_specs=[SMEM_SPEC] + [VMEM_SPEC] * len(parts),
        out_specs=VMEM_SPEC,
        compiler_params=pltpu.CompilerParams(vmem_limit_bytes=LIMIT),
        name="finish",
    )(place, *parts)


def turn_kernel(x_ref, out_ref):
    bases, rows, taps, slots, block, _ = x_ref.shape
    unit = (lax.broadcasted_iota(jnp.int32, (block, block), 0) == lax.broadcasted_iota(jnp.int32, (block, block), 1))
    unit = unit.astype(jnp.float32).astype(x_ref.dtype)

    def one_row(r, carry):
        for k in range(bases):
            for t in range(taps):
                cells = x_ref[k, r, t].reshape(slots * block, block)
                turned = lax.dot_general(unit, cells, (((1,), (1,)), ((), ())), preferred_element_type=jnp.float32)
                out_ref[r, k * taps + t] = turned.astype(out_ref.dtype)
        return carry

    lax.fori_loop(0, rows, one_row, 0)


def turn(x):
    bases, rows, taps, slots, block, _ = x.shape
    return pl.pallas_call(
        turn_kernel,
        out_shape=jax.ShapeDtypeStruct((rows, bases * taps, block, slots * block), x.dtype),
        in_specs=[VMEM_SPEC],
        out_specs=VMEM_SPEC,
        compiler_params=pltpu.CompilerParams(vmem_limit_bytes=LIMIT),
        name="turn",
    )(x)


def pairs(*cores):
    return [(4 * c + a, 4 * c + b) for c, planes in enumerate(cores) for a, b in planes]


NEAR = [(0, 1), (1, 0), (2, 3), (3, 2)]
FAR = [(0, 2), (2, 0), (1, 3), (3, 1)]
MIDDLE = [(1, 2), (2, 1)]
TO_ENDS = [(1, 0), (2, 3)]


def gather(spread, mix, kernels, late, owners):
    core, own = lax.axis_index("late"), lax.axis_index("lonp")
    if owners != 4 or late != 2:
        fields = [[spread]] + [[trade(spread, "lonp", d, owners)] for d in range(1, owners)]
        mixes = [[mix]] + [[trade(mix, "lonp", d, owners)] for d in range(1, owners)]
        return fields, mixes, [partner(own, d, owners) for d in range(owners)], kernels
    first = lax.ppermute(mix, ("late", "lonp"), pairs(NEAR, FAR))
    spread, first, *kernels = lax.optimization_barrier((spread, first, *kernels))
    two = lax.ppermute(spread, "lonp", FAR)
    one = lax.ppermute(spread, "lonp", NEAR)
    spread_late, two, first = lax.optimization_barrier((spread, two, first))
    passed = lax.ppermute(two, "lonp", TO_ENDS)
    middle = lax.ppermute(spread_late, "lonp", MIDDLE)
    third = lax.ppermute(first, ("late", "lonp"), pairs([], NEAR))
    other = trade(first, "late", 1, late)
    copied = lax.ppermute(third, "late", [(1, 0)])
    fields = [[spread], [one], [two], [middle, passed]]
    mixes = [[mix], [first], [other], [third, copied]]
    return fields, mixes, [own, own ^ (1 + core), own ^ (2 - core), own ^ 3], kernels


def per_device(sizes, fields, kernel, band_low, block_shift, mix_weight):
    halves, late, owners, groups = sizes
    members, rows, channels, cells = fields.shape
    block = kernel.shape[-1]
    all_rows = late * rows
    halo = HALO if halves > 1 else 0

    kernels = [kernel] + [trade(kernel, "late", s, late) for s in range(1, late)]
    packed = pack(fields.transpose(0, 1, 3, 2), groups, owners)
    packed = packed.reshape((late * groups,) + packed.shape[2:])
    spread = lax.all_to_all(packed, ("late", "lonq"), split_axis=0, concat_axis=0, tiled=True)
    spread = spread.reshape(late, groups * cells, -1)
    spread, mix, origins, kernels = gather(spread, mix_weight, kernels, late, owners)
    weights = [turn(x) for x in kernels]

    start = lax.axis_index("lath") * all_rows
    low = lax.dynamic_slice_in_dim(band_low, start, all_rows, 1)
    shift = lax.dynamic_slice_in_dim(block_shift, start, all_rows, 0)
    place = [lax.axis_index("late"), lax.axis_index("lonp"), lax.axis_index("lonq")] + origins
    place = jnp.stack(place).astype(jnp.int32)
    partial = conv_mix(low, shift, place, spread, weights, mix, halo, groups, block)
    if halo:
        *partial, beyond = partial
        below = lax.ppermute(beyond[1], "lath", [(i, i + 1) for i in range(halves - 1)])
        above = lax.ppermute(beyond[0], "lath", [(i + 1, i) for i in range(halves - 1)])
        filler = jnp.zeros((all_rows - 2 * halo,) + below.shape[1:], below.dtype)
        extra = jnp.concatenate([below, filler, above], axis=0).reshape(late, rows, groups, cells, -1)
        for dl in range(late):
            lat = partner(lax.axis_index("late"), dl, late)
            for dq in range(groups):
                group = partner(lax.axis_index("lonq"), dq, groups)
                partial[dl * groups + dq] += extra[lat, :, group]
    parts = [
        lax.ppermute(
            partial[dl * groups + dq],
            ("late", "lonq"),
            [
                (l * groups + q, partner(l, dl, late) * groups + partner(q, dq, groups))
                for l in range(late)
                for q in range(groups)
            ],
        )
        if dl or dq
        else partial[0]
        for dl in range(late)
        for dq in range(groups)
    ]
    return finish(place, parts, groups)


def solution(mesh):
    lat, lon = mesh.shape["lat"], mesh.shape["lon"]
    groups = max(g for g in range(1, lon + 1) if lon % g == 0 and g * g <= lon)

    def whole(fields, kernel, band_low, block_shift, mix_weight):
        late = fields.shape[0]
        sizes = (lat // late, late, lon // groups, groups)
        split = Mesh(mesh.devices.reshape(sizes), ("lath", "late", "lonp", "lonq"))
        rows, cells = ("lath", "late"), ("lonp", "lonq")
        return jax.shard_map(
            functools.partial(per_device, sizes),
            mesh=split,
            in_specs=(
                P(None, rows, None, cells),
                P(None, rows, None, None, None, None),
                P(),
                P(),
                P(None, cells, None),
            ),
            out_specs=P(None, rows, cells, None),
            check_vma=False,
        )(fields, kernel, band_low, block_shift, mix_weight)

    return whole
```

```python
import functools
import math

import jax
import jax.numpy as jnp
from jax import lax
from jax.experimental import pallas as pl
from jax.experimental.pallas import tpu as pltpu
from jax.sharding import Mesh
from jax.sharding import PartitionSpec as P

HALO = 2
LANES = 128
VMEM = pltpu.VMEM
LIMIT = 16 * 1024 * 1024
SMEM_SPEC = pl.BlockSpec(memory_space=pltpu.SMEM)
VMEM_SPEC = pl.BlockSpec(memory_space=VMEM)


def partner(index, distance, size):
    if size & (size - 1) == 0:
        return index ^ distance
    return (distance - index) % size


def partner_in_kernel(index, distance, size):
    if size & (size - 1) == 0:
        return lax.bitwise_xor(index, distance)
    return lax.rem(distance - index + size, size)


def trade(x, axis, distance, size):
    return lax.ppermute(x, axis, [(i, partner(i, distance, size)) for i in range(size)])


def pack_kernel(groups, owners, x_ref, out_ref):
    members, rows, cells, channels = x_ref.shape
    width = channels // (groups * owners)
    for e in range(members):
        for q in range(groups):
            parts = [
                x_ref[e, i, :, (p * groups + q) * width : (p * groups + q + 1) * width]
                for i in range(rows)
                for p in range(owners)
            ]
            out_ref[e, q] = jnp.concatenate(parts, axis=-1)


def pack(x, groups, owners):
    members, rows, cells, channels = x.shape
    return pl.pallas_call(
        functools.partial(pack_kernel, groups, owners),
        out_shape=jax.ShapeDtypeStruct((members, groups, cells, rows * channels // groups), x.dtype),
        in_specs=[VMEM_SPEC],
        out_specs=VMEM_SPEC,
        compiler_params=pltpu.CompilerParams(vmem_limit_bytes=LIMIT),
        name="pack",
    )(x)


def conv_mix_kernel(geometry, counts, low_ref, shift_ref, place_ref, *refs):
    bases, taps, slots, halo, sub, groups = geometry
    refs = list(refs)
    field_refs, weight_refs, mix_refs = [[refs.pop(0) for _ in range(n)] for n in counts]
    field_rows, total, mix_all, mixed = refs[-4:]
    outs = refs[:-4]
    late, span, _ = field_refs[0].shape
    owners = len(field_refs)
    depth, width = mix_refs[0].shape[1:]
    channels = owners * depth
    padded = total.shape[-1]
    rows, _, block, _ = weight_refs[0].shape
    nblocks = owners * span // block
    cells = span // groups
    member, owner, group = place_ref[0], place_ref[1], place_ref[2]

    total[...] = jnp.zeros_like(total)
    field_rows[...] = jnp.zeros_like(field_rows)
    for s in range(late):
        lat = partner_in_kernel(member, s, late)
        for d, ref in enumerate(field_refs):
            at = pl.ds(pl.multiple_of(partner_in_kernel(owner, d, owners) * span, sub), span)
            value = ref[lat]
            for r in range(rows):
                field_rows[r, at, :channels] = value[:, r * channels : (r + 1) * channels]

        def one_row(r, carry):
            row = lat * rows + r
            for piece in range(span // sub):
                cell = owner * span + piece * sub
                b = lax.div(cell, block)
                q = pl.multiple_of(lax.rem(cell, block), sub)
                chosen = []
                for j in range(slots):
                    source = lax.rem(b + shift_ref[row, j] + nblocks, nblocks)
                    chosen.append(field_rows[r, pl.ds(pl.multiple_of(source * block, block), block)])
                picked = jnp.concatenate(chosen, axis=0)
                lhs = weight_refs[s][r, :, pl.ds(q, sub), :].reshape(bases * taps * sub, slots * block)
                product = jnp.dot(lhs, picked, preferred_element_type=jnp.float32)
                for k in range(bases):
                    at = pl.ds(row + low_ref[k, row] + HALO, taps)
                    slab = product[k * taps * sub : (k + 1) * taps * sub].reshape(taps, sub, padded)
                    total[k, at, piece * sub : (piece + 1) * sub] += slab
            return carry

        lax.fori_loop(0, rows, one_row, 0, unroll=2)

    for d, ref in enumerate(mix_refs):
        mix_all[partner_in_kernel(owner, d, owners)] = ref[...]
    fill = jnp.zeros((padded - channels, width), jnp.bfloat16)
    matrix = jnp.concatenate(
        [x for k in range(bases) for x in [mix_all[p, k] for p in range(owners)] + [fill]], axis=0
    )

    def one_out(first, count):
        at = pl.ds(first + HALO, count)
        lhs = [total[k, at].astype(jnp.bfloat16).reshape(count * span, padded) for k in range(bases)]
        product = jnp.dot(jnp.concatenate(lhs, axis=-1), matrix, preferred_element_type=jnp.float32)
        return product.reshape(count, span, width)

    for lat in range(late):
        mixed[lat * rows : (lat + 1) * rows] = one_out(lat * rows, rows)
    for dl in range(late):
        lat = partner_in_kernel(member, dl, late)
        for dq in range(groups):
            start = pl.multiple_of(partner_in_kernel(group, dq, groups) * cells, 8 if cells % 8 == 0 else cells)
            for r in range(rows):
                outs[dl * groups + dq][r] = mixed[lat * rows + r, pl.ds(start, cells)].astype(jnp.bfloat16)
    if halo:
        for side, first in enumerate((-halo, late * rows)):
            outs[-1][side] = one_out(first, halo).astype(jnp.bfloat16)


def conv_mix(low, shift, place, fields, weights, mix, halo, groups, block):
    bases, all_rows = low.shape
    slots = shift.shape[1]
    late, span, _ = fields[0].shape
    owners = len(fields)
    rows = all_rows // late
    depth, width = mix[0].shape[1:]
    padded = -(-owners * depth // LANES) * LANES
    taps = weights[0].shape[1] // bases
    sub = math.gcd(span, block)
    shapes = [jax.ShapeDtypeStruct((rows, span // groups, width), jnp.bfloat16)] * (late * groups)
    if halo:
        shapes.append(jax.ShapeDtypeStruct((2, halo, span, width), jnp.bfloat16))
    operands = fields + weights + mix
    counts = (len(fields), len(weights), len(mix))
    return pl.pallas_call(
        functools.partial(conv_mix_kernel, (bases, taps, slots, halo, sub, groups), counts),
        out_shape=shapes,
        in_specs=[SMEM_SPEC] * 3 + [VMEM_SPEC] * len(operands),
        out_specs=[VMEM_SPEC] * len(shapes),
        scratch_shapes=[
            VMEM((rows, owners * span, padded), jnp.bfloat16),
            VMEM((bases, all_rows + 2 * HALO, span, padded), jnp.float32),
            VMEM((owners, bases, depth, width), jnp.bfloat16),
            VMEM((all_rows, span, width), jnp.float32),
        ],
        compiler_params=pltpu.CompilerParams(vmem_limit_bytes=LIMIT),
        name="conv_mix",
    )(low, shift, place, *operands)


def finish_kernel(groups, place_ref, *refs):
    out_ref = refs[-1]
    late = out_ref.shape[0]
    for dl in range(late):
        total = refs[dl * groups][...].astype(jnp.float32)
        for dq in range(1, groups):
            total += refs[dl * groups + dq][...].astype(jnp.float32)
        value = total * (1.0 + lax.erf(total * (0.5**0.5))) * 0.5
        out_ref[partner_in_kernel(place_ref[0], dl, late)] = value.astype(jnp.bfloat16)


def finish(place, parts, groups):
    return pl.pallas_call(
        functools.partial(finish_kernel, groups),
        out_shape=jax.ShapeDtypeStruct((len(parts) // groups,) + parts[0].shape, jnp.bfloat16),
        in_specs=[SMEM_SPEC] + [VMEM_SPEC] * len(parts),
        out_specs=VMEM_SPEC,
        compiler_params=pltpu.CompilerParams(vmem_limit_bytes=LIMIT),
        name="finish",
    )(place, *parts)


def turn_kernel(x_ref, out_ref):
    bases, rows, taps, slots, block, _ = x_ref.shape
    unit = (lax.broadcasted_iota(jnp.int32, (block, block), 0) == lax.broadcasted_iota(jnp.int32, (block, block), 1))
    unit = unit.astype(jnp.float32).astype(x_ref.dtype)

    def one_row(r, carry):
        for k in range(bases):
            for t in range(taps):
                cells = x_ref[k, r, t].reshape(slots * block, block)
                turned = lax.dot_general(unit, cells, (((1,), (1,)), ((), ())), preferred_element_type=jnp.float32)
                out_ref[r, k * taps + t] = turned.astype(out_ref.dtype)
        return carry

    lax.fori_loop(0, rows, one_row, 0)


def turn(x):
    bases, rows, taps, slots, block, _ = x.shape
    return pl.pallas_call(
        turn_kernel,
        out_shape=jax.ShapeDtypeStruct((rows, bases * taps, block, slots * block), x.dtype),
        in_specs=[VMEM_SPEC],
        out_specs=VMEM_SPEC,
        compiler_params=pltpu.CompilerParams(vmem_limit_bytes=LIMIT),
        name="turn",
    )(x)


def gather(spread, mix, kernels, late, owners):
    if owners != 4:
        return *([x] + [trade(x, "lonp", d, owners) for d in range(1, owners)] for x in (spread, mix)), kernels
    mixes = [mix, trade(mix, "lonp", 1, owners), trade(mix, "lonp", 2, owners)]
    spread, *tied = lax.optimization_barrier((spread, *mixes[1:], *kernels))
    mixes[1:], kernels = tied[:2], tied[2:]
    fields = [spread] + [trade(spread, "lonp", d, owners) for d in (1, 2, 3)]
    return fields, mixes + [trade(mixes[2], "lonp", 1, owners)], kernels


def per_device(sizes, fields, kernel, band_low, block_shift, mix_weight):
    halves, late, owners, groups = sizes
    members, rows, channels, cells = fields.shape
    block = kernel.shape[-1]
    all_rows = late * rows
    halo = HALO if halves > 1 else 0

    kernels = [kernel] + [trade(kernel, "late", s, late) for s in range(1, late)]
    packed = pack(fields.transpose(0, 1, 3, 2), groups, owners)
    packed = packed.reshape((late * groups,) + packed.shape[2:])
    spread = lax.all_to_all(packed, ("late", "lonq"), split_axis=0, concat_axis=0, tiled=True)
    spread = spread.reshape(late, groups * cells, -1)
    spread, mix, kernels = gather(spread, mix_weight, kernels, late, owners)
    weights = [turn(x) for x in kernels]

    start = lax.axis_index("lath") * all_rows
    low = lax.dynamic_slice_in_dim(band_low, start, all_rows, 1)
    shift = lax.dynamic_slice_in_dim(block_shift, start, all_rows, 0)
    place = [lax.axis_index("late"), lax.axis_index("lonp"), lax.axis_index("lonq")]
    place = jnp.stack(place).astype(jnp.int32)
    partial = conv_mix(low, shift, place, spread, weights, mix, halo, groups, block)
    if halo:
        *partial, beyond = partial
        below = lax.ppermute(beyond[1], "lath", [(i, i + 1) for i in range(halves - 1)])
        above = lax.ppermute(beyond[0], "lath", [(i + 1, i) for i in range(halves - 1)])
        filler = jnp.zeros((all_rows - 2 * halo,) + below.shape[1:], below.dtype)
        extra = jnp.concatenate([below, filler, above], axis=0).reshape(late, rows, groups, cells, -1)
        for dl in range(late):
            lat = partner(lax.axis_index("late"), dl, late)
            for dq in range(groups):
                group = partner(lax.axis_index("lonq"), dq, groups)
                partial[dl * groups + dq] += extra[lat, :, group]
    parts = [
        lax.ppermute(
            partial[dl * groups + dq],
            ("late", "lonq"),
            [
                (l * groups + q, partner(l, dl, late) * groups + partner(q, dq, groups))
                for l in range(late)
                for q in range(groups)
            ],
        )
        if dl or dq
        else partial[0]
        for dl in range(late)
        for dq in range(groups)
    ]
    return finish(place, parts, groups)


def solution(mesh):
    lat, lon = mesh.shape["lat"], mesh.shape["lon"]
    groups = max(g for g in range(1, lon + 1) if lon % g == 0 and g * g <= lon)

    def whole(fields, kernel, band_low, block_shift, mix_weight):
        late = fields.shape[0]
        sizes = (lat // late, late, lon // groups, groups)
        split = Mesh(mesh.devices.reshape(sizes), ("lath", "late", "lonp", "lonq"))
        rows, cells = ("lath", "late"), ("lonp", "lonq")
        return jax.shard_map(
            functools.partial(per_device, sizes),
            mesh=split,
            in_specs=(
                P(None, rows, None, cells),
                P(None, rows, None, None, None, None),
                P(),
                P(),
                P(None, cells, None),
            ),
            out_specs=P(None, rows, cells, None),
            check_vma=False,
        )(fields, kernel, band_low, block_shift, mix_weight)

    return whole
```

```python
import functools
import math

import jax
import jax.numpy as jnp
from jax import lax
from jax.experimental import pallas as pl
from jax.experimental.pallas import tpu as pltpu
from jax.sharding import Mesh
from jax.sharding import PartitionSpec as P

HALO = 2
LANES = 128
VMEM = pltpu.VMEM
LIMIT = 16 * 1024 * 1024
SMEM_SPEC = pl.BlockSpec(memory_space=pltpu.SMEM)
VMEM_SPEC = pl.BlockSpec(memory_space=VMEM)


def partner(index, distance, size):
    if size & (size - 1) == 0:
        return index ^ distance
    return (distance - index) % size


def partner_in_kernel(index, distance, size):
    if size & (size - 1) == 0:
        return lax.bitwise_xor(index, distance)
    return lax.rem(distance - index + size, size)


def trade(x, axis, distance, size):
    return lax.ppermute(x, axis, [(i, partner(i, distance, size)) for i in range(size)])


def pack_kernel(groups, owners, x_ref, out_ref):
    members, rows, cells, channels = x_ref.shape
    width = channels // (groups * owners)
    for e in range(members):
        for q in range(groups):
            parts = [
                x_ref[e, i, :, (p * groups + q) * width : (p * groups + q + 1) * width]
                for i in range(rows)
                for p in range(owners)
            ]
            block = jnp.concatenate(parts, axis=-1)
            for p in range(owners):
                out_ref[e, p, q] = block


def pack(x, groups, owners):
    members, rows, cells, channels = x.shape
    return pl.pallas_call(
        functools.partial(pack_kernel, groups, owners),
        out_shape=jax.ShapeDtypeStruct((members, owners, groups, cells, rows * channels // groups), x.dtype),
        in_specs=[VMEM_SPEC],
        out_specs=VMEM_SPEC,
        compiler_params=pltpu.CompilerParams(vmem_limit_bytes=LIMIT),
        name="pack",
    )(x)


def conv_kernel(geometry, low_ref, shift_ref, place_ref, fields_ref, *refs):
    bases, taps, slots, halo, sub = geometry
    late, owners, span, _ = fields_ref.shape
    weight_refs = refs[:late]
    outs = refs[late:-2]
    field_rows, total = refs[-2:]
    padded = total.shape[-1]
    rows, _, block, _ = weight_refs[0].shape
    channels = fields_ref.shape[-1] // rows
    nblocks = owners * span // block
    member, owner = place_ref[0], place_ref[1]

    total[...] = jnp.zeros_like(total)
    field_rows[...] = jnp.zeros_like(field_rows)
    for s in range(late):
        lat = partner_in_kernel(member, s, late)
        for p in range(owners):
            value = fields_ref[lat, p]
            for r in range(rows):
                field_rows[r, p * span : (p + 1) * span, :channels] = value[:, r * channels : (r + 1) * channels]

        def one_row(r, carry):
            row = lat * rows + r
            for piece in range(span // sub):
                cell = owner * span + piece * sub
                b = lax.div(cell, block)
                q = pl.multiple_of(lax.rem(cell, block), sub)
                chosen = []
                for j in range(slots):
                    source = lax.rem(b + shift_ref[row, j] + nblocks, nblocks)
                    chosen.append(field_rows[r, pl.ds(pl.multiple_of(source * block, block), block)])
                picked = jnp.concatenate(chosen, axis=0)
                lhs = weight_refs[s][r, :, pl.ds(q, sub), :].reshape(bases * taps * sub, slots * block)
                product = jnp.dot(lhs, picked, preferred_element_type=jnp.float32)
                for k in range(bases):
                    at = pl.ds(row + low_ref[k, row] + HALO, taps)
                    slab = product[k * taps * sub : (k + 1) * taps * sub].reshape(taps, sub, padded)
                    total[k, at, piece * sub : (piece + 1) * sub] += slab
            return carry

        lax.fori_loop(0, rows, one_row, 0, unroll=2)

    for dl in range(late):
        at = pl.ds(partner_in_kernel(member, dl, late) * rows + HALO, rows)
        for k in range(bases):
            outs[dl][:, :, k * padded : (k + 1) * padded] = total[k, at].astype(jnp.bfloat16)
    if halo:
        for side, first in enumerate((0, late * rows + HALO)):
            for k in range(bases):
                outs[-1][side * halo : (side + 1) * halo, :, k * padded : (k + 1) * padded] = total[
                    k, first : first + halo
                ].astype(jnp.bfloat16)


def conv(low, shift, place, fields, weights, halo, block):
    bases, all_rows = low.shape
    slots = shift.shape[1]
    late, owners, span, lanes = fields.shape
    rows = all_rows // late
    padded = -(-lanes // rows // LANES) * LANES
    taps = weights[0].shape[1] // bases
    shapes = [jax.ShapeDtypeStruct((rows, span, bases * padded), jnp.bfloat16)] * late
    if halo:
        shapes.append(jax.ShapeDtypeStruct((2 * halo, span, bases * padded), jnp.bfloat16))
    return pl.pallas_call(
        functools.partial(conv_kernel, (bases, taps, slots, halo, math.gcd(span, block))),
        out_shape=shapes,
        in_specs=[SMEM_SPEC] * 3 + [VMEM_SPEC] * (1 + late),
        out_specs=[VMEM_SPEC] * len(shapes),
        scratch_shapes=[
            VMEM((rows, owners * span, padded), jnp.bfloat16),
            VMEM((bases, all_rows + 2 * HALO, span, padded), jnp.float32),
        ],
        compiler_params=pltpu.CompilerParams(vmem_limit_bytes=LIMIT),
        name="conv",
    )(low, shift, place, fields, *weights)


def mix_kernel(groups, counts, place_ref, conv_ref, *refs):
    refs = list(refs)
    slots = [[refs.pop(0) for _ in range(n)] for n in counts]
    ordered, mixed = refs[-2:]
    outs = refs[:-2]
    owners, bases, depth, width = ordered.shape
    rows, span, lanes = conv_ref.shape
    cells = span // groups
    for d, slot in enumerate(slots):
        value = slot[0][...]
        for ref in slot[1:]:
            value = value + ref[...]
        ordered[place_ref[3 + d]] = value
    fill = jnp.zeros((lanes // bases - owners * depth, width), jnp.bfloat16)
    parts = [x for k in range(bases) for x in [ordered[p, k] for p in range(owners)] + [fill]]
    matrix = jnp.concatenate(parts, axis=0)
    lhs = conv_ref[...].reshape(rows * span, lanes)
    mixed[...] = jnp.dot(lhs, matrix, preferred_element_type=jnp.float32).reshape(rows, span, width)
    for dq in range(groups):
        start = pl.multiple_of(partner_in_kernel(place_ref[2], dq, groups) * cells, 8 if cells % 8 == 0 else cells)
        for r in range(rows):
            outs[dq][r] = mixed[r, pl.ds(start, cells)].astype(jnp.bfloat16)


def mix_rows(place, rows, mix, groups):
    count, span, _ = rows.shape
    bases, depth, width = mix[0][0].shape
    operands = [x for slot in mix for x in slot]
    return pl.pallas_call(
        functools.partial(mix_kernel, groups, [len(slot) for slot in mix]),
        out_shape=[jax.ShapeDtypeStruct((count, span // groups, width), jnp.bfloat16)] * groups,
        in_specs=[SMEM_SPEC] + [VMEM_SPEC] * (1 + len(operands)),
        out_specs=[VMEM_SPEC] * groups,
        scratch_shapes=[VMEM((len(mix), bases, depth, width), jnp.bfloat16), VMEM((count, span, width), jnp.float32)],
        compiler_params=pltpu.CompilerParams(vmem_limit_bytes=LIMIT),
        name="mix",
    )(place, rows, *operands)


def finish_kernel(groups, place_ref, *refs):
    out_ref = refs[-1]
    late = out_ref.shape[0]
    for dl in range(late):
        total = refs[dl * groups][...].astype(jnp.float32)
        for dq in range(1, groups):
            total += refs[dl * groups + dq][...].astype(jnp.float32)
        value = total * (1.0 + lax.erf(total * (0.5**0.5))) * 0.5
        out_ref[partner_in_kernel(place_ref[0], dl, late)] = value.astype(jnp.bfloat16)


def finish(place, parts, groups):
    return pl.pallas_call(
        functools.partial(finish_kernel, groups),
        out_shape=jax.ShapeDtypeStruct((len(parts) // groups,) + parts[0].shape, jnp.bfloat16),
        in_specs=[SMEM_SPEC] + [VMEM_SPEC] * len(parts),
        out_specs=VMEM_SPEC,
        compiler_params=pltpu.CompilerParams(vmem_limit_bytes=LIMIT),
        name="finish",
    )(place, *parts)


def turn_kernel(x_ref, out_ref):
    bases, rows, taps, slots, block, _ = x_ref.shape
    unit = (lax.broadcasted_iota(jnp.int32, (block, block), 0) == lax.broadcasted_iota(jnp.int32, (block, block), 1))
    unit = unit.astype(jnp.float32).astype(x_ref.dtype)

    def one_row(r, carry):
        for k in range(bases):
            for t in range(taps):
                cells = x_ref[k, r, t].reshape(slots * block, block)
                turned = lax.dot_general(unit, cells, (((1,), (1,)), ((), ())), preferred_element_type=jnp.float32)
                out_ref[r, k * taps + t] = turned.astype(out_ref.dtype)
        return carry

    lax.fori_loop(0, rows, one_row, 0)


def turn(x):
    bases, rows, taps, slots, block, _ = x.shape
    return pl.pallas_call(
        turn_kernel,
        out_shape=jax.ShapeDtypeStruct((rows, bases * taps, block, slots * block), x.dtype),
        in_specs=[VMEM_SPEC],
        out_specs=VMEM_SPEC,
        compiler_params=pltpu.CompilerParams(vmem_limit_bytes=LIMIT),
        name="turn",
    )(x)


def fetch_mix(mix, late, owners):
    if owners == 4 and late == 2:
        first = lax.ppermute(mix, ("late", "lonp"), [(4 * c + p, 4 * c + (p ^ (1 + c))) for c in range(2) for p in range(4)])
        far = [(0, 3), (3, 0)], [(1, 2), (2, 1)]
        third = lax.ppermute(mix, ("late", "lonp"), [(4 * c + a, 4 * c + b) for c in range(2) for a, b in far[c]])
        return [first, third]
    return [trade(mix, "lonp", d, owners) for d in range(1, owners)]


def gather_mix(mix, fetched, late, owners):
    core, own = lax.axis_index("late"), lax.axis_index("lonp")
    if owners == 4 and late == 2:
        first, third = fetched
        slots = [[mix], [first], [trade(first, "late", 1, late)], [third, trade(third, "late", 1, late)]]
        return slots, [own, own ^ (1 + core), own ^ (2 - core), own ^ 3]
    return [[mix]] + [[x] for x in fetched], [partner(own, d, owners) for d in range(owners)]


def per_device(sizes, fields, kernel, band_low, block_shift, mix_weight):
    halves, late, owners, groups = sizes
    members, rows, channels, cells = fields.shape
    block = kernel.shape[-1]
    all_rows = late * rows
    halo = HALO if halves > 1 else 0

    packed = pack(fields.transpose(0, 1, 3, 2), groups, owners)
    packed = packed.reshape((-1,) + packed.shape[3:])
    spread = lax.all_to_all(packed, ("late", "lonp", "lonq"), split_axis=0, concat_axis=0, tiled=True)
    spread = spread.reshape(late, owners, groups * cells, -1)
    weights = [turn(x) for x in [kernel] + [trade(kernel, "late", s, late) for s in range(1, late)]]
    fetched = fetch_mix(mix_weight, late, owners)

    start = lax.axis_index("lath") * all_rows
    low = lax.dynamic_slice_in_dim(band_low, start, all_rows, 1)
    shift = lax.dynamic_slice_in_dim(block_shift, start, all_rows, 0)
    place = [lax.axis_index("late"), lax.axis_index("lonp"), lax.axis_index("lonq")]
    convolved = conv(low, shift, jnp.stack(place).astype(jnp.int32), spread, weights, halo, block)
    fetched, convolved = lax.optimization_barrier((fetched, convolved))
    mix, origins = gather_mix(mix_weight, fetched, late, owners)
    place = jnp.stack(place + origins).astype(jnp.int32)
    partial = [None] * late
    for dl in reversed(range(late)):
        partial[dl] = list(mix_rows(place, convolved[dl], mix, groups))
    if halo:
        beyond = mix_rows(place, convolved[-1], mix, groups)
        below = [lax.ppermute(x[halo:], "lath", [(i, i + 1) for i in range(halves - 1)]) for x in beyond]
        above = [lax.ppermute(x[:halo], "lath", [(i + 1, i) for i in range(halves - 1)]) for x in beyond]
        for dq in range(groups):
            filler = jnp.zeros((all_rows - 2 * halo,) + below[dq].shape[1:], below[dq].dtype)
            extra = jnp.concatenate([below[dq], filler, above[dq]], axis=0).reshape((late,) + partial[0][dq].shape)
            for dl in range(late):
                partial[dl][dq] += extra[partner(lax.axis_index("late"), dl, late)]
    parts = [
        lax.ppermute(
            partial[dl][dq],
            ("late", "lonq"),
            [
                (l * groups + q, partner(l, dl, late) * groups + partner(q, dq, groups))
                for l in range(late)
                for q in range(groups)
            ],
        )
        if dl or dq
        else partial[0][0]
        for dl in range(late)
        for dq in range(groups)
    ]
    return finish(place, parts, groups)


def solution(mesh):
    lat, lon = mesh.shape["lat"], mesh.shape["lon"]
    groups = max(g for g in range(1, lon + 1) if lon % g == 0 and g * g <= lon)

    def whole(fields, kernel, band_low, block_shift, mix_weight):
        late = fields.shape[0]
        sizes = (lat // late, late, lon // groups, groups)
        split = Mesh(mesh.devices.reshape(sizes), ("lath", "late", "lonp", "lonq"))
        rows, cells = ("lath", "late"), ("lonp", "lonq")
        return jax.shard_map(
            functools.partial(per_device, sizes),
            mesh=split,
            in_specs=(
                P(None, rows, None, cells),
                P(None, rows, None, None, None, None),
                P(),
                P(),
                P(None, cells, None),
            ),
            out_specs=P(None, rows, cells, None),
            check_vma=False,
        )(fields, kernel, band_low, block_shift, mix_weight)

    return whole
```

```python
import functools
import math

import jax
import jax.numpy as jnp
from jax import lax
from jax.experimental import pallas as pl
from jax.experimental.pallas import tpu as pltpu
from jax.sharding import Mesh
from jax.sharding import PartitionSpec as P

HALO = 2
LANES = 128
VMEM = pltpu.VMEM
LIMIT = 16 * 1024 * 1024
SMEM_SPEC = pl.BlockSpec(memory_space=pltpu.SMEM)
VMEM_SPEC = pl.BlockSpec(memory_space=VMEM)


def partner(index, distance, size):
    if size & (size - 1) == 0:
        return index ^ distance
    return (distance - index) % size


def partner_in_kernel(index, distance, size):
    if size & (size - 1) == 0:
        return lax.bitwise_xor(index, distance)
    return lax.rem(distance - index + size, size)


def trade(x, axis, distance, size):
    return lax.ppermute(x, axis, [(i, partner(i, distance, size)) for i in range(size)])


def pack_kernel(groups, owners, x_ref, out_ref):
    members, rows, cells, channels = x_ref.shape
    width = channels // (groups * owners)
    for e in range(members):
        for q in range(groups):
            parts = [
                x_ref[e, i, :, (p * groups + q) * width : (p * groups + q + 1) * width]
                for i in range(rows)
                for p in range(owners)
            ]
            out_ref[e, q] = jnp.concatenate(parts, axis=-1)


def pack(x, groups, owners):
    members, rows, cells, channels = x.shape
    return pl.pallas_call(
        functools.partial(pack_kernel, groups, owners),
        out_shape=jax.ShapeDtypeStruct((members, groups, cells, rows * channels // groups), x.dtype),
        in_specs=[VMEM_SPEC],
        out_specs=VMEM_SPEC,
        compiler_params=pltpu.CompilerParams(vmem_limit_bytes=LIMIT),
        name="pack",
    )(x)


def conv_mix_kernel(geometry, counts, low_ref, shift_ref, place_ref, *refs):
    bases, taps, slots, halo, sub, groups = geometry
    refs = list(refs)
    field_refs, weight_refs, mix_refs = [[refs.pop(0) for _ in range(n)] for n in counts]
    field_rows, total, mix_all, mixed = refs[-4:]
    outs = refs[:-4]
    late, span, _ = field_refs[0].shape
    owners = len(field_refs)
    depth, width = mix_refs[0].shape[1:]
    channels = owners * depth
    padded = total.shape[-1]
    rows, _, block, _ = weight_refs[0].shape
    nblocks = owners * span // block
    cells = span // groups
    member, owner, group = place_ref[0], place_ref[1], place_ref[2]

    total[...] = jnp.zeros_like(total)
    field_rows[...] = jnp.zeros_like(field_rows)
    for s in range(late):
        lat = partner_in_kernel(member, s, late)
        for d, ref in enumerate(field_refs):
            at = pl.ds(pl.multiple_of(partner_in_kernel(owner, d, owners) * span, sub), span)
            value = ref[lat]
            for r in range(rows):
                field_rows[r, at, :channels] = value[:, r * channels : (r + 1) * channels]

        def one_row(r, carry):
            row = lat * rows + r
            for piece in range(span // sub):
                cell = owner * span + piece * sub
                b = lax.div(cell, block)
                q = pl.multiple_of(lax.rem(cell, block), sub)
                chosen = []
                for j in range(slots):
                    source = lax.rem(b + shift_ref[row, j] + nblocks, nblocks)
                    chosen.append(field_rows[r, pl.ds(pl.multiple_of(source * block, block), block)])
                picked = jnp.concatenate(chosen, axis=0)
                lhs = weight_refs[s][r, :, pl.ds(q, sub), :].reshape(bases * taps * sub, slots * block)
                product = jnp.dot(lhs, picked, preferred_element_type=jnp.float32)
                for k in range(bases):
                    at = pl.ds(row + low_ref[k, row] + HALO, taps)
                    slab = product[k * taps * sub : (k + 1) * taps * sub].reshape(taps, sub, padded)
                    total[k, at, piece * sub : (piece + 1) * sub] += slab
            return carry

        lax.fori_loop(0, rows, one_row, 0, unroll=2)

    for d, ref in enumerate(mix_refs):
        mix_all[partner_in_kernel(owner, d, owners)] = ref[...]
    fill = jnp.zeros((padded - channels, width), jnp.bfloat16)
    matrix = jnp.concatenate(
        [x for k in range(bases) for x in [mix_all[p, k] for p in range(owners)] + [fill]], axis=0
    )

    def one_out(first, count):
        at = pl.ds(first + HALO, count)
        lhs = [total[k, at].astype(jnp.bfloat16).reshape(count * span, padded) for k in range(bases)]
        product = jnp.dot(jnp.concatenate(lhs, axis=-1), matrix, preferred_element_type=jnp.float32)
        return product.reshape(count, span, width)

    for lat in range(late):
        mixed[lat * rows : (lat + 1) * rows] = one_out(lat * rows, rows)
    for dl in range(late):
        lat = partner_in_kernel(member, dl, late)
        for dq in range(groups):
            start = pl.multiple_of(partner_in_kernel(group, dq, groups) * cells, 8 if cells % 8 == 0 else cells)
            for r in range(rows):
                outs[dl * groups + dq][r] = mixed[lat * rows + r, pl.ds(start, cells)].astype(jnp.bfloat16)
    if halo:
        for side, first in enumerate((-halo, late * rows)):
            outs[-1][side] = one_out(first, halo).astype(jnp.bfloat16)


def conv_mix(low, shift, place, fields, weights, mix, halo, groups, block):
    bases, all_rows = low.shape
    slots = shift.shape[1]
    late, span, _ = fields[0].shape
    owners = len(fields)
    rows = all_rows // late
    depth, width = mix[0].shape[1:]
    padded = -(-owners * depth // LANES) * LANES
    taps = weights[0].shape[1] // bases
    sub = math.gcd(span, block)
    shapes = [jax.ShapeDtypeStruct((rows, span // groups, width), jnp.bfloat16)] * (late * groups)
    if halo:
        shapes.append(jax.ShapeDtypeStruct((2, halo, span, width), jnp.bfloat16))
    operands = fields + weights + mix
    counts = (len(fields), len(weights), len(mix))
    return pl.pallas_call(
        functools.partial(conv_mix_kernel, (bases, taps, slots, halo, sub, groups), counts),
        out_shape=shapes,
        in_specs=[SMEM_SPEC] * 3 + [VMEM_SPEC] * len(operands),
        out_specs=[VMEM_SPEC] * len(shapes),
        scratch_shapes=[
            VMEM((rows, owners * span, padded), jnp.bfloat16),
            VMEM((bases, all_rows + 2 * HALO, span, padded), jnp.float32),
            VMEM((owners, bases, depth, width), jnp.bfloat16),
            VMEM((all_rows, span, width), jnp.float32),
        ],
        compiler_params=pltpu.CompilerParams(vmem_limit_bytes=LIMIT),
        name="conv_mix",
    )(low, shift, place, *operands)


def finish_kernel(groups, place_ref, *refs):
    out_ref = refs[-1]
    late = out_ref.shape[0]
    for dl in range(late):
        total = refs[dl * groups][...].astype(jnp.float32)
        for dq in range(1, groups):
            total += refs[dl * groups + dq][...].astype(jnp.float32)
        value = total * (1.0 + lax.erf(total * (0.5**0.5))) * 0.5
        out_ref[partner_in_kernel(place_ref[0], dl, late)] = value.astype(jnp.bfloat16)


def finish(place, parts, groups):
    return pl.pallas_call(
        functools.partial(finish_kernel, groups),
        out_shape=jax.ShapeDtypeStruct((len(parts) // groups,) + parts[0].shape, jnp.bfloat16),
        in_specs=[SMEM_SPEC] + [VMEM_SPEC] * len(parts),
        out_specs=VMEM_SPEC,
        compiler_params=pltpu.CompilerParams(vmem_limit_bytes=LIMIT),
        name="finish",
    )(place, *parts)


def turn_kernel(x_ref, out_ref):
    bases, rows, taps, slots, block, _ = x_ref.shape
    unit = (lax.broadcasted_iota(jnp.int32, (block, block), 0) == lax.broadcasted_iota(jnp.int32, (block, block), 1))
    unit = unit.astype(jnp.float32).astype(x_ref.dtype)

    def one_row(r, carry):
        for k in range(bases):
            for t in range(taps):
                cells = x_ref[k, r, t].reshape(slots * block, block)
                turned = lax.dot_general(unit, cells, (((1,), (1,)), ((), ())), preferred_element_type=jnp.float32)
                out_ref[r, k * taps + t] = turned.astype(out_ref.dtype)
        return carry

    lax.fori_loop(0, rows, one_row, 0)


def turn(x):
    bases, rows, taps, slots, block, _ = x.shape
    return pl.pallas_call(
        turn_kernel,
        out_shape=jax.ShapeDtypeStruct((rows, bases * taps, block, slots * block), x.dtype),
        in_specs=[VMEM_SPEC],
        out_specs=VMEM_SPEC,
        compiler_params=pltpu.CompilerParams(vmem_limit_bytes=LIMIT),
        name="turn",
    )(x)


def gather(spread, mix, kernels, late, owners):
    if owners != 4:
        return *([x] + [trade(x, "lonp", d, owners) for d in range(1, owners)] for x in (spread, mix)), kernels
    two = trade(mix, "lonp", 2, owners)
    one = trade(mix, "lonp", 1, owners)
    spread, two, one, *kernels = lax.optimization_barrier((spread, two, one, *kernels))
    fields = [trade(spread, "lonp", d, owners) for d in (3, 2, 1)] + [spread]
    return fields[::-1], [mix, one, two, trade(two, "lonp", 1, owners)], kernels


def send_rank(dl, dq):
    first = [(0, 0), (1, 0), (0, 1), (0, 3), (1, 3), (1, 1), (0, 2), (1, 2)]
    return first.index((dl, dq)) if (dl, dq) in first else len(first) + dl + dq


def per_device(sizes, fields, kernel, band_low, block_shift, mix_weight):
    halves, late, owners, groups = sizes
    members, rows, channels, cells = fields.shape
    block = kernel.shape[-1]
    all_rows = late * rows
    halo = HALO if halves > 1 else 0

    kernels = [kernel] + [trade(kernel, "late", s, late) for s in range(1, late)]
    packed = pack(fields.transpose(0, 1, 3, 2), groups, owners)
    packed = packed.reshape((late * groups,) + packed.shape[2:])
    spread = lax.all_to_all(packed, ("late", "lonq"), split_axis=0, concat_axis=0, tiled=True)
    spread = spread.reshape(late, groups * cells, -1)
    spread, mix, kernels = gather(spread, mix_weight, kernels, late, owners)
    weights = [turn(x) for x in kernels]

    start = lax.axis_index("lath") * all_rows
    low = lax.dynamic_slice_in_dim(band_low, start, all_rows, 1)
    shift = lax.dynamic_slice_in_dim(block_shift, start, all_rows, 0)
    place = [lax.axis_index("late"), lax.axis_index("lonp"), lax.axis_index("lonq")]
    place = jnp.stack(place).astype(jnp.int32)
    partial = conv_mix(low, shift, place, spread, weights, mix, halo, groups, block)
    if halo:
        *partial, beyond = partial
        below = lax.ppermute(beyond[1], "lath", [(i, i + 1) for i in range(halves - 1)])
        above = lax.ppermute(beyond[0], "lath", [(i + 1, i) for i in range(halves - 1)])
        filler = jnp.zeros((all_rows - 2 * halo,) + below.shape[1:], below.dtype)
        extra = jnp.concatenate([below, filler, above], axis=0).reshape(late, rows, groups, cells, -1)
        for dl in range(late):
            lat = partner(lax.axis_index("late"), dl, late)
            for dq in range(groups):
                group = partner(lax.axis_index("lonq"), dq, groups)
                partial[dl * groups + dq] += extra[lat, :, group]
    order = sorted(((dl, dq) for dl in range(late) for dq in range(groups)), key=lambda at: send_rank(*at))
    parts = [[None] * groups for _ in range(late)]
    for dl, dq in order:
        route = [
            (l * groups + q, partner(l, dl, late) * groups + partner(q, dq, groups))
            for l in range(late)
            for q in range(groups)
        ]
        block = partial[dl * groups + dq]
        parts[dl][dq] = lax.ppermute(block, ("late", "lonq"), route) if dl or dq else block
    parts = [x for row in parts for x in row]
    return finish(place, parts, groups)


def solution(mesh):
    lat, lon = mesh.shape["lat"], mesh.shape["lon"]
    groups = max(g for g in range(1, lon + 1) if lon % g == 0 and g * g <= lon)

    def whole(fields, kernel, band_low, block_shift, mix_weight):
        late = fields.shape[0]
        sizes = (lat // late, late, lon // groups, groups)
        split = Mesh(mesh.devices.reshape(sizes), ("lath", "late", "lonp", "lonq"))
        rows, cells = ("lath", "late"), ("lonp", "lonq")
        return jax.shard_map(
            functools.partial(per_device, sizes),
            mesh=split,
            in_specs=(
                P(None, rows, None, cells),
                P(None, rows, None, None, None, None),
                P(),
                P(),
                P(None, cells, None),
            ),
            out_specs=P(None, rows, cells, None),
            check_vma=False,
        )(fields, kernel, band_low, block_shift, mix_weight)

    return whole
```

```python
import functools
import math

import jax
import jax.numpy as jnp
from jax import lax
from jax.experimental import pallas as pl
from jax.experimental.pallas import tpu as pltpu
from jax.sharding import Mesh
from jax.sharding import PartitionSpec as P

HALO = 2
LANES = 128
VMEM = pltpu.VMEM
LIMIT = 16 * 1024 * 1024
SMEM_SPEC = pl.BlockSpec(memory_space=pltpu.SMEM)
VMEM_SPEC = pl.BlockSpec(memory_space=VMEM)


def partner(index, distance, size):
    if size & (size - 1) == 0:
        return index ^ distance
    return (distance - index) % size


def partner_in_kernel(index, distance, size):
    if size & (size - 1) == 0:
        return lax.bitwise_xor(index, distance)
    return lax.rem(distance - index + size, size)


def trade(x, axis, distance, size):
    return lax.ppermute(x, axis, [(i, partner(i, distance, size)) for i in range(size)])


def pack_kernel(groups, owners, x_ref, out_ref):
    members, rows, cells, channels = x_ref.shape
    width = channels // (groups * owners)
    for e in range(members):
        for q in range(groups):
            parts = [
                x_ref[e, i, :, (p * groups + q) * width : (p * groups + q + 1) * width]
                for i in range(rows)
                for p in range(owners)
            ]
            out_ref[e, q] = jnp.concatenate(parts, axis=-1)


def pack(x, groups, owners):
    members, rows, cells, channels = x.shape
    return pl.pallas_call(
        functools.partial(pack_kernel, groups, owners),
        out_shape=jax.ShapeDtypeStruct((members, groups, cells, rows * channels // groups), x.dtype),
        in_specs=[VMEM_SPEC],
        out_specs=VMEM_SPEC,
        compiler_params=pltpu.CompilerParams(vmem_limit_bytes=LIMIT),
        name="pack",
    )(x)


def conv_mix_kernel(geometry, counts, low_ref, shift_ref, place_ref, *refs):
    bases, taps, slots, halo, sub, groups = geometry
    refs = list(refs)
    field_refs, weight_refs, mix_refs = [[refs.pop(0) for _ in range(n)] for n in counts]
    field_refs = field_refs[::-1]
    field_rows, total, mix_all, mixed = refs[-4:]
    outs = refs[:-4]
    late, span, _ = field_refs[0].shape
    owners = len(field_refs)
    depth, width = mix_refs[0].shape[1:]
    channels = owners * depth
    padded = total.shape[-1]
    rows, _, block, _ = weight_refs[0].shape
    nblocks = owners * span // block
    cells = span // groups
    member, owner, group = place_ref[0], place_ref[1], place_ref[2]

    total[...] = jnp.zeros_like(total)
    field_rows[...] = jnp.zeros_like(field_rows)
    for s in range(late):
        lat = partner_in_kernel(member, s, late)
        for d, ref in enumerate(field_refs):
            at = pl.ds(pl.multiple_of(partner_in_kernel(owner, d, owners) * span, sub), span)
            value = ref[lat]
            for r in range(rows):
                field_rows[r, at, :channels] = value[:, r * channels : (r + 1) * channels]

        def one_row(r, carry):
            row = lat * rows + r
            for piece in range(span // sub):
                cell = owner * span + piece * sub
                b = lax.div(cell, block)
                q = pl.multiple_of(lax.rem(cell, block), sub)
                chosen = []
                for j in range(slots):
                    source = lax.rem(b + shift_ref[row, j] + nblocks, nblocks)
                    chosen.append(field_rows[r, pl.ds(pl.multiple_of(source * block, block), block)])
                picked = jnp.concatenate(chosen, axis=0)
                lhs = weight_refs[s][r, :, pl.ds(q, sub), :].reshape(bases * taps * sub, slots * block)
                product = jnp.dot(lhs, picked, preferred_element_type=jnp.float32)
                for k in range(bases):
                    at = pl.ds(row + low_ref[k, row] + HALO, taps)
                    slab = product[k * taps * sub : (k + 1) * taps * sub].reshape(taps, sub, padded)
                    total[k, at, piece * sub : (piece + 1) * sub] += slab
            return carry

        lax.fori_loop(0, rows, one_row, 0, unroll=2)

    for d, ref in enumerate(mix_refs):
        mix_all[partner_in_kernel(owner, d, owners)] = ref[...]
    fill = jnp.zeros((padded - channels, width), jnp.bfloat16)
    matrix = jnp.concatenate(
        [x for k in range(bases) for x in [mix_all[p, k] for p in range(owners)] + [fill]], axis=0
    )

    def one_out(first, count):
        at = pl.ds(first + HALO, count)
        lhs = [total[k, at].astype(jnp.bfloat16).reshape(count * span, padded) for k in range(bases)]
        product = jnp.dot(jnp.concatenate(lhs, axis=-1), matrix, preferred_element_type=jnp.float32)
        return product.reshape(count, span, width)

    for lat in range(late):
        mixed[lat * rows : (lat + 1) * rows] = one_out(lat * rows, rows)
    for dl in range(late):
        lat = partner_in_kernel(member, dl, late)
        for dq in range(groups):
            start = pl.multiple_of(partner_in_kernel(group, dq, groups) * cells, 8 if cells % 8 == 0 else cells)
            for r in range(rows):
                outs[dl * groups + dq][r] = mixed[lat * rows + r, pl.ds(start, cells)].astype(jnp.bfloat16)
    if halo:
        for side, first in enumerate((-halo, late * rows)):
            outs[-1][side] = one_out(first, halo).astype(jnp.bfloat16)


def conv_mix(low, shift, place, fields, weights, mix, halo, groups, block):
    bases, all_rows = low.shape
    slots = shift.shape[1]
    late, span, _ = fields[0].shape
    owners = len(fields)
    rows = all_rows // late
    depth, width = mix[0].shape[1:]
    padded = -(-owners * depth // LANES) * LANES
    taps = weights[0].shape[1] // bases
    sub = math.gcd(span, block)
    shapes = [jax.ShapeDtypeStruct((rows, span // groups, width), jnp.bfloat16)] * (late * groups)
    if halo:
        shapes.append(jax.ShapeDtypeStruct((2, halo, span, width), jnp.bfloat16))
    operands = fields[::-1] + weights + mix
    counts = (len(fields), len(weights), len(mix))
    return pl.pallas_call(
        functools.partial(conv_mix_kernel, (bases, taps, slots, halo, sub, groups), counts),
        out_shape=shapes,
        in_specs=[SMEM_SPEC] * 3 + [VMEM_SPEC] * len(operands),
        out_specs=[VMEM_SPEC] * len(shapes),
        scratch_shapes=[
            VMEM((rows, owners * span, padded), jnp.bfloat16),
            VMEM((bases, all_rows + 2 * HALO, span, padded), jnp.float32),
            VMEM((owners, bases, depth, width), jnp.bfloat16),
            VMEM((all_rows, span, width), jnp.float32),
        ],
        compiler_params=pltpu.CompilerParams(vmem_limit_bytes=LIMIT),
        name="conv_mix",
    )(low, shift, place, *operands)


def finish_kernel(owners, place_ref, *refs):
    out_ref = refs[-1]
    late = out_ref.shape[0]
    for dl in range(late):
        mine = [ref for ref, owner in zip(refs, owners) if owner == dl]
        total = mine[0][...].astype(jnp.float32)
        for ref in mine[1:]:
            total += ref[...].astype(jnp.float32)
        value = total * (1.0 + lax.erf(total * (0.5**0.5))) * 0.5
        out_ref[partner_in_kernel(place_ref[0], dl, late)] = value.astype(jnp.bfloat16)


def finish(place, parts, owners):
    return pl.pallas_call(
        functools.partial(finish_kernel, owners),
        out_shape=jax.ShapeDtypeStruct((len(set(owners)),) + parts[0].shape, jnp.bfloat16),
        in_specs=[SMEM_SPEC] + [VMEM_SPEC] * len(parts),
        out_specs=VMEM_SPEC,
        compiler_params=pltpu.CompilerParams(vmem_limit_bytes=LIMIT),
        name="finish",
    )(place, *parts)


def turn_kernel(x_ref, out_ref):
    bases, rows, taps, slots, block, _ = x_ref.shape
    unit = (lax.broadcasted_iota(jnp.int32, (block, block), 0) == lax.broadcasted_iota(jnp.int32, (block, block), 1))
    unit = unit.astype(jnp.float32).astype(x_ref.dtype)

    def one_row(r, carry):
        for k in range(bases):
            for t in range(taps):
                cells = x_ref[k, r, t].reshape(slots * block, block)
                turned = lax.dot_general(unit, cells, (((1,), (1,)), ((), ())), preferred_element_type=jnp.float32)
                out_ref[r, k * taps + t] = turned.astype(out_ref.dtype)
        return carry

    lax.fori_loop(0, rows, one_row, 0)


def turn(x):
    bases, rows, taps, slots, block, _ = x.shape
    return pl.pallas_call(
        turn_kernel,
        out_shape=jax.ShapeDtypeStruct((rows, bases * taps, block, slots * block), x.dtype),
        in_specs=[VMEM_SPEC],
        out_specs=VMEM_SPEC,
        compiler_params=pltpu.CompilerParams(vmem_limit_bytes=LIMIT),
        name="turn",
    )(x)


def gather(spread, mix, kernels, late, owners):
    if owners != 4:
        return *([x] + [trade(x, "lonp", d, owners) for d in range(1, owners)] for x in (spread, mix)), kernels
    two = trade(mix, "lonp", 2, owners)
    one = trade(mix, "lonp", 1, owners)
    spread, two, one, *kernels = lax.optimization_barrier((spread, two, one, *kernels))
    fields = [trade(spread, "lonp", d, owners) for d in (3, 2, 1)] + [spread]
    return fields[::-1], [mix, one, two, trade(two, "lonp", 1, owners)], kernels


def send_rank(dl, dq):
    first = [(0, 0), (1, 0), (0, 1), (0, 3), (1, 3), (1, 1), (0, 2), (1, 2)]
    return first.index((dl, dq)) if (dl, dq) in first else len(first) + dl + dq


def per_device(sizes, fields, kernel, band_low, block_shift, mix_weight):
    halves, late, owners, groups = sizes
    members, rows, channels, cells = fields.shape
    block = kernel.shape[-1]
    all_rows = late * rows
    halo = HALO if halves > 1 else 0

    kernels = [kernel] + [trade(kernel, "late", s, late) for s in range(1, late)]
    packed = pack(fields.transpose(0, 1, 3, 2), groups, owners)
    packed = packed.reshape((late * groups,) + packed.shape[2:])
    spread = lax.all_to_all(packed, ("late", "lonq"), split_axis=0, concat_axis=0, tiled=True)
    spread = spread.reshape(late, groups * cells, -1)
    spread, mix, kernels = gather(spread, mix_weight, kernels, late, owners)
    weights = [turn(x) for x in kernels]

    start = lax.axis_index("lath") * all_rows
    low = lax.dynamic_slice_in_dim(band_low, start, all_rows, 1)
    shift = lax.dynamic_slice_in_dim(block_shift, start, all_rows, 0)
    place = [lax.axis_index("late"), lax.axis_index("lonp"), lax.axis_index("lonq")]
    place = jnp.stack(place).astype(jnp.int32)
    partial = conv_mix(low, shift, place, spread, weights, mix, halo, groups, block)
    if halo:
        *partial, beyond = partial
        below = lax.ppermute(beyond[1], "lath", [(i, i + 1) for i in range(halves - 1)])
        above = lax.ppermute(beyond[0], "lath", [(i + 1, i) for i in range(halves - 1)])
        filler = jnp.zeros((all_rows - 2 * halo,) + below.shape[1:], below.dtype)
        extra = jnp.concatenate([below, filler, above], axis=0).reshape(late, rows, groups, cells, -1)
        for dl in range(late):
            lat = partner(lax.axis_index("late"), dl, late)
            for dq in range(groups):
                group = partner(lax.axis_index("lonq"), dq, groups)
                partial[dl * groups + dq] += extra[lat, :, group]
    order = sorted(((dl, dq) for dl in range(late) for dq in range(groups)), key=lambda at: send_rank(*at))
    parts = []
    for dl, dq in order:
        route = [
            (l * groups + q, partner(l, dl, late) * groups + partner(q, dq, groups))
            for l in range(late)
            for q in range(groups)
        ]
        block = partial[dl * groups + dq]
        parts.append(lax.ppermute(block, ("late", "lonq"), route) if dl or dq else block)
    return finish(place, parts, [dl for dl, _ in order])


def solution(mesh):
    lat, lon = mesh.shape["lat"], mesh.shape["lon"]
    groups = max(g for g in range(1, lon + 1) if lon % g == 0 and g * g <= lon)

    def whole(fields, kernel, band_low, block_shift, mix_weight):
        late = fields.shape[0]
        sizes = (lat // late, late, lon // groups, groups)
        split = Mesh(mesh.devices.reshape(sizes), ("lath", "late", "lonp", "lonq"))
        rows, cells = ("lath", "late"), ("lonp", "lonq")
        return jax.shard_map(
            functools.partial(per_device, sizes),
            mesh=split,
            in_specs=(
                P(None, rows, None, cells),
                P(None, rows, None, None, None, None),
                P(),
                P(),
                P(None, cells, None),
            ),
            out_specs=P(None, rows, cells, None),
            check_vma=False,
        )(fields, kernel, band_low, block_shift, mix_weight)

    return whole
```

```python
import functools
import math

import jax
import jax.numpy as jnp
from jax import lax
from jax.experimental import pallas as pl
from jax.experimental.pallas import tpu as pltpu
from jax.sharding import Mesh
from jax.sharding import PartitionSpec as P

HALO = 2
LANES = 128
VMEM = pltpu.VMEM
LIMIT = 16 * 1024 * 1024
SMEM_SPEC = pl.BlockSpec(memory_space=pltpu.SMEM)
VMEM_SPEC = pl.BlockSpec(memory_space=VMEM)


def partner(index, distance, size):
    if size & (size - 1) == 0:
        return index ^ distance
    return (distance - index) % size


def partner_in_kernel(index, distance, size):
    if size & (size - 1) == 0:
        return lax.bitwise_xor(index, distance)
    return lax.rem(distance - index + size, size)


def trade(x, axis, distance, size):
    return lax.ppermute(x, axis, [(i, partner(i, distance, size)) for i in range(size)])


def pack_kernel(groups, owners, x_ref, out_ref):
    members, rows, cells, channels = x_ref.shape
    width = channels // (groups * owners)
    for e in range(members):
        for q in range(groups):
            parts = [
                x_ref[e, i, :, (p * groups + q) * width : (p * groups + q + 1) * width]
                for i in range(rows)
                for p in range(owners)
            ]
            out_ref[e, q] = jnp.concatenate(parts, axis=-1)


def pack(x, groups, owners):
    members, rows, cells, channels = x.shape
    return pl.pallas_call(
        functools.partial(pack_kernel, groups, owners),
        out_shape=jax.ShapeDtypeStruct((members, groups, cells, rows * channels // groups), x.dtype),
        in_specs=[VMEM_SPEC],
        out_specs=VMEM_SPEC,
        compiler_params=pltpu.CompilerParams(vmem_limit_bytes=LIMIT),
        name="pack",
    )(x)


def conv_mix_kernel(geometry, counts, low_ref, shift_ref, place_ref, *refs):
    bases, taps, slots, halo, sub, groups = geometry
    refs = list(refs)
    field_refs, weight_refs, mix_refs = [[refs.pop(0) for _ in range(n)] for n in counts]
    field_refs = field_refs[::-1]
    field_rows, total, mix_all, mixed = refs[-4:]
    outs = refs[:-4]
    late, span, _ = field_refs[0].shape
    owners = len(field_refs)
    depth, width = mix_refs[0].shape[1:]
    channels = owners * depth
    padded = total.shape[-1]
    rows, _, block, _ = weight_refs[0].shape
    nblocks = owners * span // block
    cells = span // groups
    member, owner, group = place_ref[0], place_ref[1], place_ref[2]

    total[...] = jnp.zeros_like(total)
    field_rows[...] = jnp.zeros_like(field_rows)
    for s in range(late):
        lat = partner_in_kernel(member, s, late)
        for d, ref in enumerate(field_refs):
            at = pl.ds(pl.multiple_of(partner_in_kernel(owner, d, owners) * span, sub), span)
            value = ref[lat]
            for r in range(rows):
                field_rows[r, at, :channels] = value[:, r * channels : (r + 1) * channels]

        def one_row(r, carry):
            row = lat * rows + r
            for piece in range(span // sub):
                cell = owner * span + piece * sub
                b = lax.div(cell, block)
                q = pl.multiple_of(lax.rem(cell, block), sub)
                chosen = []
                for j in range(slots):
                    source = lax.rem(b + shift_ref[row, j] + nblocks, nblocks)
                    chosen.append(field_rows[r, pl.ds(pl.multiple_of(source * block, block), block)])
                picked = jnp.concatenate(chosen, axis=0)
                lhs = weight_refs[s][r, :, pl.ds(q, sub), :].reshape(bases * taps * sub, slots * block)
                product = jnp.dot(lhs, picked, preferred_element_type=jnp.float32)
                for k in range(bases):
                    at = pl.ds(row + low_ref[k, row] + HALO, taps)
                    slab = product[k * taps * sub : (k + 1) * taps * sub].reshape(taps, sub, padded)
                    total[k, at, piece * sub : (piece + 1) * sub] += slab
            return carry

        lax.fori_loop(0, rows, one_row, 0, unroll=2)

    for d, ref in enumerate(mix_refs):
        mix_all[place_ref[3 + d]] = ref[...]
    fill = jnp.zeros((padded - channels, width), jnp.bfloat16)
    matrix = jnp.concatenate(
        [x for k in range(bases) for x in [mix_all[p, k] for p in range(owners)] + [fill]], axis=0
    )

    def one_out(first, count):
        at = pl.ds(first + HALO, count)
        lhs = [total[k, at].astype(jnp.bfloat16).reshape(count * span, padded) for k in range(bases)]
        product = jnp.dot(jnp.concatenate(lhs, axis=-1), matrix, preferred_element_type=jnp.float32)
        return product.reshape(count, span, width)

    for lat in range(late):
        mixed[lat * rows : (lat + 1) * rows] = one_out(lat * rows, rows)
    for dl in range(late):
        lat = partner_in_kernel(member, dl, late)
        for dq in range(groups):
            start = pl.multiple_of(partner_in_kernel(group, dq, groups) * cells, 8 if cells % 8 == 0 else cells)
            for r in range(rows):
                outs[dl * groups + dq][r] = mixed[lat * rows + r, pl.ds(start, cells)].astype(jnp.bfloat16)
    if halo:
        for side, first in enumerate((-halo, late * rows)):
            outs[-1][side] = one_out(first, halo).astype(jnp.bfloat16)


def conv_mix(low, shift, place, fields, weights, mix, halo, groups, block):
    bases, all_rows = low.shape
    slots = shift.shape[1]
    late, span, _ = fields[0].shape
    owners = len(fields)
    rows = all_rows // late
    depth, width = mix[0].shape[1:]
    padded = -(-owners * depth // LANES) * LANES
    taps = weights[0].shape[1] // bases
    sub = math.gcd(span, block)
    shapes = [jax.ShapeDtypeStruct((rows, span // groups, width), jnp.bfloat16)] * (late * groups)
    if halo:
        shapes.append(jax.ShapeDtypeStruct((2, halo, span, width), jnp.bfloat16))
    operands = fields[::-1] + weights + mix
    counts = (len(fields), len(weights), len(mix))
    return pl.pallas_call(
        functools.partial(conv_mix_kernel, (bases, taps, slots, halo, sub, groups), counts),
        out_shape=shapes,
        in_specs=[SMEM_SPEC] * 3 + [VMEM_SPEC] * len(operands),
        out_specs=[VMEM_SPEC] * len(shapes),
        scratch_shapes=[
            VMEM((rows, owners * span, padded), jnp.bfloat16),
            VMEM((bases, all_rows + 2 * HALO, span, padded), jnp.float32),
            VMEM((owners, bases, depth, width), jnp.bfloat16),
            VMEM((all_rows, span, width), jnp.float32),
        ],
        compiler_params=pltpu.CompilerParams(vmem_limit_bytes=LIMIT),
        name="conv_mix",
    )(low, shift, place, *operands)


def finish_kernel(owners, place_ref, *refs):
    out_ref = refs[-1]
    late = out_ref.shape[0]
    for dl in range(late):
        mine = [ref for ref, owner in zip(refs, owners) if owner == dl]
        total = mine[0][...].astype(jnp.float32)
        for ref in mine[1:]:
            total += ref[...].astype(jnp.float32)
        value = total * (1.0 + lax.erf(total * (0.5**0.5))) * 0.5
        out_ref[partner_in_kernel(place_ref[0], dl, late)] = value.astype(jnp.bfloat16)


def finish(place, parts, owners):
    return pl.pallas_call(
        functools.partial(finish_kernel, owners),
        out_shape=jax.ShapeDtypeStruct((len(set(owners)),) + parts[0].shape, jnp.bfloat16),
        in_specs=[SMEM_SPEC] + [VMEM_SPEC] * len(parts),
        out_specs=VMEM_SPEC,
        compiler_params=pltpu.CompilerParams(vmem_limit_bytes=LIMIT),
        name="finish",
    )(place, *parts)


def turn_kernel(x_ref, out_ref):
    bases, rows, taps, slots, block, _ = x_ref.shape
    unit = (lax.broadcasted_iota(jnp.int32, (block, block), 0) == lax.broadcasted_iota(jnp.int32, (block, block), 1))
    unit = unit.astype(jnp.float32).astype(x_ref.dtype)

    def one_row(r, carry):
        for k in range(bases):
            for t in range(taps):
                cells = x_ref[k, r, t].reshape(slots * block, block)
                turned = lax.dot_general(unit, cells, (((1,), (1,)), ((), ())), preferred_element_type=jnp.float32)
                out_ref[r, k * taps + t] = turned.astype(out_ref.dtype)
        return carry

    lax.fori_loop(0, rows, one_row, 0)


def turn(x):
    bases, rows, taps, slots, block, _ = x.shape
    return pl.pallas_call(
        turn_kernel,
        out_shape=jax.ShapeDtypeStruct((rows, bases * taps, block, slots * block), x.dtype),
        in_specs=[VMEM_SPEC],
        out_specs=VMEM_SPEC,
        compiler_params=pltpu.CompilerParams(vmem_limit_bytes=LIMIT),
        name="turn",
    )(x)


def gather(spread, mix, kernels, late, owners):
    core, own = lax.axis_index("late"), lax.axis_index("lonp")
    if owners != 4 or late != 2:
        fields, mixes = [[x] + [trade(x, "lonp", d, owners) for d in range(1, owners)] for x in (spread, mix)]
        return fields, mixes, [partner(own, d, owners) for d in range(owners)], kernels
    route = [(4 * c + p, 4 * c + (p ^ (3 - c))) for c in range(2) for p in range(4)]
    far = lax.ppermute(mix, ("late", "lonp"), route)
    near = trade(mix, "lonp", 1, owners)
    spread, far, near, *kernels = lax.optimization_barrier((spread, far, near, *kernels))
    fields = [trade(spread, "lonp", d, owners) for d in (3, 2, 1)] + [spread]
    mixes = [mix, near, far, trade(far, "late", 1, late)]
    return fields[::-1], mixes, [own, own ^ 1, own ^ (3 - core), own ^ (2 + core)], kernels


def send_rank(dl, dq):
    first = [(0, 0), (1, 0), (0, 1), (0, 2), (1, 1), (1, 2), (0, 3), (1, 3)]
    return first.index((dl, dq)) if (dl, dq) in first else len(first) + dl + dq


def per_device(sizes, fields, kernel, band_low, block_shift, mix_weight):
    halves, late, owners, groups = sizes
    members, rows, channels, cells = fields.shape
    block = kernel.shape[-1]
    all_rows = late * rows
    halo = HALO if halves > 1 else 0

    kernels = [kernel] + [trade(kernel, "late", s, late) for s in range(1, late)]
    packed = pack(fields.transpose(0, 1, 3, 2), groups, owners)
    packed = packed.reshape((late * groups,) + packed.shape[2:])
    spread = lax.all_to_all(packed, ("late", "lonq"), split_axis=0, concat_axis=0, tiled=True)
    spread = spread.reshape(late, groups * cells, -1)
    spread, mix, origins, kernels = gather(spread, mix_weight, kernels, late, owners)
    weights = [turn(x) for x in kernels]

    start = lax.axis_index("lath") * all_rows
    low = lax.dynamic_slice_in_dim(band_low, start, all_rows, 1)
    shift = lax.dynamic_slice_in_dim(block_shift, start, all_rows, 0)
    place = [lax.axis_index("late"), lax.axis_index("lonp"), lax.axis_index("lonq")] + origins
    place = jnp.stack(place).astype(jnp.int32)
    partial = conv_mix(low, shift, place, spread, weights, mix, halo, groups, block)
    if halo:
        *partial, beyond = partial
        below = lax.ppermute(beyond[1], "lath", [(i, i + 1) for i in range(halves - 1)])
        above = lax.ppermute(beyond[0], "lath", [(i + 1, i) for i in range(halves - 1)])
        filler = jnp.zeros((all_rows - 2 * halo,) + below.shape[1:], below.dtype)
        extra = jnp.concatenate([below, filler, above], axis=0).reshape(late, rows, groups, cells, -1)
        for dl in range(late):
            lat = partner(lax.axis_index("late"), dl, late)
            for dq in range(groups):
                group = partner(lax.axis_index("lonq"), dq, groups)
                partial[dl * groups + dq] += extra[lat, :, group]
    order = sorted(((dl, dq) for dl in range(late) for dq in range(groups)), key=lambda at: send_rank(*at))
    parts = []
    for dl, dq in order:
        route = [
            (l * groups + q, partner(l, dl, late) * groups + partner(q, dq, groups))
            for l in range(late)
            for q in range(groups)
        ]
        block = partial[dl * groups + dq]
        parts.append(lax.ppermute(block, ("late", "lonq"), route) if dl or dq else block)
    return finish(place, parts, [dl for dl, _ in order])


def solution(mesh):
    lat, lon = mesh.shape["lat"], mesh.shape["lon"]
    groups = max(g for g in range(1, lon + 1) if lon % g == 0 and g * g <= lon)

    def whole(fields, kernel, band_low, block_shift, mix_weight):
        late = fields.shape[0]
        sizes = (lat // late, late, lon // groups, groups)
        split = Mesh(mesh.devices.reshape(sizes), ("lath", "late", "lonp", "lonq"))
        rows, cells = ("lath", "late"), ("lonp", "lonq")
        return jax.shard_map(
            functools.partial(per_device, sizes),
            mesh=split,
            in_specs=(
                P(None, rows, None, cells),
                P(None, rows, None, None, None, None),
                P(),
                P(),
                P(None, cells, None),
            ),
            out_specs=P(None, rows, cells, None),
            check_vma=False,
        )(fields, kernel, band_low, block_shift, mix_weight)

    return whole
```

```python
import functools
import math

import jax
import jax.numpy as jnp
from jax import lax
from jax.experimental import pallas as pl
from jax.experimental.pallas import tpu as pltpu
from jax.sharding import Mesh
from jax.sharding import PartitionSpec as P

HALO = 2
LANES = 128
VMEM = pltpu.VMEM
LIMIT = 16 * 1024 * 1024
SMEM_SPEC = pl.BlockSpec(memory_space=pltpu.SMEM)
VMEM_SPEC = pl.BlockSpec(memory_space=VMEM)


def partner(index, distance, size):
    if size & (size - 1) == 0:
        return index ^ distance
    return (distance - index) % size


def partner_in_kernel(index, distance, size):
    if size & (size - 1) == 0:
        return lax.bitwise_xor(index, distance)
    return lax.rem(distance - index + size, size)


def trade(x, axis, distance, size):
    return lax.ppermute(x, axis, [(i, partner(i, distance, size)) for i in range(size)])


def pack_kernel(groups, owners, x_ref, out_ref):
    members, rows, cells, channels = x_ref.shape
    width = channels // (groups * owners)
    for e in range(members):
        for q in range(groups):
            parts = [
                x_ref[e, i, :, (p * groups + q) * width : (p * groups + q + 1) * width]
                for i in range(rows)
                for p in range(owners)
            ]
            out_ref[e, q] = jnp.concatenate(parts, axis=-1)


def pack(x, groups, owners):
    members, rows, cells, channels = x.shape
    return pl.pallas_call(
        functools.partial(pack_kernel, groups, owners),
        out_shape=jax.ShapeDtypeStruct((members, groups, cells, rows * channels // groups), x.dtype),
        in_specs=[VMEM_SPEC],
        out_specs=VMEM_SPEC,
        compiler_params=pltpu.CompilerParams(vmem_limit_bytes=LIMIT),
        name="pack",
    )(x)


def conv_mix_kernel(geometry, counts, low_ref, shift_ref, place_ref, *refs):
    bases, taps, slots, halo, sub, groups = geometry
    refs = list(refs)
    field_refs, weight_refs, mix_refs = [[refs.pop(0) for _ in range(n)] for n in counts]
    field_refs = field_refs[::-1]
    field_rows, total, mix_all, mixed = refs[-4:]
    outs = refs[:-4]
    late, span, _ = field_refs[0].shape
    owners = len(mix_refs)
    depth, width = mix_refs[0].shape[1:]
    channels = owners * depth
    padded = total.shape[-1]
    rows, _, block, _ = weight_refs[0].shape
    nblocks = owners * span // block
    cells = span // groups
    member, owner, group = place_ref[0], place_ref[1], place_ref[2]

    total[...] = jnp.zeros_like(total)
    field_rows[...] = jnp.zeros_like(field_rows)
    for s in range(late):
        lat = partner_in_kernel(member, s, late)
        for d in range(owners):
            at = pl.ds(pl.multiple_of(partner_in_kernel(owner, d, owners) * span, sub), span)
            value = field_refs[d][lat]
            if d == owners - 1 and len(field_refs) > owners:
                value = value + field_refs[owners][lat]
            for r in range(rows):
                field_rows[r, at, :channels] = value[:, r * channels : (r + 1) * channels]

        def one_row(r, carry):
            row = lat * rows + r
            for piece in range(span // sub):
                cell = owner * span + piece * sub
                b = lax.div(cell, block)
                q = pl.multiple_of(lax.rem(cell, block), sub)
                chosen = []
                for j in range(slots):
                    source = lax.rem(b + shift_ref[row, j] + nblocks, nblocks)
                    chosen.append(field_rows[r, pl.ds(pl.multiple_of(source * block, block), block)])
                picked = jnp.concatenate(chosen, axis=0)
                lhs = weight_refs[s][r, :, pl.ds(q, sub), :].reshape(bases * taps * sub, slots * block)
                product = jnp.dot(lhs, picked, preferred_element_type=jnp.float32)
                for k in range(bases):
                    at = pl.ds(row + low_ref[k, row] + HALO, taps)
                    slab = product[k * taps * sub : (k + 1) * taps * sub].reshape(taps, sub, padded)
                    total[k, at, piece * sub : (piece + 1) * sub] += slab
            return carry

        lax.fori_loop(0, rows, one_row, 0, unroll=2)

    for d, ref in enumerate(mix_refs):
        mix_all[place_ref[3 + d]] = ref[...]
    fill = jnp.zeros((padded - channels, width), jnp.bfloat16)
    matrix = jnp.concatenate(
        [x for k in range(bases) for x in [mix_all[p, k] for p in range(owners)] + [fill]], axis=0
    )

    def one_out(first, count):
        at = pl.ds(first + HALO, count)
        lhs = [total[k, at].astype(jnp.bfloat16).reshape(count * span, padded) for k in range(bases)]
        product = jnp.dot(jnp.concatenate(lhs, axis=-1), matrix, preferred_element_type=jnp.float32)
        return product.reshape(count, span, width)

    for lat in range(late):
        mixed[lat * rows : (lat + 1) * rows] = one_out(lat * rows, rows)
    for dl in range(late):
        lat = partner_in_kernel(member, dl, late)
        for dq in range(groups):
            start = pl.multiple_of(partner_in_kernel(group, dq, groups) * cells, 8 if cells % 8 == 0 else cells)
            for r in range(rows):
                outs[dl * groups + dq][r] = mixed[lat * rows + r, pl.ds(start, cells)].astype(jnp.bfloat16)
    if halo:
        for side, first in enumerate((-halo, late * rows)):
            outs[-1][side] = one_out(first, halo).astype(jnp.bfloat16)


def conv_mix(low, shift, place, fields, weights, mix, halo, groups, block):
    bases, all_rows = low.shape
    slots = shift.shape[1]
    late, span, _ = fields[0].shape
    owners = len(mix)
    rows = all_rows // late
    depth, width = mix[0].shape[1:]
    padded = -(-owners * depth // LANES) * LANES
    taps = weights[0].shape[1] // bases
    sub = math.gcd(span, block)
    shapes = [jax.ShapeDtypeStruct((rows, span // groups, width), jnp.bfloat16)] * (late * groups)
    if halo:
        shapes.append(jax.ShapeDtypeStruct((2, halo, span, width), jnp.bfloat16))
    operands = fields[::-1] + weights + mix
    counts = (len(fields), len(weights), len(mix))
    return pl.pallas_call(
        functools.partial(conv_mix_kernel, (bases, taps, slots, halo, sub, groups), counts),
        out_shape=shapes,
        in_specs=[SMEM_SPEC] * 3 + [VMEM_SPEC] * len(operands),
        out_specs=[VMEM_SPEC] * len(shapes),
        scratch_shapes=[
            VMEM((rows, owners * span, padded), jnp.bfloat16),
            VMEM((bases, all_rows + 2 * HALO, span, padded), jnp.float32),
            VMEM((owners, bases, depth, width), jnp.bfloat16),
            VMEM((all_rows, span, width), jnp.float32),
        ],
        compiler_params=pltpu.CompilerParams(vmem_limit_bytes=LIMIT),
        name="conv_mix",
    )(low, shift, place, *operands)


def finish_kernel(owners, place_ref, *refs):
    out_ref = refs[-1]
    late = out_ref.shape[0]
    for dl in range(late):
        mine = [ref for ref, owner in zip(refs, owners) if owner == dl]
        total = mine[0][...].astype(jnp.float32)
        for ref in mine[1:]:
            total += ref[...].astype(jnp.float32)
        value = total * (1.0 + lax.erf(total * (0.5**0.5))) * 0.5
        out_ref[partner_in_kernel(place_ref[0], dl, late)] = value.astype(jnp.bfloat16)


def finish(place, parts, owners):
    return pl.pallas_call(
        functools.partial(finish_kernel, owners),
        out_shape=jax.ShapeDtypeStruct((len(set(owners)),) + parts[0].shape, jnp.bfloat16),
        in_specs=[SMEM_SPEC] + [VMEM_SPEC] * len(parts),
        out_specs=VMEM_SPEC,
        compiler_params=pltpu.CompilerParams(vmem_limit_bytes=LIMIT),
        name="finish",
    )(place, *parts)


def turn_kernel(x_ref, out_ref):
    bases, rows, taps, slots, block, _ = x_ref.shape
    unit = (lax.broadcasted_iota(jnp.int32, (block, block), 0) == lax.broadcasted_iota(jnp.int32, (block, block), 1))
    unit = unit.astype(jnp.float32).astype(x_ref.dtype)

    def one_row(r, carry):
        for k in range(bases):
            for t in range(taps):
                cells = x_ref[k, r, t].reshape(slots * block, block)
                turned = lax.dot_general(unit, cells, (((1,), (1,)), ((), ())), preferred_element_type=jnp.float32)
                out_ref[r, k * taps + t] = turned.astype(out_ref.dtype)
        return carry

    lax.fori_loop(0, rows, one_row, 0)


def turn(x):
    bases, rows, taps, slots, block, _ = x.shape
    return pl.pallas_call(
        turn_kernel,
        out_shape=jax.ShapeDtypeStruct((rows, bases * taps, block, slots * block), x.dtype),
        in_specs=[VMEM_SPEC],
        out_specs=VMEM_SPEC,
        compiler_params=pltpu.CompilerParams(vmem_limit_bytes=LIMIT),
        name="turn",
    )(x)


def gather(spread, mix, kernels, late, owners):
    core, own = lax.axis_index("late"), lax.axis_index("lonp")
    if owners != 4 or late != 2:
        fields, mixes = [[x] + [trade(x, "lonp", d, owners) for d in range(1, owners)] for x in (spread, mix)]
        return fields, mixes, [partner(own, d, owners) for d in range(owners)], [turn(x) for x in kernels]
    route = [(4 * c + p, 4 * c + (p ^ (3 - c))) for c in range(2) for p in range(4)]
    far = lax.ppermute(mix, ("late", "lonp"), route)
    near = trade(mix, "lonp", 1, owners)
    spread, far, near, *kernels = lax.optimization_barrier((spread, far, near, *kernels))
    two, one, swapped = trade(spread, "lonp", 2, owners), trade(spread, "lonp", 1, owners), trade(far, "late", 1, late)
    weights = [turn(x) for x in kernels]
    middle, two, one, swapped, *weights = lax.optimization_barrier((spread, two, one, swapped, *weights))
    passed = lax.ppermute(two, "lonp", [(1, 0), (2, 3)])
    middle = lax.ppermute(middle, "lonp", [(1, 2), (2, 1)])
    origins = [own, own ^ 1, own ^ (3 - core), own ^ (2 + core)]
    return [spread, one, two, middle, passed], [mix, near, far, swapped], origins, weights


def send_rank(dl, dq):
    first = [(0, 0), (1, 0), (0, 1), (0, 2), (1, 1), (1, 2), (0, 3), (1, 3)]
    return first.index((dl, dq)) if (dl, dq) in first else len(first) + dl + dq


def per_device(sizes, fields, kernel, band_low, block_shift, mix_weight):
    halves, late, owners, groups = sizes
    members, rows, channels, cells = fields.shape
    block = kernel.shape[-1]
    all_rows = late * rows
    halo = HALO if halves > 1 else 0

    kernels = [kernel] + [trade(kernel, "late", s, late) for s in range(1, late)]
    packed = pack(fields.transpose(0, 1, 3, 2), groups, owners)
    packed = packed.reshape((late * groups,) + packed.shape[2:])
    spread = lax.all_to_all(packed, ("late", "lonq"), split_axis=0, concat_axis=0, tiled=True)
    spread = spread.reshape(late, groups * cells, -1)
    spread, mix, origins, weights = gather(spread, mix_weight, kernels, late, owners)

    start = lax.axis_index("lath") * all_rows
    low = lax.dynamic_slice_in_dim(band_low, start, all_rows, 1)
    shift = lax.dynamic_slice_in_dim(block_shift, start, all_rows, 0)
    place = [lax.axis_index("late"), lax.axis_index("lonp"), lax.axis_index("lonq")] + origins
    place = jnp.stack(place).astype(jnp.int32)
    partial = conv_mix(low, shift, place, spread, weights, mix, halo, groups, block)
    if halo:
        *partial, beyond = partial
        below = lax.ppermute(beyond[1], "lath", [(i, i + 1) for i in range(halves - 1)])
        above = lax.ppermute(beyond[0], "lath", [(i + 1, i) for i in range(halves - 1)])
        filler = jnp.zeros((all_rows - 2 * halo,) + below.shape[1:], below.dtype)
        extra = jnp.concatenate([below, filler, above], axis=0).reshape(late, rows, groups, cells, -1)
        for dl in range(late):
            lat = partner(lax.axis_index("late"), dl, late)
            for dq in range(groups):
                group = partner(lax.axis_index("lonq"), dq, groups)
                partial[dl * groups + dq] += extra[lat, :, group]
    order = sorted(((dl, dq) for dl in range(late) for dq in range(groups)), key=lambda at: send_rank(*at))
    parts = []
    for dl, dq in order:
        route = [
            (l * groups + q, partner(l, dl, late) * groups + partner(q, dq, groups))
            for l in range(late)
            for q in range(groups)
        ]
        block = partial[dl * groups + dq]
        parts.append(lax.ppermute(block, ("late", "lonq"), route) if dl or dq else block)
    return finish(place, parts, [dl for dl, _ in order])


def solution(mesh):
    lat, lon = mesh.shape["lat"], mesh.shape["lon"]
    groups = max(g for g in range(1, lon + 1) if lon % g == 0 and g * g <= lon)

    def whole(fields, kernel, band_low, block_shift, mix_weight):
        late = fields.shape[0]
        sizes = (lat // late, late, lon // groups, groups)
        split = Mesh(mesh.devices.reshape(sizes), ("lath", "late", "lonp", "lonq"))
        rows, cells = ("lath", "late"), ("lonp", "lonq")
        return jax.shard_map(
            functools.partial(per_device, sizes),
            mesh=split,
            in_specs=(
                P(None, rows, None, cells),
                P(None, rows, None, None, None, None),
                P(),
                P(),
                P(None, cells, None),
            ),
            out_specs=P(None, rows, cells, None),
            check_vma=False,
        )(fields, kernel, band_low, block_shift, mix_weight)

    return whole
```

```python
import functools
import math

import jax
import jax.numpy as jnp
from jax import lax
from jax.experimental import pallas as pl
from jax.experimental.pallas import tpu as pltpu
from jax.sharding import Mesh
from jax.sharding import PartitionSpec as P

HALO = 2
LANES = 128
VMEM = pltpu.VMEM
LIMIT = 16 * 1024 * 1024
SMEM_SPEC = pl.BlockSpec(memory_space=pltpu.SMEM)
VMEM_SPEC = pl.BlockSpec(memory_space=VMEM)


def partner(index, distance, size):
    if size & (size - 1) == 0:
        return index ^ distance
    return (distance - index) % size


def partner_in_kernel(index, distance, size):
    if size & (size - 1) == 0:
        return lax.bitwise_xor(index, distance)
    return lax.rem(distance - index + size, size)


def trade(x, axis, distance, size):
    return lax.ppermute(x, axis, [(i, partner(i, distance, size)) for i in range(size)])


def pack_kernel(groups, owners, x_ref, out_ref):
    members, rows, cells, channels = x_ref.shape
    width = channels // (groups * owners)
    for e in range(members):
        for q in range(groups):
            parts = [
                x_ref[e, i, :, (p * groups + q) * width : (p * groups + q + 1) * width]
                for i in range(rows)
                for p in range(owners)
            ]
            out_ref[e, q] = jnp.concatenate(parts, axis=-1)


def pack(x, groups, owners):
    members, rows, cells, channels = x.shape
    return pl.pallas_call(
        functools.partial(pack_kernel, groups, owners),
        out_shape=jax.ShapeDtypeStruct((members, groups, cells, rows * channels // groups), x.dtype),
        in_specs=[VMEM_SPEC],
        out_specs=VMEM_SPEC,
        compiler_params=pltpu.CompilerParams(vmem_limit_bytes=LIMIT),
        name="pack",
    )(x)


def conv_mix_kernel(geometry, counts, low_ref, shift_ref, place_ref, *refs):
    bases, taps, slots, halo, sub, groups = geometry
    refs = list(refs)
    field_refs, weight_refs, mix_refs = [[refs.pop(0) for _ in range(n)] for n in counts]
    field_refs = field_refs[::-1]
    field_rows, total, mix_all, mixed = refs[-4:]
    outs = refs[:-4]
    late, span, _ = field_refs[0].shape
    owners = len(field_refs)
    depth, width = mix_refs[0].shape[1:]
    channels = owners * depth
    padded = total.shape[-1]
    rows, _, block, _ = weight_refs[0].shape
    nblocks = owners * span // block
    cells = span // groups
    member, owner, group = place_ref[0], place_ref[1], place_ref[2]

    read = pl.ds(HALO - halo, late * rows + 2 * halo)
    total[:, read] = jnp.zeros((bases, late * rows + 2 * halo) + total.shape[2:], total.dtype)
    upper = pl.ds(padded - LANES, LANES)
    field_rows[:, :, upper] = jnp.zeros(field_rows.shape[:2] + (LANES,), field_rows.dtype)
    for s in range(late):
        lat = partner_in_kernel(member, s, late)
        for d, ref in enumerate(field_refs):
            at = pl.ds(pl.multiple_of(partner_in_kernel(owner, d, owners) * span, sub), span)
            value = ref[lat]
            for r in range(rows):
                field_rows[r, at, :channels] = value[:, r * channels : (r + 1) * channels]

        def one_row(r, carry):
            row = lat * rows + r
            for piece in range(span // sub):
                cell = owner * span + piece * sub
                b = lax.div(cell, block)
                q = pl.multiple_of(lax.rem(cell, block), sub)
                chosen = []
                for j in range(slots):
                    source = lax.rem(b + shift_ref[row, j] + nblocks, nblocks)
                    chosen.append(field_rows[r, pl.ds(pl.multiple_of(source * block, block), block)])
                picked = jnp.concatenate(chosen, axis=0)
                lhs = weight_refs[s][r, :, pl.ds(q, sub), :].reshape(bases * taps * sub, slots * block)
                product = jnp.dot(lhs, picked, preferred_element_type=jnp.float32)
                for k in range(bases):
                    at = pl.ds(row + low_ref[k, row] + HALO, taps)
                    slab = product[k * taps * sub : (k + 1) * taps * sub].reshape(taps, sub, padded)
                    total[k, at, piece * sub : (piece + 1) * sub] += slab
            return carry

        lax.fori_loop(0, rows, one_row, 0, unroll=2)

    for d, ref in enumerate(mix_refs):
        mix_all[place_ref[3 + d]] = ref[...]
    fill = jnp.zeros((padded - channels, width), jnp.bfloat16)
    matrix = jnp.concatenate(
        [x for k in range(bases) for x in [mix_all[p, k] for p in range(owners)] + [fill]], axis=0
    )

    def one_out(first, count):
        at = pl.ds(first + HALO, count)
        lhs = [total[k, at].astype(jnp.bfloat16).reshape(count * span, padded) for k in range(bases)]
        product = jnp.dot(jnp.concatenate(lhs, axis=-1), matrix, preferred_element_type=jnp.float32)
        return product.reshape(count, span, width)

    mixed[...] = one_out(0, late * rows)
    for dl in range(late):
        lat = partner_in_kernel(member, dl, late)
        for dq in range(groups):
            start = pl.multiple_of(partner_in_kernel(group, dq, groups) * cells, 8 if cells % 8 == 0 else cells)
            for r in range(rows):
                outs[dl * groups + dq][r] = mixed[lat * rows + r, pl.ds(start, cells)].astype(jnp.bfloat16)
    if halo:
        for side, first in enumerate((-halo, late * rows)):
            outs[-1][side] = one_out(first, halo).astype(jnp.bfloat16)


def conv_mix(low, shift, place, fields, weights, mix, halo, groups, block):
    bases, all_rows = low.shape
    slots = shift.shape[1]
    late, span, _ = fields[0].shape
    owners = len(fields)
    rows = all_rows // late
    depth, width = mix[0].shape[1:]
    padded = -(-owners * depth // LANES) * LANES
    taps = weights[0].shape[1] // bases
    sub = math.gcd(span, block)
    shapes = [jax.ShapeDtypeStruct((rows, span // groups, width), jnp.bfloat16)] * (late * groups)
    if halo:
        shapes.append(jax.ShapeDtypeStruct((2, halo, span, width), jnp.bfloat16))
    operands = fields[::-1] + weights + mix
    counts = (len(fields), len(weights), len(mix))
    return pl.pallas_call(
        functools.partial(conv_mix_kernel, (bases, taps, slots, halo, sub, groups), counts),
        out_shape=shapes,
        in_specs=[SMEM_SPEC] * 3 + [VMEM_SPEC] * len(operands),
        out_specs=[VMEM_SPEC] * len(shapes),
        scratch_shapes=[
            VMEM((rows, owners * span, padded), jnp.bfloat16),
            VMEM((bases, all_rows + 2 * HALO, span, padded), jnp.float32),
            VMEM((owners, bases, depth, width), jnp.bfloat16),
            VMEM((all_rows, span, width), jnp.float32),
        ],
        compiler_params=pltpu.CompilerParams(vmem_limit_bytes=LIMIT),
        name="conv_mix",
    )(low, shift, place, *operands)


def finish_kernel(owners, place_ref, *refs):
    out_ref = refs[-1]
    late = out_ref.shape[0]
    for dl in range(late):
        mine = [ref for ref, owner in zip(refs, owners) if owner == dl]
        total = mine[0][...].astype(jnp.float32)
        for ref in mine[1:]:
            total += ref[...].astype(jnp.float32)
        value = total * (1.0 + lax.erf(total * (0.5**0.5))) * 0.5
        out_ref[partner_in_kernel(place_ref[0], dl, late)] = value.astype(jnp.bfloat16)


def finish(place, parts, owners):
    return pl.pallas_call(
        functools.partial(finish_kernel, owners),
        out_shape=jax.ShapeDtypeStruct((len(set(owners)),) + parts[0].shape, jnp.bfloat16),
        in_specs=[SMEM_SPEC] + [VMEM_SPEC] * len(parts),
        out_specs=VMEM_SPEC,
        compiler_params=pltpu.CompilerParams(vmem_limit_bytes=LIMIT),
        name="finish",
    )(place, *parts)


def turn_kernel(x_ref, out_ref):
    bases, rows, taps, slots, block, _ = x_ref.shape
    unit = (lax.broadcasted_iota(jnp.int32, (block, block), 0) == lax.broadcasted_iota(jnp.int32, (block, block), 1))
    unit = unit.astype(jnp.float32).astype(x_ref.dtype)

    def one_row(r, carry):
        for k in range(bases):
            for t in range(taps):
                cells = x_ref[k, r, t].reshape(slots * block, block)
                turned = lax.dot_general(unit, cells, (((1,), (1,)), ((), ())), preferred_element_type=jnp.float32)
                out_ref[r, k * taps + t] = turned.astype(out_ref.dtype)
        return carry

    lax.fori_loop(0, rows, one_row, 0)


def turn(x):
    bases, rows, taps, slots, block, _ = x.shape
    return pl.pallas_call(
        turn_kernel,
        out_shape=jax.ShapeDtypeStruct((rows, bases * taps, block, slots * block), x.dtype),
        in_specs=[VMEM_SPEC],
        out_specs=VMEM_SPEC,
        compiler_params=pltpu.CompilerParams(vmem_limit_bytes=LIMIT),
        name="turn",
    )(x)


def gather(spread, mix, kernels, late, owners):
    core, own = lax.axis_index("late"), lax.axis_index("lonp")
    if owners != 4 or late != 2:
        fields, mixes = [[x] + [trade(x, "lonp", d, owners) for d in range(1, owners)] for x in (spread, mix)]
        return fields, mixes, [partner(own, d, owners) for d in range(owners)], kernels
    route = [(4 * c + p, 4 * c + (p ^ (3 - c))) for c in range(2) for p in range(4)]
    far = lax.ppermute(mix, ("late", "lonp"), route)
    near = trade(mix, "lonp", 1, owners)
    spread, far, near, *kernels = lax.optimization_barrier((spread, far, near, *kernels))
    fields = [trade(spread, "lonp", d, owners) for d in (3, 2, 1)] + [spread]
    mixes = [mix, near, far, trade(far, "late", 1, late)]
    return fields[::-1], mixes, [own, own ^ 1, own ^ (3 - core), own ^ (2 + core)], kernels


def per_device(sizes, fields, kernel, band_low, block_shift, mix_weight):
    halves, late, owners, groups = sizes
    members, rows, channels, cells = fields.shape
    block = kernel.shape[-1]
    all_rows = late * rows
    halo = HALO if halves > 1 else 0

    kernels = [kernel] + [trade(kernel, "late", s, late) for s in range(1, late)]
    packed = pack(fields.transpose(0, 1, 3, 2), groups, owners)
    packed = packed.reshape((late * groups,) + packed.shape[2:])
    spread = lax.all_to_all(packed, ("late", "lonq"), split_axis=0, concat_axis=0, tiled=True)
    spread = spread.reshape(late, groups * cells, -1)
    spread, mix, origins, kernels = gather(spread, mix_weight, kernels, late, owners)
    weights = [turn(x) for x in kernels]

    start = lax.axis_index("lath") * all_rows
    low = lax.dynamic_slice_in_dim(band_low, start, all_rows, 1)
    shift = lax.dynamic_slice_in_dim(block_shift, start, all_rows, 0)
    place = [lax.axis_index("late"), lax.axis_index("lonp"), lax.axis_index("lonq")] + origins
    place = jnp.stack(place).astype(jnp.int32)
    partial = conv_mix(low, shift, place, spread, weights, mix, halo, groups, block)
    if halo:
        *partial, beyond = partial
        below = lax.ppermute(beyond[1], "lath", [(i, i + 1) for i in range(halves - 1)])
        above = lax.ppermute(beyond[0], "lath", [(i + 1, i) for i in range(halves - 1)])
        filler = jnp.zeros((all_rows - 2 * halo,) + below.shape[1:], below.dtype)
        extra = jnp.concatenate([below, filler, above], axis=0).reshape(late, rows, groups, cells, -1)
        for dl in range(late):
            lat = partner(lax.axis_index("late"), dl, late)
            for dq in range(groups):
                group = partner(lax.axis_index("lonq"), dq, groups)
                partial[dl * groups + dq] += extra[lat, :, group]
    order = [(dl, dq) for dl in range(late) for dq in range(groups)]
    parts = []
    for dl, dq in order:
        route = [
            (l * groups + q, partner(l, dl, late) * groups + partner(q, dq, groups))
            for l in range(late)
            for q in range(groups)
        ]
        block = partial[dl * groups + dq]
        parts.append(lax.ppermute(block, ("late", "lonq"), route) if dl or dq else block)
    return finish(place, parts, [dl for dl, _ in order])


def solution(mesh):
    lat, lon = mesh.shape["lat"], mesh.shape["lon"]
    groups = max(g for g in range(1, lon + 1) if lon % g == 0 and g * g <= lon)

    def whole(fields, kernel, band_low, block_shift, mix_weight):
        late = fields.shape[0]
        sizes = (lat // late, late, lon // groups, groups)
        split = Mesh(mesh.devices.reshape(sizes), ("lath", "late", "lonp", "lonq"))
        rows, cells = ("lath", "late"), ("lonp", "lonq")
        return jax.shard_map(
            functools.partial(per_device, sizes),
            mesh=split,
            in_specs=(
                P(None, rows, None, cells),
                P(None, rows, None, None, None, None),
                P(),
                P(),
                P(None, cells, None),
            ),
            out_specs=P(None, rows, cells, None),
            check_vma=False,
        )(fields, kernel, band_low, block_shift, mix_weight)

    return whole
```

```python
import functools
import math

import jax
import jax.numpy as jnp
from jax import lax
from jax.experimental import pallas as pl
from jax.experimental.pallas import tpu as pltpu
from jax.sharding import Mesh
from jax.sharding import PartitionSpec as P

HALO = 2
LANES = 128
VMEM = pltpu.VMEM
LIMIT = 16 * 1024 * 1024
SMEM_SPEC = pl.BlockSpec(memory_space=pltpu.SMEM)
VMEM_SPEC = pl.BlockSpec(memory_space=VMEM)


def partner(index, distance, size):
    if size & (size - 1) == 0:
        return index ^ distance
    return (distance - index) % size


def partner_in_kernel(index, distance, size):
    if size & (size - 1) == 0:
        return lax.bitwise_xor(index, distance)
    return lax.rem(distance - index + size, size)


def trade(x, axis, distance, size):
    return lax.ppermute(x, axis, [(i, partner(i, distance, size)) for i in range(size)])


def pack_kernel(groups, owners, x_ref, out_ref):
    members, rows, cells, channels = x_ref.shape
    width = channels // (groups * owners)
    for e in range(members):
        for q in range(groups):
            parts = [
                x_ref[e, i, :, (p * groups + q) * width : (p * groups + q + 1) * width]
                for i in range(rows)
                for p in range(owners)
            ]
            block = jnp.concatenate(parts, axis=-1)
            for p in range(owners):
                out_ref[e, p, q] = block


def pack(x, groups, owners):
    members, rows, cells, channels = x.shape
    return pl.pallas_call(
        functools.partial(pack_kernel, groups, owners),
        out_shape=jax.ShapeDtypeStruct((members, owners, groups, cells, rows * channels // groups), x.dtype),
        in_specs=[VMEM_SPEC],
        out_specs=VMEM_SPEC,
        compiler_params=pltpu.CompilerParams(vmem_limit_bytes=LIMIT),
        name="pack",
    )(x)


def conv_mix_kernel(geometry, counts, low_ref, shift_ref, place_ref, fields_ref, *refs):
    bases, taps, slots, halo, sub, groups = geometry
    refs = list(refs)
    weight_refs, mix_refs = [[refs.pop(0) for _ in range(n)] for n in counts]
    field_rows, total, mix_all, mixed = refs[-4:]
    outs = refs[:-4]
    late, owners, span, _ = fields_ref.shape
    depth, width = mix_refs[0].shape[1:]
    channels = owners * depth
    padded = total.shape[-1]
    rows, _, block, _ = weight_refs[0].shape
    nblocks = owners * span // block
    member, owner, group = place_ref[0], place_ref[1], place_ref[2]

    read = pl.ds(HALO - halo, late * rows + 2 * halo)
    total[:, read] = jnp.zeros((bases, late * rows + 2 * halo) + total.shape[2:], total.dtype)
    upper = pl.ds(padded - LANES, LANES)
    field_rows[:, :, upper] = jnp.zeros(field_rows.shape[:2] + (LANES,), field_rows.dtype)
    for s in range(late):
        lat = partner_in_kernel(member, s, late)
        for p in range(owners):
            value = fields_ref[lat, p]
            for r in range(rows):
                field_rows[r, p * span : (p + 1) * span, :channels] = value[:, r * channels : (r + 1) * channels]

        def one_row(r, carry):
            row = lat * rows + r
            for piece in range(span // sub):
                cell = owner * span + piece * sub
                b = lax.div(cell, block)
                q = pl.multiple_of(lax.rem(cell, block), sub)
                chosen = []
                for j in range(slots):
                    source = lax.rem(b + shift_ref[row, j] + nblocks, nblocks)
                    chosen.append(field_rows[r, pl.ds(pl.multiple_of(source * block, block), block)])
                picked = jnp.concatenate(chosen, axis=0)
                lhs = weight_refs[s][r, :, pl.ds(q, sub), :].reshape(bases * taps * sub, slots * block)
                product = jnp.dot(lhs, picked, preferred_element_type=jnp.float32)
                for k in range(bases):
                    at = pl.ds(row + low_ref[k, row] + HALO, taps)
                    slab = product[k * taps * sub : (k + 1) * taps * sub].reshape(taps, sub, padded)
                    total[k, at, piece * sub : (piece + 1) * sub] += slab
            return carry

        lax.fori_loop(0, rows, one_row, 0, unroll=2)

    for d in range(owners):
        value = mix_refs[d][...]
        if d == owners - 1 and len(mix_refs) > owners:
            value = value + mix_refs[owners][...]
        mix_all[place_ref[3 + d]] = value
    fill = jnp.zeros((padded - channels, width), jnp.bfloat16)
    matrix = jnp.concatenate(
        [x for k in range(bases) for x in [mix_all[p, k] for p in range(owners)] + [fill]], axis=0
    )
    own_ref, matrix_ref = outs[:2]
    matrix_ref[...] = matrix

    def rounded(first, count):
        at = pl.ds(first + HALO, count)
        return jnp.concatenate([total[k, at].astype(jnp.bfloat16) for k in range(bases)], axis=-1)

    own_ref[...] = rounded(member * rows, rows)
    for dl in range(1, late):
        first = partner_in_kernel(member, dl, late) * rows
        mix_into(mixed, outs[2 + (dl - 1) * groups :], rounded(first, rows), matrix, group, groups)
    if halo:
        for side, first in enumerate((-halo, late * rows)):
            lhs = rounded(first, halo).reshape(halo * span, -1)
            product = jnp.dot(lhs, matrix, preferred_element_type=jnp.float32)
            outs[-1][side] = product.reshape(halo, span, width).astype(jnp.bfloat16)


def mix_into(mixed, outs, rounded, matrix, group, groups):
    rows, span, lanes = rounded.shape
    cells = span // groups
    product = jnp.dot(rounded.reshape(rows * span, lanes), matrix, preferred_element_type=jnp.float32)
    mixed[...] = product.reshape(mixed.shape)
    for dq in range(groups):
        start = pl.multiple_of(partner_in_kernel(group, dq, groups) * cells, 8 if cells % 8 == 0 else cells)
        for r in range(rows):
            outs[dq][r] = mixed[r, pl.ds(start, cells)].astype(jnp.bfloat16)


def mix_own_kernel(groups, place_ref, rounded_ref, matrix_ref, *refs):
    mix_into(refs[-1], refs[:-1], rounded_ref[...], matrix_ref[...], place_ref[2], groups)


def mix_own(place, rounded, matrix, groups):
    rows, span, _ = rounded.shape
    width = matrix.shape[-1]
    return pl.pallas_call(
        functools.partial(mix_own_kernel, groups),
        out_shape=[jax.ShapeDtypeStruct((rows, span // groups, width), jnp.bfloat16)] * groups,
        in_specs=[SMEM_SPEC] + [VMEM_SPEC] * 2,
        out_specs=[VMEM_SPEC] * groups,
        scratch_shapes=[VMEM((rows, span, width), jnp.float32)],
        compiler_params=pltpu.CompilerParams(vmem_limit_bytes=LIMIT),
        name="mix_own",
    )(place, rounded, matrix)


def conv_mix(low, shift, place, fields, weights, mix, halo, groups, block):
    bases, all_rows = low.shape
    slots = shift.shape[1]
    late, owners, span, _ = fields.shape
    rows = all_rows // late
    depth, width = mix[0].shape[1:]
    padded = -(-owners * depth // LANES) * LANES
    taps = weights[0].shape[1] // bases
    sub = math.gcd(span, block)
    shapes = [
        jax.ShapeDtypeStruct((rows, span, bases * padded), jnp.bfloat16),
        jax.ShapeDtypeStruct((bases * padded, width), jnp.bfloat16),
    ]
    shapes += [jax.ShapeDtypeStruct((rows, span // groups, width), jnp.bfloat16)] * ((late - 1) * groups)
    if halo:
        shapes.append(jax.ShapeDtypeStruct((2, halo, span, width), jnp.bfloat16))
    operands = [fields] + weights + mix
    counts = (len(weights), len(mix))
    return pl.pallas_call(
        functools.partial(conv_mix_kernel, (bases, taps, slots, halo, sub, groups), counts),
        out_shape=shapes,
        in_specs=[SMEM_SPEC] * 3 + [VMEM_SPEC] * len(operands),
        out_specs=[VMEM_SPEC] * len(shapes),
        scratch_shapes=[
            VMEM((rows, owners * span, padded), jnp.bfloat16),
            VMEM((bases, all_rows + 2 * HALO, span, padded), jnp.float32),
            VMEM((owners, bases, depth, width), jnp.bfloat16),
            VMEM((rows, span, width), jnp.float32),
        ],
        compiler_params=pltpu.CompilerParams(vmem_limit_bytes=LIMIT),
        name="conv_mix",
    )(low, shift, place, *operands)


def finish_kernel(owners, place_ref, *refs):
    out_ref = refs[-1]
    late = out_ref.shape[0]
    for dl in range(late):
        mine = [ref for ref, owner in zip(refs, owners) if owner == dl]
        total = mine[0][...].astype(jnp.float32)
        for ref in mine[1:]:
            total += ref[...].astype(jnp.float32)
        value = total * (1.0 + lax.erf(total * (0.5**0.5))) * 0.5
        out_ref[partner_in_kernel(place_ref[0], dl, late)] = value.astype(jnp.bfloat16)


def finish(place, parts, owners):
    return pl.pallas_call(
        functools.partial(finish_kernel, owners),
        out_shape=jax.ShapeDtypeStruct((len(set(owners)),) + parts[0].shape, jnp.bfloat16),
        in_specs=[SMEM_SPEC] + [VMEM_SPEC] * len(parts),
        out_specs=VMEM_SPEC,
        compiler_params=pltpu.CompilerParams(vmem_limit_bytes=LIMIT),
        name="finish",
    )(place, *parts)


def turn_kernel(x_ref, out_ref):
    bases, rows, taps, slots, block, _ = x_ref.shape
    unit = (lax.broadcasted_iota(jnp.int32, (block, block), 0) == lax.broadcasted_iota(jnp.int32, (block, block), 1))
    unit = unit.astype(jnp.float32).astype(x_ref.dtype)

    def one_row(r, carry):
        for k in range(bases):
            for t in range(taps):
                cells = x_ref[k, r, t].reshape(slots * block, block)
                turned = lax.dot_general(unit, cells, (((1,), (1,)), ((), ())), preferred_element_type=jnp.float32)
                out_ref[r, k * taps + t] = turned.astype(out_ref.dtype)
        return carry

    lax.fori_loop(0, rows, one_row, 0)


def turn(x):
    bases, rows, taps, slots, block, _ = x.shape
    return pl.pallas_call(
        turn_kernel,
        out_shape=jax.ShapeDtypeStruct((rows, bases * taps, block, slots * block), x.dtype),
        in_specs=[VMEM_SPEC],
        out_specs=VMEM_SPEC,
        compiler_params=pltpu.CompilerParams(vmem_limit_bytes=LIMIT),
        name="turn",
    )(x)


def gather_mix(mix, packed, late, owners):
    core, own = lax.axis_index("late"), lax.axis_index("lonp")
    if owners != 4 or late != 2:
        mixes = [mix] + [trade(mix, "lonp", d, owners) for d in range(1, owners)]
        return mixes, [partner(own, d, owners) for d in range(owners)], packed
    route = [(4 * c + p, 4 * c + (p ^ (1 + c))) for c in range(2) for p in range(4)]
    first = lax.ppermute(mix, ("late", "lonp"), route)
    packed, first = lax.optimization_barrier((packed, first))
    third = lax.ppermute(first, ("late", "lonp"), [(4 + p, 4 + (p ^ 1)) for p in range(4)])
    other = trade(first, "late", 1, late)
    copied = lax.ppermute(third, "late", [(1, 0)])
    return [mix, first, other, third, copied], [own, own ^ (1 + core), own ^ (2 - core), own ^ 3], packed


def per_device(sizes, fields, kernel, band_low, block_shift, mix_weight):
    halves, late, owners, groups = sizes
    members, rows, channels, cells = fields.shape
    block = kernel.shape[-1]
    all_rows = late * rows
    halo = HALO if halves > 1 else 0

    kernels = [kernel] + [trade(kernel, "late", s, late) for s in range(1, late)]
    packed = pack(fields.transpose(0, 1, 3, 2), groups, owners)
    packed = packed.reshape((-1,) + packed.shape[3:])
    mix, origins, packed = gather_mix(mix_weight, packed, late, owners)
    spread = lax.all_to_all(packed, ("late", "lonp", "lonq"), split_axis=0, concat_axis=0, tiled=True)
    spread = spread.reshape(late, owners, groups * cells, -1)
    weights = [turn(x) for x in kernels]

    start = lax.axis_index("lath") * all_rows
    low = lax.dynamic_slice_in_dim(band_low, start, all_rows, 1)
    shift = lax.dynamic_slice_in_dim(block_shift, start, all_rows, 0)
    place = [lax.axis_index("late"), lax.axis_index("lonp"), lax.axis_index("lonq")] + origins
    place = jnp.stack(place).astype(jnp.int32)
    rounded, matrix, *partial = conv_mix(low, shift, place, spread, weights, mix, halo, groups, block)
    partial = list(mix_own(place, rounded, matrix, groups)) + partial
    if halo:
        *partial, beyond = partial
        below = lax.ppermute(beyond[1], "lath", [(i, i + 1) for i in range(halves - 1)])
        above = lax.ppermute(beyond[0], "lath", [(i + 1, i) for i in range(halves - 1)])
        filler = jnp.zeros((all_rows - 2 * halo,) + below.shape[1:], below.dtype)
        extra = jnp.concatenate([below, filler, above], axis=0).reshape(late, rows, groups, cells, -1)
        for dl in range(late):
            lat = partner(lax.axis_index("late"), dl, late)
            for dq in range(groups):
                group = partner(lax.axis_index("lonq"), dq, groups)
                partial[dl * groups + dq] += extra[lat, :, group]
    order = [(dl, dq) for dl in reversed(range(late)) for dq in range(groups)]
    parts = []
    for dl, dq in order:
        route = [
            (l * groups + q, partner(l, dl, late) * groups + partner(q, dq, groups))
            for l in range(late)
            for q in range(groups)
        ]
        block = partial[dl * groups + dq]
        parts.append(lax.ppermute(block, ("late", "lonq"), route) if dl or dq else block)
    return finish(place, parts, [dl for dl, _ in order])


def solution(mesh):
    lat, lon = mesh.shape["lat"], mesh.shape["lon"]
    groups = max(g for g in range(1, lon + 1) if lon % g == 0 and g * g <= lon)

    def whole(fields, kernel, band_low, block_shift, mix_weight):
        late = fields.shape[0]
        sizes = (lat // late, late, lon // groups, groups)
        split = Mesh(mesh.devices.reshape(sizes), ("lath", "late", "lonp", "lonq"))
        rows, cells = ("lath", "late"), ("lonp", "lonq")
        return jax.shard_map(
            functools.partial(per_device, sizes),
            mesh=split,
            in_specs=(
                P(None, rows, None, cells),
                P(None, rows, None, None, None, None),
                P(),
                P(),
                P(None, cells, None),
            ),
            out_specs=P(None, rows, cells, None),
            check_vma=False,
        )(fields, kernel, band_low, block_shift, mix_weight)

    return whole
```

```python
import functools
import math

import jax
import jax.numpy as jnp
from jax import lax
from jax.experimental import pallas as pl
from jax.experimental.pallas import tpu as pltpu
from jax.sharding import Mesh
from jax.sharding import PartitionSpec as P

HALO = 2
LANES = 128
VMEM = pltpu.VMEM
LIMIT = 16 * 1024 * 1024
SMEM_SPEC = pl.BlockSpec(memory_space=pltpu.SMEM)
VMEM_SPEC = pl.BlockSpec(memory_space=VMEM)


def partner(index, distance, size):
    if size & (size - 1) == 0:
        return index ^ distance
    return (distance - index) % size


def partner_in_kernel(index, distance, size):
    if size & (size - 1) == 0:
        return lax.bitwise_xor(index, distance)
    return lax.rem(distance - index + size, size)


def trade(x, axis, distance, size):
    return lax.ppermute(x, axis, [(i, partner(i, distance, size)) for i in range(size)])


def pack_kernel(groups, owners, x_ref, out_ref):
    members, rows, cells, channels = x_ref.shape
    width = channels // (groups * owners)
    for e in range(members):
        for q in range(groups):
            parts = [
                x_ref[e, i, :, (p * groups + q) * width : (p * groups + q + 1) * width]
                for i in range(rows)
                for p in range(owners)
            ]
            block = jnp.concatenate(parts, axis=-1)
            for p in range(owners):
                out_ref[e, p, q] = block


def pack(x, groups, owners):
    members, rows, cells, channels = x.shape
    return pl.pallas_call(
        functools.partial(pack_kernel, groups, owners),
        out_shape=jax.ShapeDtypeStruct((members, owners, groups, cells, rows * channels // groups), x.dtype),
        in_specs=[VMEM_SPEC],
        out_specs=VMEM_SPEC,
        compiler_params=pltpu.CompilerParams(vmem_limit_bytes=LIMIT),
        name="pack",
    )(x)


def added(refs, *at):
    value = refs[0][at]
    for ref in refs[1:]:
        value = value + ref[at]
    return value


def conv_mix_kernel(geometry, counts, low_ref, shift_ref, place_ref, *refs):
    bases, taps, slots, halo, sub, groups = geometry
    refs = list(refs)
    fields_ref = refs.pop(0)
    weight_refs = [refs.pop(0) for _ in range(counts[0])]
    mix_slots = [[refs.pop(0) for _ in range(n)] for n in counts[1]]
    field_rows, total, mix_all, mixed = refs[-4:]
    outs = refs[:-4]
    late, owners, span, _ = fields_ref.shape
    depth, width = mix_slots[0][0].shape[1:]
    channels = owners * depth
    padded = total.shape[-1]
    rows, _, block, _ = weight_refs[0].shape
    nblocks = owners * span // block
    cells = span // groups
    member, owner, group = place_ref[0], place_ref[1], place_ref[2]

    read = pl.ds(HALO - halo, late * rows + 2 * halo)
    total[:, read] = jnp.zeros((bases, late * rows + 2 * halo) + total.shape[2:], total.dtype)
    upper = pl.ds(padded - LANES, LANES)
    field_rows[:, :, upper] = jnp.zeros(field_rows.shape[:2] + (LANES,), field_rows.dtype)
    for s in range(late):
        lat = partner_in_kernel(member, s, late)
        for p in range(owners):
            value = fields_ref[lat, p]
            for r in range(rows):
                field_rows[r, p * span : (p + 1) * span, :channels] = value[:, r * channels : (r + 1) * channels]

        def one_row(r, carry):
            row = lat * rows + r
            for piece in range(span // sub):
                cell = owner * span + piece * sub
                b = lax.div(cell, block)
                q = pl.multiple_of(lax.rem(cell, block), sub)
                chosen = []
                for j in range(slots):
                    source = lax.rem(b + shift_ref[row, j] + nblocks, nblocks)
                    chosen.append(field_rows[r, pl.ds(pl.multiple_of(source * block, block), block)])
                picked = jnp.concatenate(chosen, axis=0)
                lhs = weight_refs[s][r, :, pl.ds(q, sub), :].reshape(bases * taps * sub, slots * block)
                product = jnp.dot(lhs, picked, preferred_element_type=jnp.float32)
                for k in range(bases):
                    at = pl.ds(row + low_ref[k, row] + HALO, taps)
                    slab = product[k * taps * sub : (k + 1) * taps * sub].reshape(taps, sub, padded)
                    total[k, at, piece * sub : (piece + 1) * sub] += slab
            return carry

        lax.fori_loop(0, rows, one_row, 0, unroll=2)

    for d, slot in enumerate(mix_slots):
        for k in range(bases):
            mix_all[place_ref[3 + d], k] = added(slot, k)
    fill = jnp.zeros((padded - channels, width), jnp.bfloat16)
    matrix = jnp.concatenate(
        [x for k in range(bases) for x in [mix_all[p, k] for p in range(owners)] + [fill]], axis=0
    )

    def one_out(first, count):
        at = pl.ds(first + HALO, count)
        lhs = [total[k, at].astype(jnp.bfloat16).reshape(count * span, padded) for k in range(bases)]
        product = jnp.dot(jnp.concatenate(lhs, axis=-1), matrix, preferred_element_type=jnp.float32)
        return product.reshape(count, span, width)

    mixed[...] = one_out(0, late * rows)
    for dl in range(late):
        lat = partner_in_kernel(member, dl, late)
        for dq in range(groups):
            start = pl.multiple_of(partner_in_kernel(group, dq, groups) * cells, 8 if cells % 8 == 0 else cells)
            for r in range(rows):
                outs[dl * groups + dq][r] = mixed[lat * rows + r, pl.ds(start, cells)].astype(jnp.bfloat16)
    if halo:
        for side, first in enumerate((-halo, late * rows)):
            outs[-1][side] = one_out(first, halo).astype(jnp.bfloat16)


def conv_mix(low, shift, place, fields, weights, mix, halo, groups, block):
    bases, all_rows = low.shape
    slots = shift.shape[1]
    late, owners, span, _ = fields.shape
    rows = all_rows // late
    depth, width = mix[0][0].shape[1:]
    padded = -(-owners * depth // LANES) * LANES
    taps = weights[0].shape[1] // bases
    sub = math.gcd(span, block)
    shapes = [jax.ShapeDtypeStruct((rows, span // groups, width), jnp.bfloat16)] * (late * groups)
    if halo:
        shapes.append(jax.ShapeDtypeStruct((2, halo, span, width), jnp.bfloat16))
    operands = [fields] + weights + [x for slot in mix for x in slot]
    counts = (len(weights), [len(s) for s in mix])
    return pl.pallas_call(
        functools.partial(conv_mix_kernel, (bases, taps, slots, halo, sub, groups), counts),
        out_shape=shapes,
        in_specs=[SMEM_SPEC] * 3 + [VMEM_SPEC] * len(operands),
        out_specs=[VMEM_SPEC] * len(shapes),
        scratch_shapes=[
            VMEM((rows, owners * span, padded), jnp.bfloat16),
            VMEM((bases, all_rows + 2 * HALO, span, padded), jnp.float32),
            VMEM((owners, bases, depth, width), jnp.bfloat16),
            VMEM((all_rows, span, width), jnp.float32),
        ],
        compiler_params=pltpu.CompilerParams(vmem_limit_bytes=LIMIT),
        name="conv_mix",
    )(low, shift, place, *operands)


def finish_kernel(groups, place_ref, *refs):
    out_ref = refs[-1]
    late = out_ref.shape[0]
    for dl in range(late):
        total = refs[dl * groups][...].astype(jnp.float32)
        for dq in range(1, groups):
            total += refs[dl * groups + dq][...].astype(jnp.float32)
        value = total * (1.0 + lax.erf(total * (0.5**0.5))) * 0.5
        out_ref[partner_in_kernel(place_ref[0], dl, late)] = value.astype(jnp.bfloat16)


def finish(place, parts, groups):
    return pl.pallas_call(
        functools.partial(finish_kernel, groups),
        out_shape=jax.ShapeDtypeStruct((len(parts) // groups,) + parts[0].shape, jnp.bfloat16),
        in_specs=[SMEM_SPEC] + [VMEM_SPEC] * len(parts),
        out_specs=VMEM_SPEC,
        compiler_params=pltpu.CompilerParams(vmem_limit_bytes=LIMIT),
        name="finish",
    )(place, *parts)


def both_kernels(kernel, late):
    bases, rows, taps, slots, block, _ = kernel.shape
    own = kernel.transpose(1, 0, 2, 5, 3, 4).reshape(rows, bases * taps, block, slots * block)
    return [own] + [trade(own, "late", s, late) for s in range(1, late)]


def gather_mix(mix, packed, late, owners):
    core, own = lax.axis_index("late"), lax.axis_index("lonp")
    if owners == 4 and late == 2:
        route = [(p, p ^ 1) for p in range(4)] + [(4 + p, 4 + (p ^ 2)) for p in range(4)]
        first = lax.ppermute(mix, ("late", "lonp"), route)
        packed, first = lax.optimization_barrier((packed, first))
        third = lax.ppermute(first, ("late", "lonp"), [(4 + p, 4 + (p ^ 1)) for p in range(4)])
        other = trade(first, "late", 1, late)
        copied = lax.ppermute(third, "late", [(1, 0)])
        slots, origins = [[mix], [first], [other], [third, copied]], [own, own ^ (1 + core), own ^ (2 - core), own ^ 3]
        return slots, origins, packed
    slots = [[mix]] + [[trade(mix, "lonp", d, owners)] for d in range(1, owners)]
    return slots, [partner(own, d, owners) for d in range(owners)], packed


def per_device(sizes, fields, kernel, band_low, block_shift, mix_weight):
    halves, late, owners, groups = sizes
    members, rows, channels, cells = fields.shape
    bases, _, taps, slots, block, _ = kernel.shape
    all_rows = late * rows
    halo = HALO if halves > 1 else 0

    packed = pack(fields.transpose(0, 1, 3, 2), groups, owners)
    packed = packed.reshape((-1,) + packed.shape[3:])
    mix, origins, packed = gather_mix(mix_weight, packed, late, owners)
    spread = lax.all_to_all(packed, ("late", "lonp", "lonq"), split_axis=0, concat_axis=0, tiled=True)
    spread = spread.reshape(late, owners, groups * cells, -1)
    weights = both_kernels(kernel, late)

    start = lax.axis_index("lath") * all_rows
    low = lax.dynamic_slice_in_dim(band_low, start, all_rows, 1)
    shift = lax.dynamic_slice_in_dim(block_shift, start, all_rows, 0)
    place = [lax.axis_index("late"), lax.axis_index("lonp"), lax.axis_index("lonq")] + origins
    place = jnp.stack(place).astype(jnp.int32)
    partial = conv_mix(low, shift, place, spread, weights, mix, halo, groups, block)
    if halo:
        *partial, beyond = partial
        below = lax.ppermute(beyond[1], "lath", [(i, i + 1) for i in range(halves - 1)])
        above = lax.ppermute(beyond[0], "lath", [(i + 1, i) for i in range(halves - 1)])
        filler = jnp.zeros((all_rows - 2 * halo,) + below.shape[1:], below.dtype)
        extra = jnp.concatenate([below, filler, above], axis=0).reshape(late, rows, groups, cells, -1)
        for dl in range(late):
            lat = partner(lax.axis_index("late"), dl, late)
            for dq in range(groups):
                group = partner(lax.axis_index("lonq"), dq, groups)
                partial[dl * groups + dq] += extra[lat, :, group]
    parts = [
        lax.ppermute(
            partial[dl * groups + dq],
            ("late", "lonq"),
            [
                (l * groups + q, partner(l, dl, late) * groups + partner(q, dq, groups))
                for l in range(late)
                for q in range(groups)
            ],
        )
        if dl or dq
        else partial[0]
        for dl in range(late)
        for dq in range(groups)
    ]
    return finish(place, parts, groups)


def solution(mesh):
    lat, lon = mesh.shape["lat"], mesh.shape["lon"]
    groups = max(g for g in range(1, lon + 1) if lon % g == 0 and g * g <= lon)

    def whole(fields, kernel, band_low, block_shift, mix_weight):
        late = fields.shape[0]
        sizes = (lat // late, late, lon // groups, groups)
        split = Mesh(mesh.devices.reshape(sizes), ("lath", "late", "lonp", "lonq"))
        rows, cells = ("lath", "late"), ("lonp", "lonq")
        return jax.shard_map(
            functools.partial(per_device, sizes),
            mesh=split,
            in_specs=(
                P(None, rows, None, cells),
                P(None, rows, None, None, None, None),
                P(),
                P(),
                P(None, cells, None),
            ),
            out_specs=P(None, rows, cells, None),
            check_vma=False,
        )(fields, kernel, band_low, block_shift, mix_weight)

    return whole
```

```python
import functools
import math

import jax
import jax.numpy as jnp
from jax import lax
from jax.experimental import pallas as pl
from jax.experimental.pallas import tpu as pltpu
from jax.sharding import Mesh
from jax.sharding import PartitionSpec as P

HALO = 2
LANES = 128
VMEM = pltpu.VMEM
LIMIT = 16 * 1024 * 1024
SMEM_SPEC = pl.BlockSpec(memory_space=pltpu.SMEM)
VMEM_SPEC = pl.BlockSpec(memory_space=VMEM)


def partner(index, distance, size):
    if size & (size - 1) == 0:
        return index ^ distance
    return (distance - index) % size


def partner_in_kernel(index, distance, size):
    if size & (size - 1) == 0:
        return lax.bitwise_xor(index, distance)
    return lax.rem(distance - index + size, size)


def trade(x, axis, distance, size):
    return lax.ppermute(x, axis, [(i, partner(i, distance, size)) for i in range(size)])


def pack_kernel(groups, owners, x_ref, out_ref):
    members, rows, cells, channels = x_ref.shape
    width = channels // (groups * owners)
    for e in range(members):
        for q in range(groups):
            parts = [
                x_ref[e, i, :, (p * groups + q) * width : (p * groups + q + 1) * width]
                for i in range(rows)
                for p in range(owners)
            ]
            block = jnp.concatenate(parts, axis=-1)
            for p in range(owners):
                out_ref[e, p, q] = block


def pack(x, groups, owners):
    members, rows, cells, channels = x.shape
    return pl.pallas_call(
        functools.partial(pack_kernel, groups, owners),
        out_shape=jax.ShapeDtypeStruct((members, owners, groups, cells, rows * channels // groups), x.dtype),
        in_specs=[VMEM_SPEC],
        out_specs=VMEM_SPEC,
        compiler_params=pltpu.CompilerParams(vmem_limit_bytes=LIMIT),
        name="pack",
    )(x)


def added(refs, *at):
    value = refs[0][at]
    for ref in refs[1:]:
        value = value + ref[at]
    return value


def conv_mix_kernel(geometry, counts, low_ref, shift_ref, place_ref, *refs):
    bases, taps, slots, halo, sub, groups = geometry
    refs = list(refs)
    fields_ref = refs.pop(0)
    weight_refs = [refs.pop(0) for _ in range(counts[0])]
    mix_slots = [[refs.pop(0) for _ in range(n)] for n in counts[1]]
    field_rows, total, mix_all, mixed = refs[-4:]
    outs = refs[:-4]
    late, owners, span, _ = fields_ref.shape
    depth, width = mix_slots[0][0].shape[1:]
    channels = owners * depth
    padded = total.shape[-1]
    rows, _, block, _ = weight_refs[0].shape
    nblocks = owners * span // block
    cells = span // groups
    member, owner, group = place_ref[0], place_ref[1], place_ref[2]

    read = pl.ds(HALO - halo, late * rows + 2 * halo)
    total[:, read] = jnp.zeros((bases, late * rows + 2 * halo) + total.shape[2:], total.dtype)
    upper = pl.ds(padded - LANES, LANES)
    field_rows[:, :, upper] = jnp.zeros(field_rows.shape[:2] + (LANES,), field_rows.dtype)
    for s in range(late):
        lat = partner_in_kernel(member, s, late)
        for p in range(owners):
            value = fields_ref[lat, p]
            for r in range(rows):
                field_rows[r, p * span : (p + 1) * span, :channels] = value[:, r * channels : (r + 1) * channels]

        def one_row(r, carry):
            row = lat * rows + r
            for piece in range(span // sub):
                cell = owner * span + piece * sub
                b = lax.div(cell, block)
                q = pl.multiple_of(lax.rem(cell, block), sub)
                chosen = []
                for j in range(slots):
                    source = lax.rem(b + shift_ref[row, j] + nblocks, nblocks)
                    chosen.append(field_rows[r, pl.ds(pl.multiple_of(source * block, block), block)])
                picked = jnp.concatenate(chosen, axis=0)
                lhs = weight_refs[s][r, :, pl.ds(q, sub), :].reshape(bases * taps * sub, slots * block)
                product = jnp.dot(lhs, picked, preferred_element_type=jnp.float32)
                for k in range(bases):
                    at = pl.ds(row + low_ref[k, row] + HALO, taps)
                    slab = product[k * taps * sub : (k + 1) * taps * sub].reshape(taps, sub, padded)
                    total[k, at, piece * sub : (piece + 1) * sub] += slab
            return carry

        lax.fori_loop(0, rows, one_row, 0, unroll=2)

    for d, slot in enumerate(mix_slots):
        for k in range(bases):
            mix_all[place_ref[3 + d], k] = added(slot, k)
    fill = jnp.zeros((padded - channels, width), jnp.bfloat16)
    matrix = jnp.concatenate(
        [x for k in range(bases) for x in [mix_all[p, k] for p in range(owners)] + [fill]], axis=0
    )

    def one_out(first, count):
        at = pl.ds(first + HALO, count)
        lhs = [total[k, at].astype(jnp.bfloat16).reshape(count * span, padded) for k in range(bases)]
        product = jnp.dot(jnp.concatenate(lhs, axis=-1), matrix, preferred_element_type=jnp.float32)
        return product.reshape(count, span, width)

    mixed[...] = one_out(0, late * rows)
    for dl in range(late):
        lat = partner_in_kernel(member, dl, late)
        for dq in range(groups):
            start = pl.multiple_of(partner_in_kernel(group, dq, groups) * cells, 8 if cells % 8 == 0 else cells)
            for r in range(rows):
                outs[dl * groups + dq][r] = mixed[lat * rows + r, pl.ds(start, cells)].astype(jnp.bfloat16)
    if halo:
        for side, first in enumerate((-halo, late * rows)):
            outs[-1][side] = one_out(first, halo).astype(jnp.bfloat16)


def conv_mix(low, shift, place, fields, weights, mix, halo, groups, block):
    bases, all_rows = low.shape
    slots = shift.shape[1]
    late, owners, span, _ = fields.shape
    rows = all_rows // late
    depth, width = mix[0][0].shape[1:]
    padded = -(-owners * depth // LANES) * LANES
    taps = weights[0].shape[1] // bases
    sub = math.gcd(span, block)
    shapes = [jax.ShapeDtypeStruct((rows, span // groups, width), jnp.bfloat16)] * (late * groups)
    if halo:
        shapes.append(jax.ShapeDtypeStruct((2, halo, span, width), jnp.bfloat16))
    operands = [fields] + weights + [x for slot in mix for x in slot]
    counts = (len(weights), [len(s) for s in mix])
    return pl.pallas_call(
        functools.partial(conv_mix_kernel, (bases, taps, slots, halo, sub, groups), counts),
        out_shape=shapes,
        in_specs=[SMEM_SPEC] * 3 + [VMEM_SPEC] * len(operands),
        out_specs=[VMEM_SPEC] * len(shapes),
        scratch_shapes=[
            VMEM((rows, owners * span, padded), jnp.bfloat16),
            VMEM((bases, all_rows + 2 * HALO, span, padded), jnp.float32),
            VMEM((owners, bases, depth, width), jnp.bfloat16),
            VMEM((all_rows, span, width), jnp.float32),
        ],
        compiler_params=pltpu.CompilerParams(vmem_limit_bytes=LIMIT),
        name="conv_mix",
    )(low, shift, place, *operands)


def finish_kernel(owners, place_ref, *refs):
    out_ref = refs[-1]
    late = out_ref.shape[0]
    for dl in range(late):
        mine = [ref for ref, owner in zip(refs, owners) if owner == dl]
        total = mine[0][...].astype(jnp.float32)
        for ref in mine[1:]:
            total += ref[...].astype(jnp.float32)
        value = total * (1.0 + lax.erf(total * (0.5**0.5))) * 0.5
        out_ref[partner_in_kernel(place_ref[0], dl, late)] = value.astype(jnp.bfloat16)


def finish(place, parts, owners):
    return pl.pallas_call(
        functools.partial(finish_kernel, owners),
        out_shape=jax.ShapeDtypeStruct((len(set(owners)),) + parts[0].shape, jnp.bfloat16),
        in_specs=[SMEM_SPEC] + [VMEM_SPEC] * len(parts),
        out_specs=VMEM_SPEC,
        compiler_params=pltpu.CompilerParams(vmem_limit_bytes=LIMIT),
        name="finish",
    )(place, *parts)


def both_kernels(kernel, late):
    bases, rows, taps, slots, block, _ = kernel.shape
    own = kernel.transpose(1, 0, 2, 5, 3, 4).reshape(rows, bases * taps, block, slots * block)
    return [own] + [trade(own, "late", s, late) for s in range(1, late)]


def gather_mix(mix, packed, late, owners):
    core, own = lax.axis_index("late"), lax.axis_index("lonp")
    if owners == 4 and late == 2:
        route = [(p, p ^ 1) for p in range(4)] + [(4 + p, 4 + (p ^ 2)) for p in range(4)]
        first = lax.ppermute(mix, ("late", "lonp"), route)
        packed, first = lax.optimization_barrier((packed, first))
        third = lax.ppermute(first, ("late", "lonp"), [(4 + p, 4 + (p ^ 1)) for p in range(4)])
        other = trade(first, "late", 1, late)
        copied = lax.ppermute(third, "late", [(1, 0)])
        slots, origins = [[mix], [first], [other], [third, copied]], [own, own ^ (1 + core), own ^ (2 - core), own ^ 3]
        return slots, origins, packed
    slots = [[mix]] + [[trade(mix, "lonp", d, owners)] for d in range(1, owners)]
    return slots, [partner(own, d, owners) for d in range(owners)], packed


def per_device(sizes, fields, kernel, band_low, block_shift, mix_weight):
    halves, late, owners, groups = sizes
    members, rows, channels, cells = fields.shape
    bases, _, taps, slots, block, _ = kernel.shape
    all_rows = late * rows
    halo = HALO if halves > 1 else 0

    packed = pack(fields.transpose(0, 1, 3, 2), groups, owners)
    packed = packed.reshape((-1,) + packed.shape[3:])
    mix, origins, packed = gather_mix(mix_weight, packed, late, owners)
    spread = lax.all_to_all(packed, ("late", "lonp", "lonq"), split_axis=0, concat_axis=0, tiled=True)
    spread = spread.reshape(late, owners, groups * cells, -1)
    weights = both_kernels(kernel, late)

    start = lax.axis_index("lath") * all_rows
    low = lax.dynamic_slice_in_dim(band_low, start, all_rows, 1)
    shift = lax.dynamic_slice_in_dim(block_shift, start, all_rows, 0)
    place = [lax.axis_index("late"), lax.axis_index("lonp"), lax.axis_index("lonq")] + origins
    place = jnp.stack(place).astype(jnp.int32)
    partial = conv_mix(low, shift, place, spread, weights, mix, halo, groups, block)
    if halo:
        *partial, beyond = partial
        below = lax.ppermute(beyond[1], "lath", [(i, i + 1) for i in range(halves - 1)])
        above = lax.ppermute(beyond[0], "lath", [(i + 1, i) for i in range(halves - 1)])
        filler = jnp.zeros((all_rows - 2 * halo,) + below.shape[1:], below.dtype)
        extra = jnp.concatenate([below, filler, above], axis=0).reshape(late, rows, groups, cells, -1)
        for dl in range(late):
            lat = partner(lax.axis_index("late"), dl, late)
            for dq in range(groups):
                group = partner(lax.axis_index("lonq"), dq, groups)
                partial[dl * groups + dq] += extra[lat, :, group]
    order = [(dl, dq) for dl in range(late) for dq in range(groups)]
    order.sort(key=lambda at: (at[1] == 0, bin(at[1]).count("1"), at))
    parts = []
    for dl, dq in order:
        route = [
            (l * groups + q, partner(l, dl, late) * groups + partner(q, dq, groups))
            for l in range(late)
            for q in range(groups)
        ]
        block = partial[dl * groups + dq]
        parts.append(lax.ppermute(block, ("late", "lonq"), route) if dl or dq else block)
    return finish(place, parts, [dl for dl, _ in order])


def solution(mesh):
    lat, lon = mesh.shape["lat"], mesh.shape["lon"]
    groups = max(g for g in range(1, lon + 1) if lon % g == 0 and g * g <= lon)

    def whole(fields, kernel, band_low, block_shift, mix_weight):
        late = fields.shape[0]
        sizes = (lat // late, late, lon // groups, groups)
        split = Mesh(mesh.devices.reshape(sizes), ("lath", "late", "lonp", "lonq"))
        rows, cells = ("lath", "late"), ("lonp", "lonq")
        return jax.shard_map(
            functools.partial(per_device, sizes),
            mesh=split,
            in_specs=(
                P(None, rows, None, cells),
                P(None, rows, None, None, None, None),
                P(),
                P(),
                P(None, cells, None),
            ),
            out_specs=P(None, rows, cells, None),
            check_vma=False,
        )(fields, kernel, band_low, block_shift, mix_weight)

    return whole
```

```python
import functools
import math

import jax
import jax.numpy as jnp
from jax import lax
from jax.experimental import pallas as pl
from jax.experimental.pallas import tpu as pltpu
from jax.sharding import Mesh
from jax.sharding import PartitionSpec as P

HALO = 2
LANES = 128
VMEM = pltpu.VMEM
LIMIT = 16 * 1024 * 1024
SMEM_SPEC = pl.BlockSpec(memory_space=pltpu.SMEM)
VMEM_SPEC = pl.BlockSpec(memory_space=VMEM)


def partner(index, distance, size):
    if size & (size - 1) == 0:
        return index ^ distance
    return (distance - index) % size


def partner_in_kernel(index, distance, size):
    if size & (size - 1) == 0:
        return lax.bitwise_xor(index, distance)
    return lax.rem(distance - index + size, size)


def trade(x, axis, distance, size):
    return lax.ppermute(x, axis, [(i, partner(i, distance, size)) for i in range(size)])


def pack_kernel(groups, owners, x_ref, out_ref):
    members, rows, cells, channels = x_ref.shape
    width = channels // (groups * owners)
    for e in range(members):
        for q in range(groups):
            parts = [
                x_ref[e, i, :, (p * groups + q) * width : (p * groups + q + 1) * width]
                for i in range(rows)
                for p in range(owners)
            ]
            block = jnp.concatenate(parts, axis=-1)
            for p in range(owners):
                out_ref[e, p, q] = block


def pack(x, groups, owners):
    members, rows, cells, channels = x.shape
    return pl.pallas_call(
        functools.partial(pack_kernel, groups, owners),
        out_shape=jax.ShapeDtypeStruct((members, owners, groups, cells, rows * channels // groups), x.dtype),
        in_specs=[VMEM_SPEC],
        out_specs=VMEM_SPEC,
        compiler_params=pltpu.CompilerParams(vmem_limit_bytes=LIMIT),
        name="pack",
    )(x)


def added(refs, *at):
    value = refs[0][at]
    for ref in refs[1:]:
        value = value + ref[at]
    return value


def conv_mix_kernel(geometry, counts, low_ref, shift_ref, place_ref, *refs):
    bases, taps, slots, halo, sub, groups = geometry
    refs = list(refs)
    fields_ref = refs.pop(0)
    weight_refs = [refs.pop(0) for _ in range(counts[0])]
    mix_slots = [[refs.pop(0) for _ in range(n)] for n in counts[1]]
    field_rows, total, mix_all, mixed, partner_rows, arrived = refs[-6:]
    outs = refs[:-6]
    late, owners, span, _ = fields_ref.shape
    depth, width = mix_slots[0][0].shape[1:]
    channels = owners * depth
    padded = total.shape[-1]
    rows, _, block, _ = weight_refs[0].shape
    nblocks = owners * span // block
    cells = span // groups
    member, owner, group = place_ref[0], place_ref[1], place_ref[2]

    copies = [pltpu.make_async_copy(weight_refs[s], partner_rows.at[s - 1], arrived.at[s - 1]) for s in range(1, late)]
    for copy in copies:
        copy.start()
    read = pl.ds(HALO - halo, late * rows + 2 * halo)
    total[:, read] = jnp.zeros((bases, late * rows + 2 * halo) + total.shape[2:], total.dtype)
    upper = pl.ds(padded - LANES, LANES)
    field_rows[:, :, upper] = jnp.zeros(field_rows.shape[:2] + (LANES,), field_rows.dtype)
    for s in range(late):
        lat = partner_in_kernel(member, s, late)
        if s:
            copies[s - 1].wait()
        kernel_rows = partner_rows.at[s - 1] if s else weight_refs[0]
        for p in range(owners):
            value = fields_ref[lat, p]
            for r in range(rows):
                field_rows[r, p * span : (p + 1) * span, :channels] = value[:, r * channels : (r + 1) * channels]

        def one_row(r, carry):
            row = lat * rows + r
            for piece in range(span // sub):
                cell = owner * span + piece * sub
                b = lax.div(cell, block)
                q = pl.multiple_of(lax.rem(cell, block), sub)
                chosen = []
                for j in range(slots):
                    source = lax.rem(b + shift_ref[row, j] + nblocks, nblocks)
                    chosen.append(field_rows[r, pl.ds(pl.multiple_of(source * block, block), block)])
                picked = jnp.concatenate(chosen, axis=0)
                lhs = kernel_rows[r, :, pl.ds(q, sub), :].reshape(bases * taps * sub, slots * block)
                product = jnp.dot(lhs, picked, preferred_element_type=jnp.float32)
                for k in range(bases):
                    at = pl.ds(row + low_ref[k, row] + HALO, taps)
                    slab = product[k * taps * sub : (k + 1) * taps * sub].reshape(taps, sub, padded)
                    total[k, at, piece * sub : (piece + 1) * sub] += slab
            return carry

        lax.fori_loop(0, rows, one_row, 0, unroll=2)

    for d, slot in enumerate(mix_slots):
        for k in range(bases):
            mix_all[place_ref[3 + d], k] = added(slot, k)
    fill = jnp.zeros((padded - channels, width), jnp.bfloat16)
    matrix = jnp.concatenate(
        [x for k in range(bases) for x in [mix_all[p, k] for p in range(owners)] + [fill]], axis=0
    )

    def one_out(first, count):
        at = pl.ds(first + HALO, count)
        lhs = [total[k, at].astype(jnp.bfloat16).reshape(count * span, padded) for k in range(bases)]
        product = jnp.dot(jnp.concatenate(lhs, axis=-1), matrix, preferred_element_type=jnp.float32)
        return product.reshape(count, span, width)

    mixed[...] = one_out(0, late * rows)
    for dl in range(late):
        lat = partner_in_kernel(member, dl, late)
        for dq in range(groups):
            start = pl.multiple_of(partner_in_kernel(group, dq, groups) * cells, 8 if cells % 8 == 0 else cells)
            for r in range(rows):
                outs[dl * groups + dq][r] = mixed[lat * rows + r, pl.ds(start, cells)].astype(jnp.bfloat16)
    if halo:
        for side, first in enumerate((-halo, late * rows)):
            outs[-1][side] = one_out(first, halo).astype(jnp.bfloat16)


def conv_mix(low, shift, place, fields, weights, mix, halo, groups, block):
    bases, all_rows = low.shape
    slots = shift.shape[1]
    late, owners, span, _ = fields.shape
    rows = all_rows // late
    depth, width = mix[0][0].shape[1:]
    padded = -(-owners * depth // LANES) * LANES
    taps = weights[0].shape[1] // bases
    sub = math.gcd(span, block)
    shapes = [jax.ShapeDtypeStruct((rows, span // groups, width), jnp.bfloat16)] * (late * groups)
    if halo:
        shapes.append(jax.ShapeDtypeStruct((2, halo, span, width), jnp.bfloat16))
    operands = [fields] + weights + [x for slot in mix for x in slot]
    counts = (len(weights), [len(s) for s in mix])
    return pl.pallas_call(
        functools.partial(conv_mix_kernel, (bases, taps, slots, halo, sub, groups), counts),
        out_shape=shapes,
        in_specs=[SMEM_SPEC] * 3
        + [VMEM_SPEC] * 2
        + [pl.BlockSpec(memory_space=pl.ANY)] * (late - 1)
        + [VMEM_SPEC] * (len(operands) - 1 - late),
        out_specs=[VMEM_SPEC] * len(shapes),
        scratch_shapes=[
            VMEM((rows, owners * span, padded), jnp.bfloat16),
            VMEM((bases, all_rows + 2 * HALO, span, padded), jnp.float32),
            VMEM((owners, bases, depth, width), jnp.bfloat16),
            VMEM((all_rows, span, width), jnp.float32),
            VMEM((max(late - 1, 1),) + weights[0].shape, jnp.bfloat16),
            pltpu.SemaphoreType.DMA((max(late - 1, 1),)),
        ],
        compiler_params=pltpu.CompilerParams(vmem_limit_bytes=LIMIT),
        name="conv_mix",
    )(low, shift, place, *operands)


def finish_kernel(owners, place_ref, *refs):
    out_ref = refs[-1]
    late = out_ref.shape[0]
    for dl in range(late):
        mine = [ref for ref, owner in zip(refs, owners) if owner == dl]
        total = mine[0][...].astype(jnp.float32)
        for ref in mine[1:]:
            total += ref[...].astype(jnp.float32)
        value = total * (1.0 + lax.erf(total * (0.5**0.5))) * 0.5
        out_ref[partner_in_kernel(place_ref[0], dl, late)] = value.astype(jnp.bfloat16)


def finish(place, parts, owners):
    return pl.pallas_call(
        functools.partial(finish_kernel, owners),
        out_shape=jax.ShapeDtypeStruct((len(set(owners)),) + parts[0].shape, jnp.bfloat16),
        in_specs=[SMEM_SPEC] + [VMEM_SPEC] * len(parts),
        out_specs=VMEM_SPEC,
        compiler_params=pltpu.CompilerParams(vmem_limit_bytes=LIMIT),
        name="finish",
    )(place, *parts)


def both_kernels(kernel, late):
    bases, rows, taps, slots, block, _ = kernel.shape
    own = kernel.transpose(1, 0, 2, 5, 3, 4).reshape(rows, bases * taps, block, slots * block)
    return [own] + [trade(own, "late", s, late) for s in range(1, late)]


def gather_mix(mix, packed, late, owners):
    core, own = lax.axis_index("late"), lax.axis_index("lonp")
    if owners == 4 and late == 2:
        route = [(p, p ^ 1) for p in range(4)] + [(4 + p, 4 + (p ^ 2)) for p in range(4)]
        first = lax.ppermute(mix, ("late", "lonp"), route)
        packed, first = lax.optimization_barrier((packed, first))
        third = lax.ppermute(first, ("late", "lonp"), [(4 + p, 4 + (p ^ 1)) for p in range(4)])
        other = trade(first, "late", 1, late)
        copied = lax.ppermute(third, "late", [(1, 0)])
        slots, origins = [[mix], [first], [other], [third, copied]], [own, own ^ (1 + core), own ^ (2 - core), own ^ 3]
        return slots, origins, packed
    slots = [[mix]] + [[trade(mix, "lonp", d, owners)] for d in range(1, owners)]
    return slots, [partner(own, d, owners) for d in range(owners)], packed


def per_device(sizes, fields, kernel, band_low, block_shift, mix_weight):
    halves, late, owners, groups = sizes
    members, rows, channels, cells = fields.shape
    bases, _, taps, slots, block, _ = kernel.shape
    all_rows = late * rows
    halo = HALO if halves > 1 else 0

    packed = pack(fields.transpose(0, 1, 3, 2), groups, owners)
    packed = packed.reshape((-1,) + packed.shape[3:])
    mix, origins, packed = gather_mix(mix_weight, packed, late, owners)
    spread = lax.all_to_all(packed, ("late", "lonp", "lonq"), split_axis=0, concat_axis=0, tiled=True)
    spread = spread.reshape(late, owners, groups * cells, -1)
    weights = both_kernels(kernel, late)

    start = lax.axis_index("lath") * all_rows
    low = lax.dynamic_slice_in_dim(band_low, start, all_rows, 1)
    shift = lax.dynamic_slice_in_dim(block_shift, start, all_rows, 0)
    place = [lax.axis_index("late"), lax.axis_index("lonp"), lax.axis_index("lonq")] + origins
    place = jnp.stack(place).astype(jnp.int32)
    partial = conv_mix(low, shift, place, spread, weights, mix, halo, groups, block)
    if halo:
        *partial, beyond = partial
        below = lax.ppermute(beyond[1], "lath", [(i, i + 1) for i in range(halves - 1)])
        above = lax.ppermute(beyond[0], "lath", [(i + 1, i) for i in range(halves - 1)])
        filler = jnp.zeros((all_rows - 2 * halo,) + below.shape[1:], below.dtype)
        extra = jnp.concatenate([below, filler, above], axis=0).reshape(late, rows, groups, cells, -1)
        for dl in range(late):
            lat = partner(lax.axis_index("late"), dl, late)
            for dq in range(groups):
                group = partner(lax.axis_index("lonq"), dq, groups)
                partial[dl * groups + dq] += extra[lat, :, group]
    order = [(dl, dq) for dl in range(late) for dq in range(groups)]
    order.sort(key=lambda at: (at[1] == 0, bin(at[1]).count("1"), at))
    parts = []
    for dl, dq in order:
        route = [
            (l * groups + q, partner(l, dl, late) * groups + partner(q, dq, groups))
            for l in range(late)
            for q in range(groups)
        ]
        block = partial[dl * groups + dq]
        parts.append(lax.ppermute(block, ("late", "lonq"), route) if dl or dq else block)
    return finish(place, parts, [dl for dl, _ in order])


def solution(mesh):
    lat, lon = mesh.shape["lat"], mesh.shape["lon"]
    groups = max(g for g in range(1, lon + 1) if lon % g == 0 and g * g <= lon)

    def whole(fields, kernel, band_low, block_shift, mix_weight):
        late = fields.shape[0]
        sizes = (lat // late, late, lon // groups, groups)
        split = Mesh(mesh.devices.reshape(sizes), ("lath", "late", "lonp", "lonq"))
        rows, cells = ("lath", "late"), ("lonp", "lonq")
        return jax.shard_map(
            functools.partial(per_device, sizes),
            mesh=split,
            in_specs=(
                P(None, rows, None, cells),
                P(None, rows, None, None, None, None),
                P(),
                P(),
                P(None, cells, None),
            ),
            out_specs=P(None, rows, cells, None),
            check_vma=False,
        )(fields, kernel, band_low, block_shift, mix_weight)

    return whole
```

```python
import functools
import math

import jax
import jax.numpy as jnp
from jax import lax
from jax.experimental import pallas as pl
from jax.experimental.pallas import tpu as pltpu
from jax.sharding import Mesh
from jax.sharding import PartitionSpec as P

HALO = 2
LANES = 128
VMEM = pltpu.VMEM
LIMIT = 16 * 1024 * 1024
SMEM_SPEC = pl.BlockSpec(memory_space=pltpu.SMEM)
VMEM_SPEC = pl.BlockSpec(memory_space=VMEM)


def partner(index, distance, size):
    if size & (size - 1) == 0:
        return index ^ distance
    return (distance - index) % size


def partner_in_kernel(index, distance, size):
    if size & (size - 1) == 0:
        return lax.bitwise_xor(index, distance)
    return lax.rem(distance - index + size, size)


def trade(x, axis, distance, size):
    return lax.ppermute(x, axis, [(i, partner(i, distance, size)) for i in range(size)])


def pack_kernel(groups, owners, x_ref, out_ref):
    members, rows, cells, channels = x_ref.shape
    width = channels // (groups * owners)
    for e in range(members):
        for q in range(groups):
            parts = [
                x_ref[e, i, :, (p * groups + q) * width : (p * groups + q + 1) * width]
                for i in range(rows)
                for p in range(owners)
            ]
            block = jnp.concatenate(parts, axis=-1)
            for p in range(owners):
                out_ref[e, p, q] = block


def pack(x, groups, owners):
    members, rows, cells, channels = x.shape
    return pl.pallas_call(
        functools.partial(pack_kernel, groups, owners),
        out_shape=jax.ShapeDtypeStruct((members, owners, groups, cells, rows * channels // groups), x.dtype),
        in_specs=[VMEM_SPEC],
        out_specs=VMEM_SPEC,
        compiler_params=pltpu.CompilerParams(vmem_limit_bytes=LIMIT),
        name="pack",
    )(x)


def added(refs, *at):
    value = refs[0][at]
    for ref in refs[1:]:
        value = value + ref[at]
    return value


def conv_mix_kernel(geometry, counts, low_ref, shift_ref, place_ref, *refs):
    bases, taps, slots, halo, sub, groups = geometry
    refs = list(refs)
    fields_ref = refs.pop(0)
    weight_refs = [refs.pop(0) for _ in range(counts[0])]
    mix_slots = [[refs.pop(0) for _ in range(n)] for n in counts[1]]
    field_rows, total, mix_all, mixed, partner_rows, arrived = refs[-6:]
    outs = refs[:-6]
    late, owners, span, _ = fields_ref.shape
    depth, width = mix_slots[0][0].shape[1:]
    channels = owners * depth
    padded = total.shape[-1]
    rows, _, block, _ = weight_refs[0].shape
    nblocks = owners * span // block
    cells = span // groups
    member, owner, group = place_ref[0], place_ref[1], place_ref[2]

    copies = [pltpu.make_async_copy(weight_refs[s], partner_rows.at[s - 1], arrived.at[s - 1]) for s in range(1, late)]
    for copy in copies:
        copy.start()
    read = pl.ds(HALO - halo, late * rows + 2 * halo)
    total[:, read] = jnp.zeros((bases, late * rows + 2 * halo) + total.shape[2:], total.dtype)
    upper = pl.ds(padded - LANES, LANES)
    field_rows[:, :, upper] = jnp.zeros(field_rows.shape[:2] + (LANES,), field_rows.dtype)
    for s in range(late):
        lat = partner_in_kernel(member, s, late)
        if s:
            copies[s - 1].wait()
        kernel_rows = partner_rows.at[s - 1] if s else weight_refs[0]
        for p in range(owners):
            value = fields_ref[lat, p]
            for r in range(rows):
                field_rows[r, p * span : (p + 1) * span, :channels] = value[:, r * channels : (r + 1) * channels]

        def one_row(r, carry):
            row = lat * rows + r
            for piece in range(span // sub):
                cell = owner * span + piece * sub
                b = lax.div(cell, block)
                q = pl.multiple_of(lax.rem(cell, block), sub)
                chosen = []
                for j in range(slots):
                    source = lax.rem(b + shift_ref[row, j] + nblocks, nblocks)
                    chosen.append(field_rows[r, pl.ds(pl.multiple_of(source * block, block), block)])
                picked = jnp.concatenate(chosen, axis=0)
                lhs = kernel_rows[r, :, pl.ds(q, sub), :].reshape(bases * taps * sub, slots * block)
                product = jnp.dot(lhs, picked, preferred_element_type=jnp.float32)
                for k in range(bases):
                    at = pl.ds(row + low_ref[k, row] + HALO, taps)
                    slab = product[k * taps * sub : (k + 1) * taps * sub].reshape(taps, sub, padded)
                    total[k, at, piece * sub : (piece + 1) * sub] += slab
            return carry

        lax.fori_loop(0, rows, one_row, 0, unroll=2)

    for d, slot in enumerate(mix_slots):
        for k in range(bases):
            mix_all[place_ref[3 + d], k] = added(slot, k)
    fill = jnp.zeros((padded - channels, width), jnp.bfloat16)
    matrix = jnp.concatenate(
        [x for k in range(bases) for x in [mix_all[p, k] for p in range(owners)] + [fill]], axis=0
    )

    def one_out(first, count):
        at = pl.ds(first + HALO, count)
        lhs = [total[k, at].astype(jnp.bfloat16).reshape(count * span, padded) for k in range(bases)]
        product = jnp.dot(jnp.concatenate(lhs, axis=-1), matrix, preferred_element_type=jnp.float32)
        return product.reshape(count, span, width)

    mixed[...] = one_out(0, late * rows)
    for dl in range(late):
        lat = partner_in_kernel(member, dl, late)
        for dq in range(groups):
            start = pl.multiple_of(partner_in_kernel(group, dq, groups) * cells, 8 if cells % 8 == 0 else cells)
            for r in range(rows):
                outs[dl * groups + dq][r] = mixed[lat * rows + r, pl.ds(start, cells)].astype(jnp.bfloat16)
    if halo:
        for side, first in enumerate((-halo, late * rows)):
            outs[-1][side] = one_out(first, halo).astype(jnp.bfloat16)


def conv_mix(low, shift, place, fields, weights, mix, halo, groups, block):
    bases, all_rows = low.shape
    slots = shift.shape[1]
    late, owners, span, _ = fields.shape
    rows = all_rows // late
    depth, width = mix[0][0].shape[1:]
    padded = -(-owners * depth // LANES) * LANES
    taps = weights[0].shape[1] // bases
    sub = math.gcd(span, block)
    shapes = [jax.ShapeDtypeStruct((rows, span // groups, width), jnp.bfloat16)] * (late * groups)
    if halo:
        shapes.append(jax.ShapeDtypeStruct((2, halo, span, width), jnp.bfloat16))
    operands = [fields] + weights + [x for slot in mix for x in slot]
    counts = (len(weights), [len(s) for s in mix])
    return pl.pallas_call(
        functools.partial(conv_mix_kernel, (bases, taps, slots, halo, sub, groups), counts),
        out_shape=shapes,
        in_specs=[SMEM_SPEC] * 3
        + [VMEM_SPEC] * 2
        + [pl.BlockSpec(memory_space=pl.ANY)] * (late - 1)
        + [VMEM_SPEC] * (len(operands) - 1 - late),
        out_specs=[VMEM_SPEC] * len(shapes),
        scratch_shapes=[
            VMEM((rows, owners * span, padded), jnp.bfloat16),
            VMEM((bases, all_rows + 2 * HALO, span, padded), jnp.float32),
            VMEM((owners, bases, depth, width), jnp.bfloat16),
            VMEM((all_rows, span, width), jnp.float32),
            VMEM((max(late - 1, 1),) + weights[0].shape, jnp.bfloat16),
            pltpu.SemaphoreType.DMA((max(late - 1, 1),)),
        ],
        compiler_params=pltpu.CompilerParams(vmem_limit_bytes=LIMIT),
        name="conv_mix",
    )(low, shift, place, *operands)


def finish_kernel(owners, place_ref, *refs):
    out_ref = refs[-1]
    late = out_ref.shape[0]
    for dl in range(late):
        mine = [ref for ref, owner in zip(refs, owners) if owner == dl]
        total = mine[0][...].astype(jnp.float32)
        for ref in mine[1:]:
            total += ref[...].astype(jnp.float32)
        value = total * (1.0 + lax.erf(total * (0.5**0.5))) * 0.5
        out_ref[partner_in_kernel(place_ref[0], dl, late)] = value.astype(jnp.bfloat16)


def finish(place, parts, owners):
    return pl.pallas_call(
        functools.partial(finish_kernel, owners),
        out_shape=jax.ShapeDtypeStruct((len(set(owners)),) + parts[0].shape, jnp.bfloat16),
        in_specs=[SMEM_SPEC] + [VMEM_SPEC] * len(parts),
        out_specs=VMEM_SPEC,
        compiler_params=pltpu.CompilerParams(vmem_limit_bytes=LIMIT),
        name="finish",
    )(place, *parts)


def both_kernels(kernel, late):
    bases, rows, taps, slots, block, _ = kernel.shape
    own = kernel.transpose(1, 0, 2, 5, 3, 4).reshape(rows, bases * taps, block, slots * block)
    return [own] + [trade(own, "late", s, late) for s in range(1, late)]


def gather_mix(mix, packed, late, owners):
    core, own = lax.axis_index("late"), lax.axis_index("lonp")
    if owners == 4 and late == 2:
        route = [(p, p ^ 1) for p in range(4)] + [(4 + p, 4 + (p ^ 2)) for p in range(4)]
        first = lax.ppermute(mix, ("late", "lonp"), route)
        packed, first = lax.optimization_barrier((packed, first))
        third = lax.ppermute(first, ("late", "lonp"), [(4 + p, 4 + (p ^ 1)) for p in range(4)])
        other = trade(first, "late", 1, late)
        copied = lax.ppermute(third, "late", [(1, 0)])
        slots, origins = [[mix], [first], [other], [third, copied]], [own, own ^ (1 + core), own ^ (2 - core), own ^ 3]
        return slots, origins, packed
    slots = [[mix]] + [[trade(mix, "lonp", d, owners)] for d in range(1, owners)]
    return slots, [partner(own, d, owners) for d in range(owners)], packed


def per_device(sizes, fields, kernel, band_low, block_shift, mix_weight):
    halves, late, owners, groups = sizes
    members, rows, channels, cells = fields.shape
    bases, _, taps, slots, block, _ = kernel.shape
    all_rows = late * rows
    halo = HALO if halves > 1 else 0

    packed = pack(fields.transpose(0, 1, 3, 2), groups, owners)
    packed = packed.reshape((-1,) + packed.shape[3:])
    mix, origins, packed = gather_mix(mix_weight, packed, late, owners)
    spread = lax.all_to_all(packed, ("late", "lonp", "lonq"), split_axis=0, concat_axis=0, tiled=True)
    spread = spread.reshape(late, owners, groups * cells, -1)
    weights = both_kernels(kernel, late)

    start = lax.axis_index("lath") * all_rows
    low = lax.dynamic_slice_in_dim(band_low, start, all_rows, 1)
    shift = lax.dynamic_slice_in_dim(block_shift, start, all_rows, 0)
    place = [lax.axis_index("late"), lax.axis_index("lonp"), lax.axis_index("lonq")] + origins
    place = jnp.stack(place).astype(jnp.int32)
    partial = conv_mix(low, shift, place, spread, weights, mix, halo, groups, block)
    if halo:
        *partial, beyond = partial
        below = lax.ppermute(beyond[1], "lath", [(i, i + 1) for i in range(halves - 1)])
        above = lax.ppermute(beyond[0], "lath", [(i + 1, i) for i in range(halves - 1)])
        filler = jnp.zeros((all_rows - 2 * halo,) + below.shape[1:], below.dtype)
        extra = jnp.concatenate([below, filler, above], axis=0).reshape(late, rows, groups, cells, -1)
        for dl in range(late):
            lat = partner(lax.axis_index("late"), dl, late)
            for dq in range(groups):
                group = partner(lax.axis_index("lonq"), dq, groups)
                partial[dl * groups + dq] += extra[lat, :, group]
    order = [(dl, dq) for dl in range(late) for dq in range(groups)]
    order.sort(key=lambda at: (at[1] == 0, at))
    parts = []
    for dl, dq in order:
        route = [
            (l * groups + q, partner(l, dl, late) * groups + partner(q, dq, groups))
            for l in range(late)
            for q in range(groups)
        ]
        block = partial[dl * groups + dq]
        parts.append(lax.ppermute(block, ("late", "lonq"), route) if dl or dq else block)
    return finish(place, parts, [dl for dl, _ in order])


def solution(mesh):
    lat, lon = mesh.shape["lat"], mesh.shape["lon"]
    groups = max(g for g in range(1, lon + 1) if lon % g == 0 and g * g <= lon)

    def whole(fields, kernel, band_low, block_shift, mix_weight):
        late = fields.shape[0]
        sizes = (lat // late, late, lon // groups, groups)
        split = Mesh(mesh.devices.reshape(sizes), ("lath", "late", "lonp", "lonq"))
        rows, cells = ("lath", "late"), ("lonp", "lonq")
        return jax.shard_map(
            functools.partial(per_device, sizes),
            mesh=split,
            in_specs=(
                P(None, rows, None, cells),
                P(None, rows, None, None, None, None),
                P(),
                P(),
                P(None, cells, None),
            ),
            out_specs=P(None, rows, cells, None),
            check_vma=False,
        )(fields, kernel, band_low, block_shift, mix_weight)

    return whole
```
